32 devices in a mesh: seq: 8 (over z, x), head: 4 (over y, core).
Axes of the slice: x: 2, y: 2, z: 4, core: 2. Of those that a mesh axis runs over, the one named last changes fastest.
Arguments:
- inputs: bfloat16 [16384, 1024], P('seq', 'head'), may hold values from -6 to 6
- input_norm_scale: float32 [1024], replicated, may hold values from 0.5 to 1.5
- w_z: bfloat16 [1024, 2048], P(None, 'head'), may hold values from -0.1875 to 0.1875
- w_x: bfloat16 [1024, 2048], P(None, 'head'), may hold values from -0.1875 to 0.1875
- w_bc: bfloat16 [1024, 256], replicated, may hold values from -0.1875 to 0.1875
- w_dt: bfloat16 [1024, 32], P(None, 'head'), may hold values from -0.1875 to 0.1875
- conv_x_w: float32 [4, 2048], P(None, 'head'), may hold values from -3 to 3
- conv_x_b: float32 [2048], P('head'), may hold values from -0.5 to 0.5
- conv_bc_w: float32 [4, 256], replicated, may hold values from -3 to 3
- conv_bc_b: float32 [256], replicated, may hold values from -0.5 to 0.5
- dt_bias: float32 [32], P('head'), may hold values from -7 to -5
- a_log: float32 [32], P('head'), as said below
- d_skip: float32 [32], P('head'), may hold values from 0.5 to 1.5
- norm_inner: float32 [2048], P('head'), may hold values from 0.5 to 1.5
- w_out: bfloat16 [2048, 1024], P('head'), may hold values from -0.125 to 0.125
- cotangent: bfloat16 [16384, 1024], P('seq', 'head'), may hold values from -6 to 6
- lengths: int32 [16], replicated, may hold values from 1 to 14337, 16384 in all
- order: int32 [16], replicated, may hold values from 0 to 15, each once
Outputs:
- output: bfloat16 [16384, 1024], P('seq', 'head')
- grad_input: float32 [16384, 1024], P('seq', 'head')
- grad_norm_gain: float32 [1024], P('head')
- grad_w_z: float32 [1024, 2048], P('seq', 'head')
- grad_w_x: float32 [1024, 2048], P('seq', 'head')
- grad_w_bc: float32 [1024, 256], replicated
- grad_w_dt: float32 [1024, 32], P('seq', 'head')
- grad_conv_x_w: float32 [4, 2048], P(None, 'head')
- grad_conv_x_b: float32 [2048], P('head')
- grad_conv_bc_w: float32 [4, 256], replicated
- grad_conv_bc_b: float32 [256], replicated
- grad_dt_bias: float32 [32], P('head')
- grad_a_log: float32 [32], P('head')
- grad_d_skip: float32 [32], P('head')
- grad_norm_inner: float32 [2048], P('head')
- grad_w_out: float32 [2048, 1024], P('head', 'seq')
The draws below stay inside these ranges and needn't reach their ends.
Inputs may be any that keep to these rules, and one draw needn't show every extreme that they name: `lengths`: they sum to 16384; the longest is exactly 14337. `order`: each sequence once. `a_log`: finite reals.
All inputs are finite; a program needn't handle non-finite values.
Results may differ from the reference program's by a relative error of at most 0.012.
The reference program's roundings to bfloat16 on the way count: a program that leaves them out, or rounds other values in their place, can miss the bound.
Values may be sent and summed in bfloat16 or wider, within the bound.
No kernel may reach another device: no remote copies, remote signals or barrier semaphores. Data moves between devices by JAX's collectives and lax.ppermute only.
A program may use at most 192 MiB of HBM per device.

```python
import math
import jax
import jax.numpy as jnp
import numpy as np
from jax import lax

D = 1024
INNER = 2048
HEADDIM = 64
STATE = 128
CONV = 4
SPAN = 256
TOK_DEV = 2048
NSEQ = 16
HEADS = 32
TOKENS = 16384
N_HEAD = 4


def draw_a_log(key, part):
    key = jax.random.fold_in(key, 17)
    pick_key, slow_key, fast_key = jax.random.split(key, 3)
    fast_share = 0.5
    is_fast = jax.random.uniform(pick_key, (HEADS,), jnp.float32) < fast_share
    slow_vals = jax.random.uniform(slow_key, (HEADS,), jnp.float32, math.log(0.3), math.log(1.5)) - math.log(TOKENS * 0.004)
    fast_vals = jax.random.uniform(fast_key, (HEADS,), jnp.float32, math.log(0.6), math.log(1.6)) - math.log(40 * 0.004)
    return jnp.where(is_fast, fast_vals, slow_vals).astype(jnp.float32)


def levels(own_key, shape, cuts, smallest, high):
    def one(axis_at, blocks):
        steps = jax.random.uniform(jax.random.fold_in(jax.random.fold_in(own_key, 6), axis_at), (blocks,), jnp.float32, smallest / len(cuts), high / len(cuts))
        return jnp.repeat(jnp.exp(steps), shape[axis_at] // blocks).reshape((-1,) + (1,) * (len(shape) - axis_at - 1))

    loudness = one(*cuts[0])
    for cut in cuts[1:]:
        loudness = loudness * one(*cut)
    return loudness


def length_profile(amount, total, most, lean):
    weights = [(1 << 20) // math.isqrt(rank ** lean) + 1 for rank in range(2, amount + 1)]
    spare, counts = total - most - (amount - 1), [1] * (amount - 1)
    while spare > 0:
        candidates = [i for i in range(amount - 1) if counts[i] < most]
        mass, left = sum([weights[i] for i in candidates]), spare
        for i in candidates:
            addition = min(most - counts[i], max(1, left * weights[i] // mass), spare)
            counts[i] = counts[i] + addition
            spare = spare - addition
    return np.array([most] + counts)


def ragged(rng, count, total, bound, slope):
    if count == 2:
        one = jax.random.randint(rng, (), max(1, total - bound), min(bound, total - 1) + 1)
        return jnp.stack([one, total - one])
    sizes = jnp.asarray(length_profile(count, total, bound, slope), jnp.int32)
    twos = (count - 1) // 2
    donor, receiver = sizes[1:1 + 2 * twos:2], sizes[2:2 + 2 * twos:2]
    slack = jnp.minimum(donor - 1, bound - receiver)
    moved = jax.random.randint(jax.random.fold_in(rng, 1), (twos,), 0, 1 << 20) % (slack + 1)
    sizes = sizes.at[1:1 + 2 * twos:2].set(donor - moved).at[2:2 + 2 * twos:2].set(receiver + moved)
    return sizes[jax.random.permutation(jax.random.fold_in(rng, 2), count)]


def bell_draw(stream_key, extent, width, limit, cuts=(), held_as=jnp.bfloat16):
    array = jax.random.normal(stream_key, extent, jnp.float32) * width
    if len(cuts) > 0:
        array = levels(stream_key, extent, cuts, -0.22, 0.18) * array
    return jnp.clip(array, min=-limit, max=limit).astype(held_as)


def setup_inputs(seed: int = 0) -> dict:
    keys = jax.random.split(jax.random.key(seed), 19)
    inputs = bell_draw(keys[0], (TOKENS, D), 1.0, 6.0, ((0, 8), (1, 4)))
    input_norm_scale = jnp.clip(1.0 + 0.1 * jax.random.normal(keys[1], (D,), jnp.float32), 0.5, 1.5)
    w_z = bell_draw(keys[2], (D, INNER), D ** -0.5, 0.1875, ((1, 4),))
    w_x = bell_draw(keys[3], (D, INNER), D ** -0.5, 0.1875, ((1, 4),))
    w_bc = bell_draw(keys[4], (D, 2 * STATE), D ** -0.5, 0.1875)
    w_dt = bell_draw(keys[5], (D, HEADS), D ** -0.5, 0.1875, ((1, 4),))
    conv_x_w = bell_draw(keys[6], (CONV, INNER), CONV ** -0.5, 3.0, ((1, 4),), jnp.float32)
    conv_x_b = jnp.clip(jax.random.uniform(keys[7], (INNER,), jnp.float32, -0.5, 0.5) * levels(keys[7], (INNER,), ((0, 4),), -0.4, 0.0), -0.5, 0.5)
    conv_bc_w = bell_draw(keys[8], (CONV, 2 * STATE), CONV ** -0.5, 3.0, (), jnp.float32)
    conv_bc_b = jnp.clip(jax.random.uniform(keys[9], (2 * STATE,), jnp.float32, -0.5, 0.5), -0.5, 0.5)
    dt_bias = jnp.clip(-7.0 + 2.0 * jax.random.uniform(keys[10], (HEADS,), jnp.float32) ** levels(keys[10], (HEADS,), ((0, 4),), -0.2, 0.2), -7.0, -5.0)
    a_log = draw_a_log(jax.random.fold_in(keys[18], 71), 0)
    d_skip = jnp.clip(0.5 + 1.0 * jax.random.uniform(keys[12], (HEADS,), jnp.float32) ** levels(keys[12], (HEADS,), ((0, 4),), -0.2, 0.2), 0.5, 1.5)
    norm_inner = jnp.clip(1.0 + 0.1 * jax.random.normal(keys[13], (INNER,), jnp.float32), 0.5, 1.5)
    w_out = bell_draw(keys[14], (INNER, D), INNER ** -0.5, 0.125, ((0, 4),))
    cotangent = bell_draw(keys[15], (TOKENS, D), 1.0, 6.0, ((0, 8), (1, 4)))
    lengths = ragged(keys[16], NSEQ, TOKENS, TOKENS - TOK_DEV + 1, 2).astype(jnp.int32)
    order = jax.random.permutation(keys[17], NSEQ).astype(jnp.int32)
    return dict(inputs=inputs, input_norm_scale=input_norm_scale, w_z=w_z, w_x=w_x, w_bc=w_bc, w_dt=w_dt, conv_x_w=conv_x_w, conv_x_b=conv_x_b, conv_bc_w=conv_bc_w, conv_bc_b=conv_bc_b, dt_bias=dt_bias, a_log=a_log, d_skip=d_skip, norm_inner=norm_inner, w_out=w_out, cotangent=cotangent, lengths=lengths, order=order)


EPSILON = 1e-05
PRECISE = lax.Precision.HIGHEST

@jax.custom_vjp
def low(v):
    return lax.optimization_barrier(v.astype(jnp.bfloat16)).astype(jnp.float32)

@jax.custom_vjp
def low_back(v):
    return v

def low_keep(v):
    return (low(v), None)

def low_pass(kept, grad):
    return (grad,)

def back_keep(v):
    return (v, None)

def back_low(kept, grad):
    return (low(grad),)
low.defvjp(low_keep, low_pass)
low_back.defvjp(back_keep, back_low)

def matmul(left, right):
    return jnp.dot(left, right, precision=PRECISE)

def positions(lengths, order):
    placed = jnp.take(lengths, order)
    starts = (jnp.cumsum(placed) - placed).astype(jnp.int32)
    where_at = jnp.arange(TOKENS, dtype=jnp.int32)
    seg_ids = lax.optimization_barrier(jnp.sum((starts[None, :] <= where_at[:, None]).astype(jnp.int32), axis=1)) - 1
    begins = lax.optimization_barrier(jnp.sum((starts[None, :] == where_at[:, None]).astype(jnp.float32), axis=1))
    return (seg_ids.astype(jnp.int32), begins)

def conv_apply(pre_vals, weight_vals, bias_vals, seg_ids):
    reach_back = weight_vals.shape[0] - 1
    result = bias_vals[None, :] + weight_vals[reach_back][None, :] * pre_vals
    for lag_steps in range(1, reach_back + 1):
        lagged = jnp.pad(pre_vals, ((lag_steps, 0), (0, 0)))[:-lag_steps]
        lagged_ids = jnp.pad(seg_ids, (lag_steps, 0), constant_values=-1)[:-lag_steps]
        matches = (lagged_ids == seg_ids).astype(jnp.float32)[:, None]
        result = result + weight_vals[reach_back - lag_steps][None, :] * lagged * matches
    return jax.nn.silu(result)

def span_step(carried, pieces, decay_rate):
    x_block, dt_block, b_block, c_block, seg_block, begin_block = pieces
    log_decay = dt_block * decay_rate[None]
    running = jnp.cumsum(log_decay, axis=0)
    places = jnp.arange(x_block.shape[0])
    allowed = (seg_block[:, None] == seg_block[None, :]) & (places[:, None] >= places[None, :])
    spread = running[:, None] - running[None, :]
    decays = jnp.where(allowed[:, :, None, None], jnp.exp(jnp.minimum(spread, 0.0)), 0.0)
    scores = jnp.einsum('tgn,sgn->tsg', c_block, b_block, precision=PRECISE)
    mixing = decays * scores[:, :, :, None] * dt_block[None]
    inside = jnp.einsum('tsgk,sgkp->tgkp', mixing, x_block, precision=PRECISE)
    alive_rows = (jnp.cumsum(begin_block) == 0).astype(jnp.float32)
    reach_rows = alive_rows[:, None, None] * jnp.exp(running)
    entering = jnp.einsum('tgn,gkpn->tgkp', c_block, carried, precision=PRECISE) * reach_rows[..., None]
    tail_sum = running[-1]
    keep_last = jnp.exp(tail_sum[None] - running) * (seg_block == seg_block[-1]).astype(jnp.float32)[:, None, None]
    fresh_part = jnp.einsum('sgk,sgkp,sgn->gkpn', keep_last * dt_block, x_block, b_block, precision=PRECISE)
    carry_next = (jnp.exp(tail_sum) * alive_rows[-1])[..., None, None] * carried + fresh_part
    return (carry_next, inside + entering)

def mixer_forward(x_heads, dt_value, decay_rate, b_groups, c_groups, d_skip, seg_ids, begins):
    block_count = TOKENS // SPAN
    groups = N_HEAD
    per_group = HEADS // N_HEAD

    def by_blocks(values):
        return values.reshape((block_count, SPAN) + values.shape[1:])
    rates = decay_rate.reshape(groups, per_group)

    def step_block(carried, pieces):
        return span_step(carried, pieces, rates)
    pieces = (by_blocks(x_heads.reshape(TOKENS, groups, per_group, HEADDIM)), by_blocks(dt_value.reshape(TOKENS, groups, per_group)), by_blocks(b_groups), by_blocks(c_groups), by_blocks(seg_ids), by_blocks(begins))
    start_state = jnp.zeros((groups, per_group, HEADDIM, STATE), jnp.float32)
    final_state, outputs = lax.scan(jax.checkpoint(step_block), start_state, pieces)
    return outputs.reshape(TOKENS, HEADS, HEADDIM) + d_skip[None, :, None] * x_heads

def layer_forward(inputs, input_norm_scale, w_z, w_x, w_bc, w_dt, conv_x_w, conv_x_b, conv_bc_w, conv_bc_b, dt_bias, a_log, d_skip, norm_inner, w_out, seg_ids, begins):
    reciprocal_root_mean_square = lax.rsqrt(lax.optimization_barrier(jnp.mean(inputs * inputs, axis=1, keepdims=True)) + EPSILON)
    normed = low(inputs * reciprocal_root_mean_square * input_norm_scale[None, :])
    z_gate = low_back(matmul(normed, w_z))
    x_pre = low_back(low(matmul(normed, w_x)))
    bc_pre = low(matmul(normed, w_bc))
    dt_raw = low_back(matmul(normed, w_dt))
    x_heads = conv_apply(x_pre, conv_x_w, conv_x_b, seg_ids).reshape(TOKENS, HEADS, HEADDIM)
    b_list = []
    c_list = []
    for group_index in range(N_HEAD):
        conv_bc = conv_apply(low_back(bc_pre), conv_bc_w, conv_bc_b, seg_ids)
        b_list.append(conv_bc[:, :STATE])
        c_list.append(conv_bc[:, STATE:])
    b_groups = jnp.stack(b_list, axis=1)
    c_groups = jnp.stack(c_list, axis=1)
    dt_value = jax.nn.softplus(dt_raw + dt_bias[None, :])
    decay_rate = -jnp.exp(a_log)
    y_flat = mixer_forward(x_heads, dt_value, decay_rate, b_groups, c_groups, d_skip, seg_ids, begins).reshape(TOKENS, INNER)
    gated_rows = y_flat * jax.nn.silu(z_gate)
    inner_inv = lax.rsqrt(lax.optimization_barrier(jnp.mean(gated_rows * gated_rows, axis=1, keepdims=True)) + EPSILON)
    y_norm = low(gated_rows * inner_inv * norm_inner[None, :])
    return inputs + matmul(y_norm, w_out)

def reference(inputs, input_norm_scale, w_z, w_x, w_bc, w_dt, conv_x_w, conv_x_b, conv_bc_w, conv_bc_b, dt_bias, a_log, d_skip, norm_inner, w_out, cotangent, lengths, order):
    seg_ids, begins = positions(lengths, order)

    def wrapped(p_in, p_gain, p_wz, p_wx, p_wbc, p_wdt, p_cxw, p_cxb, p_cbw, p_cbb, p_dtb, p_alog, p_dsk, p_ninner, p_wout):
        return layer_forward(p_in, p_gain, p_wz, p_wx, p_wbc, p_wdt, p_cxw, p_cxb, p_cbw, p_cbb, p_dtb, p_alog, p_dsk, p_ninner, p_wout, seg_ids, begins)
    result, pull_back = jax.vjp(wrapped, inputs.astype(jnp.float32), input_norm_scale.astype(jnp.float32), w_z.astype(jnp.float32), w_x.astype(jnp.float32), w_bc.astype(jnp.float32), w_dt.astype(jnp.float32), conv_x_w.astype(jnp.float32), conv_x_b.astype(jnp.float32), conv_bc_w.astype(jnp.float32), conv_bc_b.astype(jnp.float32), dt_bias.astype(jnp.float32), a_log.astype(jnp.float32), d_skip.astype(jnp.float32), norm_inner.astype(jnp.float32), w_out.astype(jnp.float32))
    grads = pull_back(cotangent.astype(jnp.float32))
    return (result.astype(jnp.bfloat16), grads[0], grads[1], grads[2], grads[3], grads[4], grads[5], grads[6], grads[7], grads[8], grads[9], grads[10], grads[11], grads[12], grads[13], grads[14])
```

```python
import functools

import jax
import jax.numpy as jnp
from jax import lax
from jax.experimental import pallas as pl
from jax.experimental.pallas import tpu as pltpu
from jax.sharding import PartitionSpec as P

SPAN = 256
EDGE = 16
EPSILON = 1e-05
F32 = jnp.float32
BF16 = jnp.bfloat16
NEAR, FAR = pltpu.VMEM, pltpu.HBM


def mm(left, right):
    return lax.dot_general(left, right, (((1,), (0,)), ((), ())), preferred_element_type=F32)


def mm_nt(left, right):
    return lax.dot_general(left, right, (((1,), (1,)), ((), ())), preferred_element_type=F32)


def mm_tn(left, right):
    return lax.dot_general(left, right, (((0,), (0,)), ((), ())), preferred_element_type=F32)


def pieces(values, count):
    found = []
    for _ in range(count):
        part = values.astype(BF16)
        found.append(part)
        values = values - part.astype(F32)
    return found


def add_all(terms):
    total = terms[0]
    for term in terms[1:]:
        total = total + term
    return total


def triangle(size, keep):
    rows = lax.broadcasted_iota(jnp.int32, (size, size), 0)
    cols = lax.broadcasted_iota(jnp.int32, (size, size), 1)
    return keep(rows, cols).astype(F32).astype(BF16)


def expander(heads, width, copies=1):
    rows = lax.broadcasted_iota(jnp.int32, (copies * heads, width), 0) & (heads - 1)
    cols = lax.broadcasted_iota(jnp.int32, (copies * heads, width), 1)
    size = width // heads
    return ((cols >= rows * size) & (cols < (rows + 1) * size)).astype(F32).astype(BF16)


def expand(values, spread):
    count = spread.shape[0] // values.shape[1]
    parts = [part.astype(F32) for part in pieces(values, count)]
    return mm(jnp.concatenate(parts, axis=1).astype(BF16), spread)


def per_head(values, spread, count=2):
    return add_all([mm_nt(part, spread) for part in pieces(values, count)])


def widen(column, width):
    lanes = column.shape[1]
    if width <= lanes:
        return column[:, :width]
    return jnp.concatenate([column] * (width // lanes), axis=1)


def row_ids(rows, lanes=128):
    return lax.broadcasted_iota(jnp.int32, (rows, lanes), 0)


def sigmoid(values):
    return 0.5 * jnp.tanh(0.5 * values) + 0.5


def softplus(values):
    return jnp.maximum(values, 0.0) + jnp.log1p(jnp.exp(-jnp.abs(values)))


def rows_of_sums(first, second):
    lane = lax.broadcasted_iota(jnp.int32, (first.shape[0], 128), 1)
    one = jnp.sum(first, axis=1, keepdims=True)
    two = jnp.sum(second, axis=1, keepdims=True)
    return jnp.where(lane == 0, one, jnp.where(lane == 1, two, 0.0)).T[:8]


def row_of_sums(values):
    lane = lax.broadcasted_iota(jnp.int32, (values.shape[0], 128), 1)
    return jnp.where(lane == 0, jnp.sum(values, axis=1, keepdims=True), 0.0).T[:8]


def column_of(rows, at):
    picks = (lax.broadcasted_iota(jnp.int32, (8, 128), 0) == at).astype(F32).astype(BF16)
    return add_all([mm_tn(part, picks) for part in pieces(rows, 3)])


def fold_rows(values):
    rows, lanes = values.shape
    return jnp.sum(values.reshape(rows // 8, 8, lanes), axis=0)


def halves_of(values):
    high = values.astype(BF16)
    return high, (values - high.astype(F32)).astype(BF16)


class Held:
    def __init__(self, array, space):
        self.array, self.space, self.shape = array, space, array.shape


def bare(one):
    return one.array if isinstance(one, Held) else one


def stays(one):
    return pltpu.with_memory_space_constraint(one.array, one.space) if isinstance(one, Held) else one


def call(body, grid, ins, outs, scratch, work, name, kept=None, after=(), carry=(), room=24):
    arrays = [ins[0]] + [stays(one[0]) for one in ins[1:]]
    specs = [one[1] for one in ins[1:]]
    aliases = {}
    own = len(arrays)
    for at, array in (kept or {}).items():
        aliases[len(arrays)] = at
        arrays.append(stays(array))
        specs.append(pl.BlockSpec(memory_space=pl.ANY))
    for array in after:
        arrays.append(stays(array))
        specs.append(pl.BlockSpec(memory_space=pl.ANY))
    for at, array in enumerate(carry):
        aliases[len(arrays)] = len(outs) + 1 + at
        arrays.append(array)
        specs.append(pl.BlockSpec(memory_space=pl.ANY))
    total = len(arrays)
    spaces = [one[3] if len(one) > 3 else None for one in outs]

    def only_own(*refs):
        token = refs[total + len(outs)]
        token[...] = jnp.zeros_like(token)
        body(*refs[:own], *refs[total : total + len(outs)], *refs[total + len(outs) + 1 + len(carry) :])

    found = pl.pallas_call(
        only_own,
        out_shape=[
            space(one[0], one[1]) if space else jax.ShapeDtypeStruct(one[0], one[1])
            for one, space in zip(outs, spaces)
        ]
        + [jax.ShapeDtypeStruct((8, 128), F32)]
        + [jax.ShapeDtypeStruct(one.shape, one.dtype) for one in carry],
        grid_spec=pltpu.PrefetchScalarGridSpec(
            num_scalar_prefetch=1,
            grid=grid,
            in_specs=specs,
            out_specs=[one[2] for one in outs]
            + [whole((8, 128))]
            + [pl.BlockSpec(memory_space=pl.ANY)] * len(carry),
            scratch_shapes=scratch,
        ),
        input_output_aliases=aliases,
        compiler_params=pltpu.CompilerParams(
            dimension_semantics=("arbitrary",) * len(grid), vmem_limit_bytes=room * 1024 * 1024
        ),
        cost_estimate=pl.CostEstimate(
            flops=int(work[0] * 1e9), bytes_accessed=int(work[1]), transcendentals=0
        ),
        name=name,
    )(*arrays)
    made = [Held(one, space) if space else one for one, space in zip(found, spaces)]
    return made + list(found[len(outs) :])


def rows_at(rows, lanes, step):
    return pl.BlockSpec((rows, lanes), lambda i, meta: (step(i), 0))


def lanes_at(rows, lanes, step):
    return pl.BlockSpec((rows, lanes), lambda i, meta: (0, step(i)))


def stack_at(shape, step):
    return pl.BlockSpec(shape, lambda i, meta: (step(i),) + (0,) * (len(shape) - 1))


def whole(shape):
    return pl.BlockSpec(shape, lambda i, meta: (0,) * len(shape))


def whole_of(array):
    return (array, whole(array.shape))


def block_at(me, k, size):
    return pl.ds(pl.multiple_of((me ^ k) * size, size), size)


LAST = 3
DT, RAW, RUN, REACH, KEEP, INV = range(6)


def column(ref, which, heads):
    return ref[:, which * heads : (which + 1) * heads]


def project_body(shards, inner, state, heads, start, steps, opens, closes, meta, *refs):
    refs = list(refs)

    def take(amount):
        found = refs[:amount]
        del refs[:amount]
        return found

    xs = take(shards)
    if opens:
        edges = take(shards)
    else:
        tail_in, carry_in, decay_in = take(3)
    begin_ref, scale, w_x, w_maps, taps, bias, dt_bias, rate = take(8)
    (
        normed_ref,
        pre_x_ref,
        pre_bc_ref,
        x_ref,
        xdt_ref,
        bc_ref,
        slope_x_ref,
        slope_bc_ref,
        cols_ref,
        runt_ref,
        state_ref,
        upto_ref,
        own_ref,
    ) = take(13)
    if opens:
        edge_ref, edge_normed = take(2)
    if closes:
        (message_ref,) = take(1)
    else:
        tail_ref, carry_out, decay_out = take(3)
    ext, carry, decay = take(3)
    step = pl.program_id(0)
    me = meta[1]
    rows = x_ref.shape[0]
    part = xs[0].shape[1]
    width = part * shards
    maps = 2 * state
    at_block = (start + step) * (rows // SPAN)
    first = meta[0] + at_block * SPAN

    def normalise(sources, target):
        loaded = [source[...].astype(F32) for source in sources]
        total = jnp.sum(add_all([one * one for one in loaded]), axis=1, keepdims=True)
        inverse = lax.rsqrt(total / width + EPSILON)
        for k, one in enumerate(loaded):
            target[:, block_at(me, k, part)] = (one * inverse * scale[me ^ k]).astype(BF16)
        return inverse

    @pl.when(step == 0)
    def _():
        if opens:
            normalise(edges, edge_normed)
            held = edge_normed[...]
            edge_ref[:, :inner] = mm(held, w_x[...]).astype(BF16)
            edge_ref[:, inner:] = mm(held, w_maps[:, :maps]).astype(BF16)
            ext[:8, :] = edge_ref[EDGE - 8 :, :].astype(F32)
            carry[...] = jnp.zeros_like(carry)
            decay[...] = jnp.ones_like(decay)
        else:
            ext[:8, :] = tail_in[EDGE - 8 :, :].astype(F32)
            carry[...] = carry_in[...]
            decay[...] = decay_in[...]

    @pl.when(step > 0)
    def _():
        ext[:8, :] = ext[rows : rows + 8, :]

    inverse = normalise(xs, normed_ref)
    held = normed_ref[...]
    pre_x_ref[...] = mm(held, w_x[...]).astype(BF16)
    both = mm(held, w_maps[...])
    pre_bc_ref[...] = both[:, :maps].astype(BF16)
    ext[8:, :inner] = pre_x_ref[...].astype(F32)
    ext[8:, inner:] = pre_bc_ref[...].astype(F32)
    raw = both[:, maps : maps + heads] + dt_bias[...]
    dt = softplus(raw)

    begin = begin_ref[...]
    place = row_ids(rows) + first
    reach = taps.shape[0] - 1
    channels = ext.shape[1]
    total = bias[...] + taps[reach : reach + 1, :] * ext[8:, :]
    for lag in range(1, reach + 1):
        valid = widen((place - lag >= begin).astype(F32), channels)
        lagged = ext[8 - lag : 8 - lag + rows, :] * valid
        total = total + taps[reach - lag : reach - lag + 1, :] * lagged
    sig = sigmoid(total)
    conv = total * sig
    slope = (sig * (1.0 + total * (1.0 - sig))).astype(BF16)
    slope_x_ref[...] = slope[:, :inner]
    slope_bc_ref[...] = slope[:, inner:]
    x = conv[:, :inner]
    x_ref[...] = x.astype(BF16)
    bc = conv[:, inner:].astype(BF16)
    bc_ref[...] = bc

    spread = expander(heads, inner, 2)
    xdt_ref[...] = (x * expand(dt, spread)).astype(BF16)
    log_decay = dt * rate[...]
    lower = triangle(SPAN, lambda r, c: r >= c)
    upper = triangle(SPAN, lambda r, c: r <= c)
    spans = [slice(s * SPAN, (s + 1) * SPAN) for s in range(rows // SPAN)]
    runs, tails, reaches, keeps, owns = [], [], [], [], []
    for s, at in enumerate(spans):
        parts = [part.astype(F32) for part in pieces(log_decay[at], 3)]
        parts = jnp.concatenate(parts, axis=1).astype(BF16)
        sums = mm(lower, parts)
        runs.append(sums[:, :heads] + sums[:, heads : 2 * heads] + sums[:, 2 * heads :])
        sums = mm_tn(parts, upper)
        runt_ref[:, at] = sums[:heads] + sums[heads : 2 * heads] + sums[2 * heads :]
    for s, at in enumerate(spans):
        run = runs[s]
        tail = run[SPAN - 1 : SPAN, :]
        last = meta[LAST + at_block + s]
        keeps.append(jnp.exp(tail - run) * (place[at] >= last).astype(F32)[:, :heads])
        reaches.append(jnp.exp(run) * (begin[at] < first + s * SPAN).astype(F32)[:, :heads])
        alive = (last < first + s * SPAN).astype(F32)
        owns.append(jnp.broadcast_to(jnp.exp(tail) * alive, (8, heads)))
    keep = jnp.concatenate(keeps, axis=0)
    run, reached = jnp.concatenate(runs, axis=0), jnp.concatenate(reaches, axis=0)
    columns = [dt, raw, run, reached, keep, jnp.broadcast_to(inverse, (rows, heads))]
    rest = cols_ref.shape[1] - len(columns) * heads
    cols_ref[...] = jnp.concatenate(columns + [jnp.zeros((rows, rest), F32)], axis=1)
    high, low = halves_of(x * expand(keep * dt, spread))
    own_all = expand(jnp.concatenate(owns, axis=0), expander(heads, inner, 3))
    for s, at in enumerate(spans):
        own = own_all[8 * s : 8 * s + 8]
        state_ref[s] = carry[...]
        upto_ref[s] = decay[...]
        own_ref[s] = own
        b = bc[at, :state]
        carry[...] = own[:1] * carry[...] + (mm_tn(b, high[at]) + mm_tn(b, low[at]))
        decay[...] = decay[...] * own

    @pl.when(step == steps - 1)
    def _():
        if closes:
            pack_message(message_ref, carry[...], decay[...])
        else:
            tail_ref[:, :inner] = pre_x_ref[rows - EDGE :, :]
            tail_ref[:, inner:] = pre_bc_ref[rows - EDGE :, :]
            carry_out[...] = carry[...]
            decay_out[...] = decay[...]


def pack_message(target, carry, decay):
    state = carry.shape[0]
    target[:state, :] = carry
    target[state:, :] = decay


def assemble(sources, me, target):
    part = sources[0].shape[1]
    for k, source in enumerate(sources):
        target[:, block_at(me, k, part)] = source[...]


def inside_body(shards, state, heads, start, meta, *refs):
    cots, refs = refs[:shards], refs[shards:]
    begin_ref, bc_ref, xdt_ref, cols_ref, runt_ref, normed_ref, w_z, w_out = refs[:8]
    y_ref, z_ref, grad_ref, cot = refs[8:]
    z_ref[...] = mm(normed_ref[...], w_z[...])
    assemble(cots, meta[1], cot)
    grad_ref[...] = mm_nt(cot[...], w_out[...])
    rows, inner = y_ref.shape
    first = meta[0] + (start + pl.program_id(0)) * rows
    row = lax.broadcasted_iota(jnp.int32, (SPAN, SPAN), 0)
    col = lax.broadcasted_iota(jnp.int32, (SPAN, SPAN), 1)
    size = inner // heads
    lane = lax.broadcasted_iota(jnp.int32, (SPAN, 2 * size), 1)
    for s in range(rows // SPAN):
        at = slice(s * SPAN, (s + 1) * SPAN)
        begin = widen(begin_ref[at, :], SPAN)
        allowed = (col <= row) & (col + (first + s * SPAN) >= begin)
        scores = mm_nt(bc_ref[at, state:], bc_ref[at, :state])
        scores = jnp.where(allowed, scores, 0.0)
        for pair in range(heads // 2):
            lanes = slice(pair * 2 * size, (pair + 1) * 2 * size)
            both = xdt_ref[at, lanes]
            total = None
            for j in range(2):
                h = 2 * pair + j
                lane_at = RUN * heads + h
                spread = cols_ref[at, lane_at : lane_at + 1] - runt_ref[h : h + 1, at]
                mixing = (scores * jnp.exp(jnp.minimum(spread, 0.0))).astype(BF16)
                mine = jnp.where((lane < size) == (j == 0), both, jnp.zeros_like(both))
                product = mm(mixing, mine)
                total = product if total is None else total + product
            y_ref[at, lanes] = total


def gate_body(state, heads, meta, *refs):
    (
        bc_ref,
        x_ref,
        cols_ref,
        z_ref,
        grad_ref,
        inside_ref,
        state_ref,
        upto_ref,
        incoming,
        skip,
        norm_inner,
        y_ref,
        sums_ref,
    ) = refs
    rows, inner = y_ref.shape
    reach = expand(column(cols_ref, REACH, heads), expander(heads, inner, 2))
    for s in range(rows // SPAN):
        at = slice(s * SPAN, (s + 1) * SPAN)
        high, low = halves_of(state_ref[s] + upto_ref[s, :1] * incoming[...])
        c = bc_ref[at, state:]
        y_ref[at, :] = inside_ref[at, :] + (mm(c, high) + mm(c, low)) * reach[at]
    y = y_ref[...] + skip[...] * x_ref[...].astype(F32)
    z = z_ref[...]
    gated = y * (z * sigmoid(z))
    sums_ref[...] = rows_of_sums(gated * gated, grad_ref[...] * norm_inner[...] * gated)


def norm_body(shards, state, heads, count, meta, *refs):
    sums, refs = refs[:shards], refs[shards:]
    (
        bc_ref,
        x_ref,
        cols_ref,
        z_ref,
        y_ref,
        grad_ref,
        own_ref,
        skip,
        norm_inner,
        y_norm_ref,
        dz_ref,
        dy_ref,
        state_ref,
        after_ref,
        message_ref,
        gain_ref,
        skip_ref,
        carry,
        decay,
    ) = refs
    step = pl.program_id(0)
    rows, inner = dy_ref.shape

    @pl.when(step == 0)
    def _():
        carry[...] = jnp.zeros_like(carry)
        decay[...] = jnp.ones_like(decay)
        gain_ref[...] = jnp.zeros_like(gain_ref)
        skip_ref[...] = jnp.zeros_like(skip_ref)

    full = inner * shards
    all_rows = add_all([one[...] for one in sums])
    inverse = widen(lax.rsqrt(column_of(all_rows, 0) / full + EPSILON), inner)
    share = widen(column_of(all_rows, 1) / full, inner) * inverse * inverse * inverse
    x = x_ref[...].astype(F32)
    y = y_ref[...] + skip[...] * x
    z = z_ref[...]
    sig = sigmoid(z)
    gate = z * sig
    gated = y * gate
    hat = gated * inverse
    grad = grad_ref[...]
    gain_ref[...] += fold_rows(grad * hat)
    y_norm_ref[...] = (hat * norm_inner[...]).astype(BF16)
    d_gated = inverse * (grad * norm_inner[...]) - gated * share
    dz_ref[...] = (d_gated * y * (sig + gate * (1.0 - sig))).astype(BF16)
    dy = d_gated * gate
    skip_ref[...] += fold_rows(dy * x)
    dy_ref[...] = dy

    reach = expand(column(cols_ref, REACH, heads), expander(heads, inner, 2))
    high, low = halves_of(dy * reach)
    for s in reversed(range(rows // SPAN)):
        at = slice(s * SPAN, (s + 1) * SPAN)
        c = bc_ref[at, state:]
        state_ref[s] = carry[...]
        after_ref[s] = decay[...]
        carry[...] = own_ref[s, :1] * carry[...] + (mm_tn(c, high[at]) + mm_tn(c, low[at]))
        decay[...] = decay[...] * own_ref[s]

    @pl.when(step == count - 1)
    def _():
        pack_message(message_ref, carry[...], decay[...])


def write_halves(total, mine, keep_ref, send_ref, columns):
    count, share = keep_ref.shape[:2]
    for j in range(count):
        here = pl.ds(pl.multiple_of((2 * j + mine) * share, share), share)
        there = pl.ds(pl.multiple_of((2 * j + 1 - mine) * share, share), share)
        keep_ref[j, :, columns] = total[here, :].astype(keep_ref.dtype)
        send_ref[j, :, columns] = total[there, :].astype(send_ref.dtype)


def early_body(shards, count, meta, *refs):
    cots, late_cots, refs = refs[:shards], refs[shards : 2 * shards], refs[2 * shards :]
    (normed_ref, y_norm_ref, dz_ref, w_out, w_z), refs = refs[:5], refs[5:]
    outs, refs = refs[:shards], refs[shards:]
    keep_ref, send_ref, gain_ref, cot, total_z, total_out = refs
    step = pl.program_id(0)
    me = meta[1]
    part = cots[0].shape[1]
    inner = dz_ref.shape[1]

    @pl.when(step == 0)
    def _():
        total_z[...] = jnp.zeros_like(total_z)
        total_out[...] = jnp.zeros_like(total_out)

    y_norm = y_norm_ref[...]
    for k in range(shards):
        outs[k][...] = mm(y_norm, w_out[:, block_at(me, k, part)]).astype(BF16)

    @pl.when(step < count // 2)
    def _():
        assemble(cots, me, cot)

    @pl.when(step >= count // 2)
    def _():
        assemble(late_cots, me, cot)

    total_z[...] += mm_tn(normed_ref[...], dz_ref[...])
    total_out[...] += mm_tn(cot[...], y_norm)

    @pl.when(step == count - 1)
    def _():
        mine = meta[2] & 1
        write_halves(total_z, mine, keep_ref, send_ref, slice(0, inner))
        write_halves(total_out, mine, keep_ref, send_ref, slice(inner, 2 * inner))
        gain_ref[...] = row_of_sums(total_z[...] * w_z[...].astype(F32))


def inside_back_body(state, heads, start, meta, begin_row, bc_ref, xdt_ref, dy_ref, cols_ref, runt_ref, dxdt_ref, dbc_ref):
    rows, inner = dxdt_ref.shape
    first = meta[0] + (start + pl.program_id(0)) * rows
    row = lax.broadcasted_iota(jnp.int32, (SPAN, SPAN), 0)
    col = lax.broadcasted_iota(jnp.int32, (SPAN, SPAN), 1)
    size = inner // heads
    lane = lax.broadcasted_iota(jnp.int32, (SPAN, 2 * size), 1)
    for s in range(rows // SPAN):
        at = slice(s * SPAN, (s + 1) * SPAN)
        allowed = (row <= col) & (row + (first + s * SPAN) >= begin_row[:1, at])
        b = bc_ref[at, :state]
        c = bc_ref[at, state:]
        scores = jnp.where(allowed, mm_nt(b, c), 0.0)
        d_scores = None
        for pair in range(heads // 2):
            lanes = slice(pair * 2 * size, (pair + 1) * 2 * size)
            x_both = xdt_ref[at, lanes]
            high, low = halves_of(dy_ref[at, lanes])
            total = None
            for j in range(2):
                h = 2 * pair + j
                lane_at = RUN * heads + h
                spread = runt_ref[h : h + 1, at] - cols_ref[at, lane_at : lane_at + 1]
                fade = jnp.exp(jnp.minimum(spread, 0.0))
                mixing = (scores * fade).astype(BF16)
                mine = (lane < size) == (j == 0)
                high_mine = jnp.where(mine, high, jnp.zeros_like(high))
                low_mine = jnp.where(mine, low, jnp.zeros_like(low))
                product = mm(mixing, high_mine)
                total = product if total is None else total + product
                faded = (mm_nt(x_both, high_mine) + mm_nt(x_both, low_mine)) * fade
                d_scores = faded if d_scores is None else d_scores + faded
            dxdt_ref[at, lanes] = total
        d_scores = jnp.where(allowed, d_scores, 0.0).astype(BF16)
        dbc_ref[at, :state] = mm(d_scores, c)
        dbc_ref[at, state:] = mm_tn(d_scores, b)


def cross_border(fresh, begins, first, edge, taps, taps_ref, lanes):
    reach = taps.shape[0] - 1
    spot = lax.broadcasted_iota(jnp.int32, (8, lanes), 0)
    place = lax.broadcasted_iota(jnp.int32, (8, 128), 0) + (first - 8)
    sent = jnp.zeros((8, lanes), F32)
    for lag in range(1, reach + 1):
        moved = jnp.concatenate([jnp.zeros((8 - lag, lanes), F32), fresh[:lag, :]], axis=0)
        starts = jnp.concatenate([jnp.zeros((8 - lag, 128), jnp.int32), begins[:lag, :]], axis=0)
        valid = widen((place >= starts).astype(F32), lanes)
        moved = jnp.where(spot >= 8 - lag, moved * valid, 0.0)
        sent = sent + taps[reach - lag : reach - lag + 1, :] * moved
        taps_ref[reach - lag] += moved * edge
    return jnp.concatenate([jnp.zeros((EDGE - 8, lanes), F32), sent], axis=0)


def conv_back(ext, begin_ext, place, pre, taps, taps_ref):
    rows, lanes = pre.shape
    reach = taps.shape[0] - 1
    du = ext[:rows, :]
    taps_ref[reach] += fold_rows(du * pre)
    total = taps[reach : reach + 1, :] * du
    for lag in range(1, reach + 1):
        valid = widen((place >= begin_ext[lag : lag + rows, :]).astype(F32), lanes)
        moved = ext[lag : lag + rows, :] * valid
        total = total + taps[reach - lag : reach - lag + 1, :] * moved
        taps_ref[reach - lag] += fold_rows(moved * pre)
    return total


def maps_back_body(state, heads, count, meta, *refs):
    (
        begin_ref,
        bc_ref,
        xdt_ref,
        dy_ref,
        cols_ref,
        slope_ref,
        pre_ref,
        edge_ref,
        normed_ref,
        edge_normed,
        w_bc,
        dbc_ref,
        state_ref,
        upto_ref,
        dstate_ref,
        after_ref,
        own_ref,
        incoming,
        outgoing,
        taps,
        dpre_ref,
        through_ref,
        ds_ref,
        tail_ref,
        left_ref,
        taps_ref,
        bias_ref,
        own_half_ref,
        send_ref,
        gain_ref,
        ext,
        begin_ext,
        weight,
    ) = refs
    step = pl.program_id(0)
    rows, inner = xdt_ref.shape
    at_step = count - 1 - step
    first = meta[0] + at_step * rows
    spread = expander(heads, inner)
    spread_two = expander(heads, inner, 2)

    @pl.when(step == 0)
    def _():
        weight[...] = jnp.zeros_like(weight)
        ext[rows:, :] = jnp.zeros_like(ext[rows:, :])
        begin_ext[rows:, :] = jnp.zeros_like(begin_ext[rows:, :])
        taps_ref[...] = jnp.zeros_like(taps_ref)
        bias_ref[...] = jnp.zeros_like(bias_ref)

    @pl.when(step > 0)
    def _():
        ext[rows:, :] = ext[:8, :]
        begin_ext[rows:, :] = begin_ext[:8, :]

    begin_ext[:rows, :] = begin_ref[...]
    place = row_ids(rows) + first
    keep = expand(column(cols_ref, KEEP, heads), spread_two)
    reach = expand(column(cols_ref, REACH, heads), spread_two)
    x_high, x_low = halves_of(xdt_ref[...].astype(F32) * keep)
    y_high, y_low = halves_of(dy_ref[...] * reach)
    for s in range(rows // SPAN):
        at = slice(s * SPAN, (s + 1) * SPAN)
        s_in = state_ref[s] + upto_ref[s, :1] * incoming[...]
        ds_out = dstate_ref[s] + after_ref[s, :1] * outgoing[...]
        ds_ref[s] = ds_out
        through = jnp.sum((s_in * ds_out).reshape(state // 8, 8, inner), axis=0) * own_ref[s]
        through_ref[s] = jnp.broadcast_to(
            jnp.sum(per_head(through, spread), axis=0, keepdims=True), (8, heads)
        )
        s_high, s_low = halves_of(s_in)
        ds_high, ds_low = halves_of(ds_out)
        d_b = mm_nt(x_high[at], ds_high) + mm_nt(x_low[at], ds_high) + mm_nt(x_high[at], ds_low)
        d_c = mm_nt(y_high[at], s_high) + mm_nt(y_low[at], s_high) + mm_nt(y_high[at], s_low)
        slope = slope_ref[at, :].astype(F32)
        ext[at, :state] = (dbc_ref[at, :state] + d_b) * slope[:, :state]
        ext[at, state:] = (dbc_ref[at, state:] + d_c) * slope[:, state:]
    bias_ref[...] += fold_rows(ext[:rows, :])
    total = conv_back(ext, begin_ext, place, pre_ref[...].astype(F32), taps, taps_ref)
    high, low = halves_of(total)
    dpre_ref[...] = high
    weight[...] += mm_tn(normed_ref[...], high) + mm_tn(normed_ref[...], low)

    @pl.when(step == 0)
    def _():
        tail_ref[...] = total[rows - EDGE :, :]

    @pl.when(step == count - 1)
    def _():
        edge = edge_ref[EDGE - 8 :, inner:].astype(F32)
        left_ref[...] = cross_border(ext, begin_ext, first, edge, taps, taps_ref, 2 * state)
        left_high, left_low = halves_of(left_ref[...])
        weight[...] += mm_tn(edge_normed[...], left_high) + mm_tn(edge_normed[...], left_low)
        half = send_ref.shape[0]
        mine = meta[1] & 1
        here = pl.ds(pl.multiple_of(mine * half, half), half)
        there = pl.ds(pl.multiple_of((1 - mine) * half, half), half)
        own_half_ref[...] = weight[here, :]
        send_ref[...] = weight[there, :]
        gain_ref[...] = row_of_sums(weight[...] * w_bc[...].astype(F32))


def inner_back_body(state, heads, start, fresh_steps, opens, meta, *refs):
    refs = list(refs)

    def take(amount):
        found = refs[:amount]
        del refs[:amount]
        return found

    (
        begin_ref,
        begin_late,
        bc_ref,
        x_ref,
        xdt_ref,
        dy_ref,
        y_ref,
        cols_ref,
        slope_ref,
        pre_late,
        normed_late,
        dxdt_ref,
        through_ref,
        ds_ref,
        skip,
        rate,
        taps,
    ) = take(17)
    if opens:
        (edge_ref,) = take(1)
    else:
        held_in, held_ddt_in, right, taps_in, bias_in, scalar_in, weight_in = take(7)
        w_x, w_dt, scale, gain_z, gain_bc, norm_gain, skip_gain, taps_bc, bias_bc = take(9)
    dpre_ref, ddt_ref = take(2)
    if opens:
        taps_ref, bias_ref, scalar_ref, held_out, held_ddt_out, left_ref, weight = take(7)
    else:
        keep_half_ref, send_ref, owned_ref, shared_ref, taps_ref, bias_ref, scalar_ref, weight = take(8)
    ext, begin_ext, fresh, ddt = take(4)
    step = pl.program_id(0)
    rows, inner = x_ref.shape
    steps = fresh_steps if opens else fresh_steps + 1
    spread = expander(heads, inner)
    spread_two = expander(heads, inner, 2)

    @pl.when(step == 0)
    def _():
        if opens:
            weight[...] = jnp.zeros_like(weight)
            taps_ref[...] = jnp.zeros_like(taps_ref)
            bias_ref[...] = jnp.zeros_like(bias_ref)
            scalar_ref[...] = jnp.zeros_like(scalar_ref)
        else:
            weight[...] = weight_in[...]
            taps_ref[...] = taps_in[...]
            bias_ref[...] = bias_in[...]
            scalar_ref[...] = scalar_in[...]
            ext[:rows, :] = held_in[...]
            ddt[...] = held_ddt_in[...]

    def renew():
        at_block = (start + step) * (rows // SPAN)
        first = meta[0] + at_block * SPAN
        place = row_ids(rows) + first
        suffix = triangle(SPAN, lambda r, c: r <= c)
        prefix = triangle(SPAN, lambda r, c: r > c)
        rate_now = rate[...]
        spans = [slice(s * SPAN, (s + 1) * SPAN) for s in range(rows // SPAN)]
        kept = []
        for s, at in enumerate(spans):
            b = bc_ref[at, :state]
            ds_high, ds_low = halves_of(ds_ref[s])
            kept.append(mm(b, ds_high) + mm(b, ds_low))
        kept = jnp.concatenate(kept, axis=0) * expand(column(cols_ref, KEEP, heads), spread_two)
        dy = dy_ref[...]
        xdt = xdt_ref[...].astype(F32)
        x = x_ref[...].astype(F32)
        dxdt_in = dxdt_ref[...]
        dxdt = dxdt_in + kept
        dt = column(cols_ref, DT, heads)
        d_x = dxdt * expand(dt, spread_two) + skip[...] * dy
        du = d_x * slope_ref[...].astype(F32)
        fresh[...] = du
        bias_ref[...] += fold_rows(du)
        dy_high = dy.astype(BF16).astype(F32)
        later = per_head(dy_high * y_ref[...] - xdt * dxdt_in, spread, 3)
        earlier = per_head(xdt * kept, spread)
        direct = per_head(x * dxdt, spread)
        q = []
        for s, at in enumerate(spans):
            after = [part.astype(F32) for part in pieces(later[at], 3)]
            after = mm(suffix, jnp.concatenate(after, axis=1).astype(BF16))
            before = [part.astype(F32) for part in pieces(earlier[at], 2)]
            before = mm(prefix, jnp.concatenate(before, axis=1).astype(BF16))
            q.append(
                (after[:, :heads] + after[:, heads : 2 * heads] + after[:, 2 * heads :])
                + (before[:, :heads] + before[:, heads:])
                + through_ref[s, :1, :]
            )
        starts = (place == begin_ref[...]).astype(F32)[:, :heads]
        q = jnp.concatenate(q, axis=0) * (1.0 - starts)
        d_raw = (direct + rate_now * q) / (1.0 + jnp.exp(-column(cols_ref, RAW, heads)))
        fresh_ddt[...] = d_raw.astype(BF16)
        scalar_ref[:8, :] += fold_rows(d_raw)
        scalar_ref[8:, :] += fold_rows(rate_now * dt * q)

    fresh_ddt = refs[0]

    def finish(closing=False):
        begin_ext[:rows, :] = begin_late[...]
        first = meta[0] + (start - (0 if opens else 1) + step - (1 if opens else 0)) * rows
        place = row_ids(rows) + first
        total = conv_back(ext, begin_ext, place, pre_late[...].astype(F32), taps, taps_ref)
        dpre_ref[...] = total.astype(BF16)
        if closing:
            dpre_ref[rows - EDGE :, :] = (total[rows - EDGE :, :] + right[...]).astype(BF16)
        ddt_ref[...] = ddt[...]
        held = normed_late[...]
        weight[:, :inner] += mm_tn(held, dpre_ref[...])
        weight[:, inner : inner + heads] += mm_tn(held, ddt[...])

    if opens:
        renew()

        @pl.when(step == 0)
        def _():
            edge = edge_ref[EDGE - 8 :, :inner].astype(F32)
            left_ref[...] = cross_border(fresh, begin_ref, meta[0], edge, taps, taps_ref, inner)

        @pl.when(step > 0)
        def _():
            ext[rows:, :] = fresh[:8, :]
            begin_ext[rows:, :] = begin_ref[:8, :]
            finish()

        ext[:rows, :] = fresh[...]
        ddt[...] = fresh_ddt[...]

        @pl.when(step == steps - 1)
        def _():
            held_out[...] = fresh[...]
            held_ddt_out[...] = fresh_ddt[...]
    else:

        @pl.when(step < steps - 1)
        def _():
            renew()
            ext[rows:, :] = fresh[:8, :]
            begin_ext[rows:, :] = begin_ref[:8, :]
            finish()
            ext[:rows, :] = fresh[...]
            ddt[...] = fresh_ddt[...]

        @pl.when(step == steps - 1)
        def _():
            ext[rows:, :] = jnp.zeros((8, inner), F32)
            begin_ext[rows:, :] = jnp.zeros((8, 128), jnp.int32)
            finish(True)
            write_halves(weight, meta[2] & 1, keep_half_ref, send_ref, slice(0, weight.shape[1]))
            gain = row_of_sums(weight[:, :inner] * w_x[...].astype(F32))
            gain_dt = row_of_sums(weight[:, inner : inner + heads] * w_dt[...].astype(F32))
            owned_ref[...] = jnp.zeros_like(owned_ref)
            shared_ref[...] = jnp.zeros_like(shared_ref)

            def one_row(values):
                return jnp.sum(values, axis=0, keepdims=True)

            for j in range(taps.shape[0]):
                owned_ref[j : j + 1, :] = one_row(taps_ref[j])
                shared_ref[j : j + 1, : 2 * state] = one_row(taps_bc[j])
            owned_ref[4:5, :] = one_row(bias_ref[...])
            shared_ref[4:5, : 2 * state] = one_row(bias_bc[...])
            owned_ref[5:6, :] = one_row(norm_gain[...])
            owned_ref[6:7, :] = one_row(skip_gain[...])
            owned_ref[7:8, :heads] = one_row(scalar_ref[:8, :])
            owned_ref[7:8, 128 : 128 + heads] = one_row(scalar_ref[8:, :])
            shared_ref[:, 2 * state :] = (gain + gain_dt + gain_z[...] + gain_bc[...]) / scale[...]


def input_body(shards, steps, closes, meta, *refs):
    xs, refs = refs[:shards], refs[shards:]
    dz_ref, dpre_ref, dbc_ref, ddt_ref, w_z, w_x, w_bc, w_dt, scale = refs[:9]
    refs = refs[9:]
    if closes:
        (tail_ref, right_ref), refs = refs[:2], refs[2:]
    outs, refs = refs[:shards], refs[shards:]
    dbc_held, sums = refs
    step = pl.program_id(0)
    me = meta[1]
    rows, part = xs[0].shape
    per_step = rows // part
    total_rows = steps * rows

    dbc_held[...] = dbc_ref[...]
    if closes:

        @pl.when(step == steps - 1)
        def _():
            dbc_held[rows - EDGE :, :] = (tail_ref[...] + right_ref[...]).astype(BF16)

    dz, dx, dbc, ddt = dz_ref[...], dpre_ref[...], dbc_held[...], ddt_ref[...]
    products = None
    here = pl.ds(pl.multiple_of(step * rows, rows), rows)
    for k in range(shards):
        at = block_at(me, k, part)
        grad = (
            mm_nt(dz, w_z[at, :])
            + mm_nt(dx, w_x[at, :])
            + mm_nt(dbc, w_bc[at, :])
            + mm_nt(ddt, w_dt[at, :])
        )
        outs[k][here, :] = grad.astype(BF16)
        product = grad * scale[me ^ k] * xs[k][...].astype(F32)
        products = product if products is None else products + product
    row = row_of_sums(products)

    @pl.when(step == 0)
    def _():
        sums[...] = jnp.zeros_like(sums)

    for s in range(steps):

        @pl.when(step == s)
        def _(s=s):
            for j in range(per_step):
                spot = s * per_step + j
                sums[spot : spot + 1, :] = row[:1, j * part : (j + 1) * part]

    @pl.when(step == steps - 1)
    def _():
        for k in range(shards):
            outs[k][total_rows:, :] = sums[...].astype(BF16)


def final_body(shards, heads, meta, *refs):
    others = shards // 2 + 1
    parts, refs = refs[:others], refs[others:]
    x_ref, cot_ref, cols_ref, scale = refs[:4]
    out_ref = refs[-1]
    me = meta[1]
    rows, part = x_ref.shape
    width = part * shards
    for j in range(rows // part):
        at = slice(j * part, (j + 1) * part)
        spot = INV * heads
        inverse = jnp.broadcast_to(cols_ref[at, spot : spot + 1], (part, part))
        group = rows + (j // 8) * 8
        sums = add_all([one[rows:, :].astype(F32) for one in parts])[group - rows : group - rows + 8]
        share = widen(column_of(sums, j % 8) / width, part) * inverse * inverse * inverse
        grad = add_all([one[at, :].astype(F32) for one in parts]) * scale[me]
        out_ref[at, :] = cot_ref[at, :].astype(F32) + inverse * grad - x_ref[at, :].astype(F32) * share


def swap(shard, axis, flip):
    return lax.ppermute(shard, axis, [(i, i ^ flip) for i in range(lax.axis_size(axis))])


def gather_head(shard):
    found = {0: shard, 1: swap(shard, "head", 1)}
    for k in range(2, lax.axis_size("head"), 2):
        found[k] = swap(shard, "head", k)
        found[k + 1] = swap(found[k], "head", 1)
    return [found[k] for k in range(lax.axis_size("head"))]


def near_body(meta, one_ref, two_ref, out_ref):
    out_ref[...] = (one_ref[...].astype(F32) + two_ref[...].astype(F32)).astype(BF16)


def scatter_near(parts):
    return [swap(parts[k + 1], "head", 1) for k in range(0, len(parts), 2)]


def scatter_far(meta, parts, got, after):
    found, sent = [parts[0], got[0]], []
    for k in range(2, len(parts), 2):
        rows, lanes = parts[k].shape
        spec = rows_at(rows // 2, lanes, lambda i: i)
        near, _ = call(
            near_body,
            (2,),
            [meta, (parts[k], spec), (got[k // 2], spec)],
            [((rows, lanes), BF16, spec)],
            [],
            (1, 1000),
            "near",
            after=after,
            room=8,
        )
        sent.append(near)
        found.append(swap(near, "head", k))
    return found, sent


def added(meta, one, two, after):
    out, _ = call(
        add_body,
        (1,),
        [meta, whole_of(one), whole_of(two)],
        [(one.shape, F32, whole(one.shape))],
        [],
        (1, 1000),
        "add",
        after=after,
        room=8,
    )
    return out


def add_body(meta, one_ref, two_ref, out_ref):
    out_ref[...] = one_ref[...] + two_ref[...]


def halve_body(axis, bit, meta, keep_ref, got_ref, kept_ref, sent_ref):
    mine = (meta[axis] >> bit) & 1
    for j in range(kept_ref.shape[0]):
        here, there = 2 * j + mine, 2 * j + 1 - mine
        kept_ref[j] = keep_ref[here].astype(F32) + got_ref[here].astype(F32)
        sent_ref[j] = (keep_ref[there].astype(F32) + got_ref[there].astype(F32)).astype(sent_ref.dtype)


def halve(meta, keep, got, bit, name, after):
    count, rows, lanes = keep.shape
    shape = (count // 2, rows, lanes)
    kept, sent, _ = call(
        functools.partial(halve_body, 2, bit),
        (1,),
        [meta, whole_of(keep), whole_of(got)],
        [(shape, F32, whole(shape)), (shape, got.dtype, whole(shape))],
        [],
        (1, 1000),
        name,
        after=after,
        room=16,
    )
    return kept, sent


def scatter_seq(meta, keep, send):
    bits = lax.axis_size("seq").bit_length() - 1
    for bit in range(bits):
        received = swap(send, "seq", 1 << bit)
        if bit == bits - 1:
            yield keep, received
            return
        after = yield send
        keep, send = halve(meta, keep, received, bit + 1, "halve", after or ())


def rest_of(stages, value):
    while True:
        try:
            value = stages.send(())
        except StopIteration:
            return value


def sum_along(values, axis):
    for bit in range(lax.axis_size(axis).bit_length() - 1):
        values = values + swap(values, axis, 1 << bit)
    return values


def sum_rows_everywhere(meta, keep, send):
    got = swap(send, "head", 1)
    after = yield send
    for bit in range(1, lax.axis_size("head").bit_length() - 1):
        keep = added(meta, keep, got, after or ())
        got = swap(keep, "head", 1 << bit)
        after = yield keep
    seq_bits = lax.axis_size("seq").bit_length() - 1
    for bit in range(seq_bits):
        rows, lanes = keep.shape
        shape = (2, rows // 2, lanes)
        kept, sent = halve(
            meta, keep.reshape(shape), got.reshape(shape), bit, "halve_maps", after or ()
        )
        keep, sent = kept.reshape(shape[1:]), sent.reshape(shape[1:])
        got = swap(sent, "seq", 1 << bit)
        after = yield sent
    total = (keep + got).astype(BF16)
    for axis, bit in reversed([("head", 0)] + [("seq", bit) for bit in range(seq_bits)]):
        mine = (lax.axis_index(axis) >> bit) & 1
        other = swap(total, axis, 1 << bit)
        low = jnp.where(mine == 0, total, other)
        high = jnp.where(mine == 0, other, total)
        total = jnp.concatenate([low, high], axis=0)
    yield total


def pair_body(forward, meta, own_ref, got_ref, sent_ref, pair):
    state = own_ref.shape[0] - 8
    half = state // 2
    odd = meta[2] & 1
    own_last = odd == (1 if forward else 0)
    own_fade, fade = own_ref[state:, :], got_ref[state:, :]
    own, other = own_ref[:state, :], got_ref[:state, :]
    pair[...] = jnp.where(own_last, own_fade[:1] * other + own, fade[:1] * own + other)
    sent_ref[:half, :] = pair[pl.ds(pl.multiple_of(odd * half, half), half), :]
    sent_ref[half:, :] = own_fade * fade


def fold_body(count, meta, *refs):
    total_ref = refs[count]
    half = total_ref.shape[0]
    total = jnp.zeros(total_ref.shape, F32)
    for one in reversed(refs[:count]):
        total = one[half : half + 1, :] * total + one[:half, :]
    total_ref[...] = total


def join_body(forward, meta, total_ref, rest_ref, got_ref, out_ref):
    state = out_ref.shape[0]
    odd = meta[2] & 1
    own_last = odd == (1 if forward else 0)
    total, rest = total_ref[...], rest_ref[...]
    low, high = jnp.where(odd == 0, total, rest), jnp.where(odd == 0, rest, total)
    total = jnp.concatenate([low, high], axis=0)
    fade, other = got_ref[state : state + 1, :], got_ref[:state, :]
    out_ref[...] = jnp.where(own_last, fade * total + other, total)


def chain(meta, message, forward):
    size = lax.axis_size("seq")
    rows, lanes = message.shape
    state = rows - 8
    half = state // 2

    def small(body, arrays, shape, scratch, name, after=(), carry=()):
        return call(
            body,
            (1,),
            [meta] + [whole_of(one) for one in arrays],
            [(shape, F32, whole(shape))],
            scratch,
            (1, 1000),
            name,
            after=after,
            carry=carry,
            room=8,
        )

    got = swap(message, "seq", 1)
    after = yield None
    sent = small(
        functools.partial(pair_body, forward),
        [message, got],
        (half + 8, lanes),
        [pltpu.VMEM((state, lanes), F32)],
        "pair",
        after,
    )[0]
    found = []
    for by in range(2, size, 2):
        if forward:
            pairs = [(i, i + by) for i in range(size - by)]
        else:
            pairs = [(i + by, i) for i in range(size - by)]
        found.append(lax.ppermute(sent, "seq", pairs))
    after = yield sent
    total = small(
        functools.partial(fold_body, len(found)), found, (half, lanes), [], "fold", after
    )[0]
    rest = swap(total, "seq", 1)
    after, carry = yield total
    body = functools.partial(join_body, forward)
    yield small(body, [total, rest, got], (state, lanes), [], "join", after, carry)


def on_device(
    inputs,
    input_norm_scale,
    w_z,
    w_x,
    w_bc,
    w_dt,
    conv_x_w,
    conv_x_b,
    conv_bc_w,
    conv_bc_b,
    dt_bias,
    a_log,
    d_skip,
    norm_inner,
    w_out,
    cotangent,
    lengths,
    order,
):
    tokens, part = inputs.shape
    shards = lax.axis_size("head")
    seq_size = lax.axis_size("seq")
    me = lax.axis_index("head")
    seq = lax.axis_index("seq")
    width = part * shards
    share = width // seq_size
    inner = w_z.shape[1]
    heads = dt_bias.shape[0]
    size = inner // heads
    state = w_bc.shape[1] // 2
    channels = inner + 2 * state
    taps_count = conv_x_w.shape[0]
    rows = 2 * SPAN
    spans = rows // SPAN
    count = tokens // rows
    half = tokens // 2
    half_count = count // 2
    first = seq * tokens

    number = lengths.shape[0]
    picker = (order[:, None] == jnp.arange(number, dtype=jnp.int32)[None, :]).astype(jnp.int32)
    placed = jnp.sum(picker * lengths[None, :], axis=1)
    starts = jnp.cumsum(placed) - placed
    spots = first + jnp.arange(tokens, dtype=jnp.int32)
    begin = jnp.max(jnp.where(starts[None, :] <= spots[:, None], starts[None, :], 0), axis=1)
    begin = begin.astype(jnp.int32)
    begin_col = jnp.broadcast_to(begin[:, None], (tokens, 128))
    begin_row = jnp.broadcast_to(begin[None, :], (8, tokens))
    ends = begin.reshape(tokens // SPAN, SPAN)[:, -1]
    meta = jnp.concatenate([jnp.stack([first, me, seq]).astype(jnp.int32), ends])

    edge = inputs[tokens - EDGE :]
    edges = [
        lax.ppermute(
            edge,
            ("seq", "head"),
            [
                (i * shards + j, (i + 1) * shards + (j ^ k))
                for i in range(seq_size - 1)
                for j in range(shards)
            ],
        )
        for k in range(shards)
    ]
    own_halves = [inputs[:half], inputs[half:]]
    xs = [gather_head(own_halves[0]), gather_head(own_halves[1])]
    cots = []

    scale = input_norm_scale.reshape(shards, 1, part)
    taps = jnp.concatenate([conv_x_w, conv_bc_w], axis=1)
    bias = jnp.concatenate([conv_x_b, conv_bc_b])[None, :]
    rate = -jnp.exp(a_log)[None, :]
    w_maps = jnp.concatenate([w_bc, w_dt, jnp.zeros((width, 128 - heads), BF16)], axis=1)
    skip = jnp.repeat(d_skip, size)[None, :]
    inner_gain = norm_inner[None, :]
    scale_row = input_norm_scale[None, :]
    prepared = [begin_row, skip, inner_gain, scale_row, rate]

    def far(one):
        return Held(one, FAR)

    def fore(i):
        return i

    def back(i):
        return count - 1 - i

    big = [
        ((tokens, width), BF16, "rows", FAR),
        ((tokens, inner), BF16, "rows", FAR),
        ((tokens, 2 * state), BF16, "rows", FAR),
        ((tokens, inner), BF16, "rows", NEAR),
        ((tokens, inner), BF16, "rows", NEAR),
        ((tokens, 2 * state), BF16, "rows", NEAR),
        ((tokens, inner), BF16, "rows", FAR),
        ((tokens, 2 * state), BF16, "rows", FAR),
        ((tokens, 128), F32, "rows", NEAR),
        ((heads, tokens), F32, "lanes", NEAR),
        ((tokens // SPAN, state, inner), F32, "stack", NEAR),
        ((tokens // SPAN, 8, inner), F32, "stack", NEAR),
        ((tokens // SPAN, 8, inner), F32, "stack", NEAR),
    ]

    def spec_of(shape, kind, step):
        if kind == "rows":
            return rows_at(rows, shape[1], step)
        if kind == "lanes":
            return lanes_at(shape[0], rows, step)
        return stack_at((spans,) + shape[1:], step)

    carried = None
    for chunk in range(2):
        opens, closes = chunk == 0, chunk == 1
        start = chunk * half_count

        def here(i, start=start):
            return start + i

        ins = [meta] + [(far(one), rows_at(rows, part, fore)) for one in xs[chunk]]
        if opens:
            ins += [whole_of(one) for one in edges]
        else:
            ins += [whole_of(one) for one in carried]
        ins += [(begin_col, rows_at(rows, 128, here))]
        ins += [
            whole_of(one)
            for one in (scale, w_x, w_maps, taps, bias, dt_bias[None, :], rate)
        ]
        outs = [
            (shape, dtype, spec_of(shape, kind, here), space) for shape, dtype, kind, space in big
        ]
        if opens:
            extra = [((EDGE, channels), BF16), ((EDGE, width), BF16)]
        else:
            extra = []
        if closes:
            extra += [((state + 8, inner), F32)]
        else:
            extra += [((EDGE, channels), BF16), ((state, inner), F32), ((8, inner), F32)]
        outs += [(shape, dtype, whole(shape)) for shape, dtype in extra]
        found = call(
            functools.partial(
                project_body, shards, inner, state, heads, start, half_count, opens, closes
            ),
            (half_count,),
            ins,
            outs,
            [
                pltpu.VMEM((rows + 8, channels), F32),
                pltpu.VMEM((state, inner), F32),
                pltpu.VMEM((8, inner), F32),
            ],
            (12, 1000000),
            "project",
            after=prepared if opens else [],
            carry=[cotangent[chunk * half : (chunk + 1) * half]],
            kept=None if opens else dict(enumerate(held)),
        )
        held = found[: len(big)]
        cots.append(gather_head(found[-1]))
        if opens:
            pre_edge, edge_normed = found[len(big) : len(big) + 2]
            carried = found[len(big) + 2 : -2]
        else:
            message = found[len(big)]
    (
        normed,
        pre_x,
        pre_bc,
        x,
        xdt,
        bc,
        slope_x,
        slope_bc,
        cols,
        runt,
        states,
        upto,
        own,
    ) = held

    links = chain(meta, message, True)
    next(links)
    found = None
    for chunk in range(2):
        start = chunk * half_count
        if chunk == 1:
            sent = links.send([found[-1]])

        def here(i, start=start):
            return start + i

        found = call(
            functools.partial(inside_body, shards, state, heads, start),
            (half_count,),
            [meta]
            + [(far(one), rows_at(rows, part, fore)) for one in cots[chunk]]
            + [
                (begin_col, rows_at(rows, 128, here)),
                (bc, rows_at(rows, 2 * state, here)),
                (xdt, rows_at(rows, inner, here)),
                (cols, rows_at(rows, 128, here)),
                (runt, lanes_at(heads, rows, here)),
                (normed, rows_at(rows, width, here)),
                whole_of(w_z),
                whole_of(w_out),
            ],
            [((tokens, inner), F32, rows_at(rows, inner, here), NEAR)] * 3,
            [pltpu.VMEM((rows, width), BF16)],
            (8, 1000000),
            "inside",
            None if found is None else dict(enumerate(found[:3])),
            () if found is None else [sent],
        )
    inside, z, grad_y, done = found
    links.send([done])
    incoming, _ = links.send(((), ()))

    y, sums, done = call(
        functools.partial(gate_body, state, heads),
        (count,),
        [meta]
        + [
            (bc, rows_at(rows, 2 * state, fore)),
            (x, rows_at(rows, inner, fore)),
            (cols, rows_at(rows, 128, fore)),
            (z, rows_at(rows, inner, fore)),
            (grad_y, rows_at(rows, inner, fore)),
            (inside, rows_at(rows, inner, fore)),
            (states, stack_at((spans, state, inner), fore)),
            (upto, stack_at((spans, 8, inner), fore)),
            whole_of(incoming),
            whole_of(skip),
            whole_of(inner_gain),
        ],
        [
            ((tokens, inner), F32, rows_at(rows, inner, fore), NEAR),
            ((8, tokens), F32, lanes_at(8, rows, fore)),
        ],
        [],
        (9, 1000000),
        "gate",
    )

    all_sums = [sums] + [swap(sums, "head", k) for k in range(1, shards)]

    y_norm, dz, dy, dstates, after, message, g_norm_inner, g_skip, done = call(
        functools.partial(norm_body, shards, state, heads, count),
        (count,),
        [meta]
        + [(one, lanes_at(8, rows, back)) for one in all_sums]
        + [
            (bc, rows_at(rows, 2 * state, back)),
            (x, rows_at(rows, inner, back)),
            (cols, rows_at(rows, 128, back)),
            (z, rows_at(rows, inner, back)),
            (y, rows_at(rows, inner, back)),
            (grad_y, rows_at(rows, inner, back)),
            (own, stack_at((spans, 8, inner), back)),
            whole_of(skip),
            whole_of(inner_gain),
        ],
        [
            ((tokens, inner), BF16, rows_at(rows, inner, back), NEAR),
            ((tokens, inner), BF16, rows_at(rows, inner, back), NEAR),
            ((tokens, inner), F32, rows_at(rows, inner, back), NEAR),
            ((tokens // SPAN, state, inner), F32, stack_at((spans, state, inner), back), NEAR),
            ((tokens // SPAN, 8, inner), F32, stack_at((spans, 8, inner), back), NEAR),
            ((state + 8, inner), F32, whole((state + 8, inner))),
            ((8, inner), F32, whole((8, inner))),
            ((8, inner), F32, whole((8, inner))),
        ],
        [pltpu.VMEM((state, inner), F32), pltpu.VMEM((8, inner), F32)],
        (12, 1000000),
        "norm",
    )


    def inside_back(chunk, kept, after):
        def here(i):
            return chunk * half_count + i

        return call(
            functools.partial(inside_back_body, state, heads, chunk * half_count),
            (half_count,),
            [
                meta,
                (begin_row, lanes_at(8, rows, here)),
                (bc, rows_at(rows, 2 * state, here)),
                (xdt, rows_at(rows, inner, here)),
                (dy, rows_at(rows, inner, here)),
                (cols, rows_at(rows, 128, here)),
                (runt, lanes_at(heads, rows, here)),
            ],
            [
                ((tokens, inner), F32, rows_at(rows, inner, here), NEAR),
                ((tokens, 2 * state), F32, rows_at(rows, 2 * state, here), NEAR),
            ],
            [],
            (7, 1000000),
            "inside_back",
            None if kept is None else dict(enumerate(kept[:2])),
            after,
        )

    links = chain(meta, message, False)
    next(links)
    held = inside_back(0, None, [])
    sent = links.send([held[-1]])

    pair_shape = (seq_size // 2, share, 2 * inner)
    found = call(
        functools.partial(early_body, shards, count),
        (count,),
        [meta]
        + [
            (far(one), rows_at(rows, part, lambda i: jnp.minimum(i, half_count - 1)))
            for one in cots[0]
        ]
        + [
            (far(one), rows_at(rows, part, lambda i: jnp.maximum(i - half_count, 0)))
            for one in cots[1]
        ]
        + [
            (normed, rows_at(rows, width, fore)),
            (y_norm, rows_at(rows, inner, fore)),
            (dz, rows_at(rows, inner, fore)),
            whole_of(w_out),
            whole_of(w_z),
        ],
        [((tokens, part), BF16, rows_at(rows, part, fore), FAR)] * shards
        + [
            (pair_shape, BF16, whole(pair_shape), FAR),
            (pair_shape, BF16, whole(pair_shape), FAR),
            ((8, width), F32, whole((8, width))),
        ],
        [
            pltpu.VMEM((rows, width), BF16),
            pltpu.VMEM((width, inner), F32),
            pltpu.VMEM((width, inner), F32),
        ],
        (12, 1000000),
        "early",
        after=[held[-1], sent],
    )
    out_parts, (early_keep, early_send, gain_z, done) = found[:shards], found[shards:]
    out_parts = [bare(one) for one in out_parts]
    out_near = scatter_near(out_parts)
    total = links.send([done])
    dxdt, dbc, done = inside_back(1, held, [total])
    outgoing, token, early_send = links.send(([done], [bare(early_send)]))
    early = scatter_seq(meta, bare(early_keep), early_send)
    next(early)
    mixed, near = scatter_far(meta, out_parts, out_near, [done])


    found = call(
        functools.partial(maps_back_body, state, heads, count),
        (count,),
        [
            meta,
            (begin_col, rows_at(rows, 128, back)),
            (bc, rows_at(rows, 2 * state, back)),
            (xdt, rows_at(rows, inner, back)),
            (dy, rows_at(rows, inner, back)),
            (cols, rows_at(rows, 128, back)),
            (slope_bc, rows_at(rows, 2 * state, back)),
            (pre_bc, rows_at(rows, 2 * state, back)),
            whole_of(pre_edge),
            (normed, rows_at(rows, width, back)),
            whole_of(edge_normed),
            whole_of(w_bc),
            (dbc, rows_at(rows, 2 * state, back)),
            (states, stack_at((spans, state, inner), back)),
            (upto, stack_at((spans, 8, inner), back)),
            (dstates, stack_at((spans, state, inner), back)),
            (after, stack_at((spans, 8, inner), back)),
            (own, stack_at((spans, 8, inner), back)),
            whole_of(incoming),
            whole_of(outgoing),
            whole_of(conv_bc_w),
        ],
        [
            ((tokens, 2 * state), BF16, rows_at(rows, 2 * state, back), NEAR),
            ((tokens // SPAN, 8, heads), F32, stack_at((spans, 8, heads), back), NEAR),
            ((tokens // SPAN, state, inner), F32, stack_at((spans, state, inner), back), NEAR),
            ((EDGE, 2 * state), F32, whole((EDGE, 2 * state))),
            ((EDGE, 2 * state), F32, whole((EDGE, 2 * state))),
            ((taps_count, 8, 2 * state), F32, whole((taps_count, 8, 2 * state))),
            ((8, 2 * state), F32, whole((8, 2 * state))),
            ((width // 2, 2 * state), F32, whole((width // 2, 2 * state))),
            ((width // 2, 2 * state), F32, whole((width // 2, 2 * state))),
            ((8, width), F32, whole((8, width))),
        ],
        [
            pltpu.VMEM((rows + 8, 2 * state), F32),
            pltpu.VMEM((rows + 8, 128), jnp.int32),
            pltpu.VMEM((width, 2 * state), F32),
        ],
        (12, 1000000),
        "maps_back",
        after=near,
    )
    dpre_bc, through, ds_all, tail_bc, left_bc, taps_bc, bias_bc = found[:7]
    bc_keep, bc_send, gain_bc, done = found[7:]
    left_pairs = [(i + 1, i) for i in range(seq_size - 1)]
    right_bc = lax.ppermute(left_bc, "seq", left_pairs)
    bc_sums = sum_rows_everywhere(meta, bc_keep, bc_send)
    next(bc_sums)
    early_sent = early.send([done])
    bc_sent = bc_sums.send([early_sent])

    late_width = inner + 128
    late_shape = (seq_size // 2, share, late_width)

    def inner_back(opens, start, fresh_steps, extra, after):
        steps = fresh_steps if opens else fresh_steps + 1

        def now(i):
            return start + jnp.minimum(i, fresh_steps - 1)

        def late(i):
            return jnp.maximum(i - 1, 0) if opens else start - 1 + i

        def written(i):
            return jnp.maximum(i - 1, 0) if opens else i

        outs = [
            ((half, inner), BF16, rows_at(rows, inner, written), NEAR),
            ((half, heads), BF16, rows_at(rows, heads, written)),
        ]
        sums = [
            ((taps_count, 8, inner), F32, whole((taps_count, 8, inner))),
            ((8, inner), F32, whole((8, inner))),
            ((16, heads), F32, whole((16, heads))),
        ]
        sums_scratch = []
        if opens:
            outs += sums + [
                ((rows, inner), F32, whole((rows, inner))),
                ((rows, heads), BF16, whole((rows, heads))),
                ((EDGE, inner), F32, whole((EDGE, inner))),
                ((width, late_width), F32, whole((width, late_width))),
            ]
        else:
            outs += [
                (late_shape, BF16, whole(late_shape)),
                (late_shape, BF16, whole(late_shape)),
                ((8, inner), F32, whole((8, inner))),
                ((8, 2 * state + width), F32, whole((8, 2 * state + width))),
            ]
            sums_scratch = [pltpu.VMEM(shape, F32) for shape, _, _ in sums]
            sums_scratch += [pltpu.VMEM((width, late_width), F32)]
        return call(
            functools.partial(inner_back_body, state, heads, start, fresh_steps, opens),
            (steps,),
            [
                meta,
                (begin_col, rows_at(rows, 128, now)),
                (begin_col, rows_at(rows, 128, late)),
                (bc, rows_at(rows, 2 * state, now)),
                (x, rows_at(rows, inner, now)),
                (xdt, rows_at(rows, inner, now)),
                (dy, rows_at(rows, inner, now)),
                (y, rows_at(rows, inner, now)),
                (cols, rows_at(rows, 128, now)),
                (slope_x, rows_at(rows, inner, now)),
                (pre_x, rows_at(rows, inner, late)),
                (normed, rows_at(rows, width, late)),
                (dxdt, rows_at(rows, inner, now)),
                (through, stack_at((spans, 8, heads), now)),
                (ds_all, stack_at((spans, state, inner), now)),
                whole_of(skip),
                whole_of(rate),
                whole_of(conv_x_w),
            ]
            + [whole_of(one) for one in extra],
            outs,
            sums_scratch
            + [
                pltpu.VMEM((rows + 8, inner), F32),
                pltpu.VMEM((rows + 8, 128), jnp.int32),
                pltpu.VMEM((rows, inner), F32),
                pltpu.VMEM((rows, heads), BF16),
                pltpu.VMEM((rows, heads), BF16),
            ],
            (6 * fresh_steps, 1000000),
            "inner_back",
            after=after,
        )

    found = inner_back(True, 0, count - 1, [pre_edge], [early_sent, bc_sent])
    early_last = rest_of(early, early.send([found[-1]]))
    if shards > 4:
        bc_sums.send([found[-1]])
    bc_sent = bc_sums.send([found[-1]])
    dpre_low, ddt_low, taps_x, bias_x, scalars, held_du, held_ddt, left_x, weight_x, done = found
    right_x = lax.ppermute(left_x, "seq", left_pairs)

    def input_grad(chunk, dpre, ddt, extra, after, carry=()):
        start = chunk * half_count

        def here(i):
            return start + i

        whole_rows = half + EDGE
        return call(
            functools.partial(input_body, shards, half_count, chunk == 1),
            (half_count,),
            [meta]
            + [(far(one), rows_at(rows, part, fore)) for one in xs[chunk]]
            + [
                (dz, rows_at(rows, inner, here)),
                (dpre, rows_at(rows, inner, fore)),
                (dpre_bc, rows_at(rows, 2 * state, here)),
                (ddt, rows_at(rows, heads, fore)),
            ]
            + [whole_of(one) for one in [w_z, w_x, w_bc, w_dt, scale] + extra],
            [((whole_rows, part), BF16, whole((whole_rows, part)))] * shards,
            [pltpu.VMEM((rows, 2 * state), BF16), pltpu.VMEM((EDGE, part), F32)],
            (8, 1000000),
            "input_grad",
            after=after,
            carry=carry,
        )

    *parts_low, done = input_grad(0, dpre_low, ddt_low, [], [bc_sent])
    near_low = scatter_near(parts_low)
    bc_sent = bc_sums.send([done])

    found = inner_back(
        False,
        count - 1,
        1,
        [held_du, held_ddt, right_x, taps_x, bias_x, scalars, weight_x]
        + [w_x, w_dt, scale_row, gain_z, gain_bc]
        + [g_norm_inner, g_skip, taps_bc, bias_bc],
        [bc_sent],
    )
    dpre_high, ddt_high, late_keep, late_send, owned, shared, done = found
    bc_sent = bc_sums.send([done])
    late = scatter_seq(meta, late_keep, late_send)
    next(late)
    got = swap(shared, "head", 1)
    shared = added(meta, shared, got, [bc_sent])
    far_low, near_low = scatter_far(meta, parts_low, near_low, [shared])
    for bit in range(1, shards.bit_length() - 1):
        got = swap(shared, "head", 1 << bit)
        if bit < shards.bit_length() - 2:
            shared = added(meta, shared, got, ())

    results = input_grad(
        1,
        dpre_high,
        ddt_high,
        [tail_bc, right_bc],
        near_low + [bc_sent],
        [mixed[0], early_last[0]],
    )
    parts_high, (done, *own_terms) = results[:shards], results[shards:]
    mixed[0], early_keep = own_terms
    near_high = scatter_near(parts_high)
    shared = shared + got
    late_sent = late.send([done])
    far_high, _ = scatter_far(meta, parts_high, near_high, ())

    grad_input = None
    for chunk, near in enumerate((far_low, far_high)):
        spot = functools.partial(lambda chunk, i: chunk + i, chunk)
        grad_input, done = call(
            functools.partial(final_body, shards, heads),
            (1,),
            [meta]
            + [whole_of(one) for one in near]
            + [
                (own_halves[chunk], rows_at(half, part, fore)),
                (cotangent, rows_at(half, part, spot)),
                (cols, rows_at(half, 128, spot)),
                whole_of(scale),
            ],
            [((tokens, part), F32, rows_at(half, part, spot))],
            [],
            (3, 1000000),
            "input_sum",
            None if grad_input is None else {0: grad_input},
        )

    small = sum_along(jnp.concatenate([owned, shared], axis=1), "seq")
    grad_gain = lax.dynamic_slice_in_dim(small[0, inner + 2 * state :], me * part, part, 0)
    output = add_all([inputs.astype(F32)] + [one.astype(F32) for one in mixed]).astype(BF16)
    sums = []
    for kept, got in ((early_keep, early_last[1]), rest_of(late, late_sent)):
        sums.append((kept.astype(F32) + got.astype(F32)).reshape(kept.shape[-2:]))
    early_grads, late_grads = sums
    grad_w_bc = rest_of(bc_sums, bc_sent).astype(F32)
    return (
        output,
        grad_input,
        grad_gain,
        early_grads[:, :inner],
        late_grads[:, :inner],
        grad_w_bc,
        late_grads[:, inner : inner + heads],
        small[:taps_count, :inner],
        small[4, :inner],
        small[:taps_count, inner : inner + 2 * state],
        small[4, inner : inner + 2 * state],
        small[7, :heads],
        small[7, 128 : 128 + heads],
        jnp.sum(small[6, :inner].reshape(heads, size), axis=1),
        small[5, :inner],
        early_grads[:, inner:].T,
    )


def solution(mesh):
    placed = (
        P("seq", "head"),
        P(),
        P(None, "head"),
        P(None, "head"),
        P(),
        P(None, "head"),
        P(None, "head"),
        P("head"),
        P(),
        P(),
        P("head"),
        P("head"),
        P("head"),
        P("head"),
        P("head", None),
        P("seq", "head"),
        P(),
        P(),
    )
    return jax.shard_map(
        on_device,
        mesh=mesh,
        in_specs=placed,
        out_specs=(
            P("seq", "head"),
            P("seq", "head"),
            P("head"),
            P("seq", "head"),
            P("seq", "head"),
            P(),
            P("seq", "head"),
            P(None, "head"),
            P("head"),
            P(),
            P(),
            P("head"),
            P("head"),
            P("head"),
            P("head"),
            P("head", "seq"),
        ),
        check_vma=False,
    )
```

```python
import functools

import jax
import jax.numpy as jnp
from jax import lax
from jax.experimental import pallas as pl
from jax.experimental.pallas import tpu as pltpu
from jax.sharding import PartitionSpec as P

SPAN = 256
EDGE = 16
EPSILON = 1e-05
F32 = jnp.float32
BF16 = jnp.bfloat16
NEAR, FAR = pltpu.VMEM, pltpu.HBM
ROOM_PROJECT, ROOM_INSIDE, ROOM_GATE, ROOM_NORM = 14, 8, 6, 8
ROOM_EARLY, ROOM_MAPS, ROOM_INNER, ROOM_INPUT = 20, 12, 22, 12


def mm(left, right):
    return lax.dot_general(left, right, (((1,), (0,)), ((), ())), preferred_element_type=F32)


def mm_nt(left, right):
    return lax.dot_general(left, right, (((1,), (1,)), ((), ())), preferred_element_type=F32)


def mm_tn(left, right):
    return lax.dot_general(left, right, (((0,), (0,)), ((), ())), preferred_element_type=F32)


def pieces(values, count):
    found = []
    for _ in range(count):
        part = values.astype(BF16)
        found.append(part)
        values = values - part.astype(F32)
    return found


def add_all(terms):
    total = terms[0]
    for term in terms[1:]:
        total = total + term
    return total


def triangle(size, keep):
    rows = lax.broadcasted_iota(jnp.int32, (size, size), 0)
    cols = lax.broadcasted_iota(jnp.int32, (size, size), 1)
    return keep(rows, cols).astype(F32).astype(BF16)


def expander(heads, width, copies=1):
    rows = lax.broadcasted_iota(jnp.int32, (copies * heads, width), 0) & (heads - 1)
    cols = lax.broadcasted_iota(jnp.int32, (copies * heads, width), 1)
    size = width // heads
    return ((cols >= rows * size) & (cols < (rows + 1) * size)).astype(F32).astype(BF16)


def expand(values, spread):
    count = spread.shape[0] // values.shape[1]
    parts = [part.astype(F32) for part in pieces(values, count)]
    return mm(jnp.concatenate(parts, axis=1).astype(BF16), spread)


def per_head(values, spread, count=2):
    return add_all([mm_nt(part, spread) for part in pieces(values, count)])


def widen(column, width):
    lanes = column.shape[1]
    if width <= lanes:
        return column[:, :width]
    return jnp.concatenate([column] * (width // lanes), axis=1)


def row_ids(rows, lanes=128):
    return lax.broadcasted_iota(jnp.int32, (rows, lanes), 0)


def sigmoid(values):
    return 0.5 * jnp.tanh(0.5 * values) + 0.5


def softplus(values):
    return jnp.maximum(values, 0.0) + jnp.log1p(jnp.exp(-jnp.abs(values)))


def rows_of_sums(first, second):
    lane = lax.broadcasted_iota(jnp.int32, (first.shape[0], 128), 1)
    one = jnp.sum(first, axis=1, keepdims=True)
    two = jnp.sum(second, axis=1, keepdims=True)
    return jnp.where(lane == 0, one, jnp.where(lane == 1, two, 0.0)).T[:8]


def row_of_sums(values):
    lane = lax.broadcasted_iota(jnp.int32, (values.shape[0], 128), 1)
    return jnp.where(lane == 0, jnp.sum(values, axis=1, keepdims=True), 0.0).T[:8]


def column_of(rows, at):
    picks = (lax.broadcasted_iota(jnp.int32, (8, 128), 0) == at).astype(F32).astype(BF16)
    return add_all([mm_tn(part, picks) for part in pieces(rows, 3)])


def fold_rows(values):
    rows, lanes = values.shape
    return jnp.sum(values.reshape(rows // 8, 8, lanes), axis=0)


def halves_of(values):
    high = values.astype(BF16)
    return high, (values - high.astype(F32)).astype(BF16)


class Held:
    def __init__(self, array, space):
        self.array, self.space, self.shape = array, space, array.shape


def bare(one):
    return one.array if isinstance(one, Held) else one


def stays(one):
    return pltpu.with_memory_space_constraint(one.array, one.space) if isinstance(one, Held) else one


def call(body, grid, ins, outs, scratch, work, name, kept=None, after=(), carry=(), room=24):
    arrays = [ins[0]] + [stays(one[0]) for one in ins[1:]]
    specs = [one[1] for one in ins[1:]]
    aliases = {}
    own = len(arrays)
    for at, array in (kept or {}).items():
        aliases[len(arrays)] = at
        arrays.append(stays(array))
        specs.append(pl.BlockSpec(memory_space=pl.ANY))
    for array in after:
        arrays.append(stays(array))
        specs.append(pl.BlockSpec(memory_space=pl.ANY))
    for at, array in enumerate(carry):
        aliases[len(arrays)] = len(outs) + 1 + at
        arrays.append(array)
        specs.append(pl.BlockSpec(memory_space=pl.ANY))
    total = len(arrays)
    spaces = [one[3] if len(one) > 3 else None for one in outs]

    def only_own(*refs):
        token = refs[total + len(outs)]
        token[...] = jnp.zeros_like(token)
        body(*refs[:own], *refs[total : total + len(outs)], *refs[total + len(outs) + 1 + len(carry) :])

    found = pl.pallas_call(
        only_own,
        out_shape=[
            space(one[0], one[1]) if space else jax.ShapeDtypeStruct(one[0], one[1])
            for one, space in zip(outs, spaces)
        ]
        + [jax.ShapeDtypeStruct((8, 128), F32)]
        + [jax.ShapeDtypeStruct(one.shape, one.dtype) for one in carry],
        grid_spec=pltpu.PrefetchScalarGridSpec(
            num_scalar_prefetch=1,
            grid=grid,
            in_specs=specs,
            out_specs=[one[2] for one in outs]
            + [whole((8, 128))]
            + [pl.BlockSpec(memory_space=pl.ANY)] * len(carry),
            scratch_shapes=scratch,
        ),
        input_output_aliases=aliases,
        compiler_params=pltpu.CompilerParams(
            dimension_semantics=("arbitrary",) * len(grid), vmem_limit_bytes=room * 1024 * 1024
        ),
        cost_estimate=pl.CostEstimate(
            flops=int(work[0] * 1e9), bytes_accessed=int(work[1]), transcendentals=0
        ),
        name=name,
    )(*arrays)
    made = [Held(one, space) if space else one for one, space in zip(found, spaces)]
    return made + list(found[len(outs) :])


def rows_at(rows, lanes, step):
    return pl.BlockSpec((rows, lanes), lambda i, meta: (step(i), 0))


def lanes_at(rows, lanes, step):
    return pl.BlockSpec((rows, lanes), lambda i, meta: (0, step(i)))


def stack_at(shape, step):
    return pl.BlockSpec(shape, lambda i, meta: (step(i),) + (0,) * (len(shape) - 1))


def whole(shape):
    return pl.BlockSpec(shape, lambda i, meta: (0,) * len(shape))


def whole_of(array):
    return (array, whole(array.shape))


def block_at(me, k, size):
    return pl.ds(pl.multiple_of((me ^ k) * size, size), size)


LAST = 3
DT, RAW, RUN, REACH, KEEP, INV = range(6)


def column(ref, which, heads):
    return ref[:, which * heads : (which + 1) * heads]


def project_body(shards, inner, state, heads, start, steps, opens, closes, meta, *refs):
    refs = list(refs)

    def take(amount):
        found = refs[:amount]
        del refs[:amount]
        return found

    xs = take(shards)
    if opens:
        edges = take(shards)
    else:
        tail_in, carry_in, decay_in = take(3)
    begin_ref, scale, w_x, w_maps, taps, bias, dt_bias, rate = take(8)
    (
        normed_ref,
        pre_x_ref,
        pre_bc_ref,
        x_ref,
        xdt_ref,
        bc_ref,
        slope_x_ref,
        slope_bc_ref,
        cols_ref,
        runt_ref,
        state_ref,
        upto_ref,
        own_ref,
    ) = take(13)
    if opens:
        edge_ref, edge_normed = take(2)
    if closes:
        (message_ref,) = take(1)
    else:
        tail_ref, carry_out, decay_out = take(3)
    ext, carry, decay = take(3)
    step = pl.program_id(0)
    me = meta[1]
    rows = x_ref.shape[0]
    part = xs[0].shape[1]
    width = part * shards
    maps = 2 * state
    at_block = (start + step) * (rows // SPAN)
    first = meta[0] + at_block * SPAN

    def normalise(sources, target):
        loaded = [source[...].astype(F32) for source in sources]
        total = jnp.sum(add_all([one * one for one in loaded]), axis=1, keepdims=True)
        inverse = lax.rsqrt(total / width + EPSILON)
        for k, one in enumerate(loaded):
            target[:, block_at(me, k, part)] = (one * inverse * scale[me ^ k]).astype(BF16)
        return inverse

    @pl.when(step == 0)
    def _():
        if opens:
            normalise(edges, edge_normed)
            held = edge_normed[...]
            edge_ref[:, :inner] = mm(held, w_x[...]).astype(BF16)
            edge_ref[:, inner:] = mm(held, w_maps[:, :maps]).astype(BF16)
            ext[:8, :] = edge_ref[EDGE - 8 :, :].astype(F32)
            carry[...] = jnp.zeros_like(carry)
            decay[...] = jnp.ones_like(decay)
        else:
            ext[:8, :] = tail_in[EDGE - 8 :, :].astype(F32)
            carry[...] = carry_in[...]
            decay[...] = decay_in[...]

    @pl.when(step > 0)
    def _():
        ext[:8, :] = ext[rows : rows + 8, :]

    inverse = normalise(xs, normed_ref)
    held = normed_ref[...]
    pre_x_ref[...] = mm(held, w_x[...]).astype(BF16)
    both = mm(held, w_maps[...])
    pre_bc_ref[...] = both[:, :maps].astype(BF16)
    ext[8:, :inner] = pre_x_ref[...].astype(F32)
    ext[8:, inner:] = pre_bc_ref[...].astype(F32)
    raw = both[:, maps : maps + heads] + dt_bias[...]
    dt = softplus(raw)

    begin = begin_ref[...]
    place = row_ids(rows) + first
    reach = taps.shape[0] - 1
    channels = ext.shape[1]
    total = bias[...] + taps[reach : reach + 1, :] * ext[8:, :]
    for lag in range(1, reach + 1):
        valid = widen((place - lag >= begin).astype(F32), channels)
        lagged = ext[8 - lag : 8 - lag + rows, :] * valid
        total = total + taps[reach - lag : reach - lag + 1, :] * lagged
    sig = sigmoid(total)
    conv = total * sig
    slope = (sig * (1.0 + total * (1.0 - sig))).astype(BF16)
    slope_x_ref[...] = slope[:, :inner]
    slope_bc_ref[...] = slope[:, inner:]
    x = conv[:, :inner]
    x_ref[...] = x.astype(BF16)
    bc = conv[:, inner:].astype(BF16)
    bc_ref[...] = bc

    spread = expander(heads, inner, 2)
    xdt_ref[...] = (x * expand(dt, spread)).astype(BF16)
    log_decay = dt * rate[...]
    lower = triangle(SPAN, lambda r, c: r >= c)
    upper = triangle(SPAN, lambda r, c: r <= c)
    spans = [slice(s * SPAN, (s + 1) * SPAN) for s in range(rows // SPAN)]
    runs, tails, reaches, keeps, owns = [], [], [], [], []
    for s, at in enumerate(spans):
        parts = [part.astype(F32) for part in pieces(log_decay[at], 3)]
        parts = jnp.concatenate(parts, axis=1).astype(BF16)
        sums = mm(lower, parts)
        runs.append(sums[:, :heads] + sums[:, heads : 2 * heads] + sums[:, 2 * heads :])
        sums = mm_tn(parts, upper)
        runt_ref[:, at] = sums[:heads] + sums[heads : 2 * heads] + sums[2 * heads :]
    for s, at in enumerate(spans):
        run = runs[s]
        tail = run[SPAN - 1 : SPAN, :]
        last = meta[LAST + at_block + s]
        keeps.append(jnp.exp(tail - run) * (place[at] >= last).astype(F32)[:, :heads])
        reaches.append(jnp.exp(run) * (begin[at] < first + s * SPAN).astype(F32)[:, :heads])
        alive = (last < first + s * SPAN).astype(F32)
        owns.append(jnp.broadcast_to(jnp.exp(tail) * alive, (8, heads)))
    keep = jnp.concatenate(keeps, axis=0)
    run, reached = jnp.concatenate(runs, axis=0), jnp.concatenate(reaches, axis=0)
    columns = [dt, raw, run, reached, keep, jnp.broadcast_to(inverse, (rows, heads))]
    rest = cols_ref.shape[1] - len(columns) * heads
    cols_ref[...] = jnp.concatenate(columns + [jnp.zeros((rows, rest), F32)], axis=1)
    high, low = halves_of(x * expand(keep * dt, spread))
    own_all = expand(jnp.concatenate(owns, axis=0), expander(heads, inner, 3))
    for s, at in enumerate(spans):
        own = own_all[8 * s : 8 * s + 8]
        state_ref[s] = carry[...]
        upto_ref[s] = decay[...]
        own_ref[s] = own
        b = bc[at, :state]
        carry[...] = own[:1] * carry[...] + (mm_tn(b, high[at]) + mm_tn(b, low[at]))
        decay[...] = decay[...] * own

    @pl.when(step == steps - 1)
    def _():
        if closes:
            pack_message(message_ref, carry[...], decay[...])
        else:
            tail_ref[:, :inner] = pre_x_ref[rows - EDGE :, :]
            tail_ref[:, inner:] = pre_bc_ref[rows - EDGE :, :]
            carry_out[...] = carry[...]
            decay_out[...] = decay[...]


def pack_message(target, carry, decay):
    state = carry.shape[0]
    target[:state, :] = carry
    target[state:, :] = decay


def assemble(sources, me, target):
    part = sources[0].shape[1]
    for k, source in enumerate(sources):
        target[:, block_at(me, k, part)] = source[...]


def inside_body(shards, state, heads, start, meta, *refs):
    cots, refs = refs[:shards], refs[shards:]
    begin_ref, bc_ref, xdt_ref, cols_ref, runt_ref, normed_ref, w_z, w_out = refs[:8]
    y_ref, z_ref, grad_ref, cot = refs[8:]
    z_ref[...] = mm(normed_ref[...], w_z[...])
    assemble(cots, meta[1], cot)
    grad_ref[...] = mm_nt(cot[...], w_out[...])
    rows, inner = y_ref.shape
    first = meta[0] + (start + pl.program_id(0)) * rows
    row = lax.broadcasted_iota(jnp.int32, (SPAN, SPAN), 0)
    col = lax.broadcasted_iota(jnp.int32, (SPAN, SPAN), 1)
    size = inner // heads
    lane = lax.broadcasted_iota(jnp.int32, (SPAN, 2 * size), 1)
    for s in range(rows // SPAN):
        at = slice(s * SPAN, (s + 1) * SPAN)
        begin = widen(begin_ref[at, :], SPAN)
        allowed = (col <= row) & (col + (first + s * SPAN) >= begin)
        scores = mm_nt(bc_ref[at, state:], bc_ref[at, :state])
        scores = jnp.where(allowed, scores, 0.0)
        for pair in range(heads // 2):
            lanes = slice(pair * 2 * size, (pair + 1) * 2 * size)
            both = xdt_ref[at, lanes]
            total = None
            for j in range(2):
                h = 2 * pair + j
                lane_at = RUN * heads + h
                spread = cols_ref[at, lane_at : lane_at + 1] - runt_ref[h : h + 1, at]
                mixing = (scores * jnp.exp(jnp.minimum(spread, 0.0))).astype(BF16)
                mine = jnp.where((lane < size) == (j == 0), both, jnp.zeros_like(both))
                product = mm(mixing, mine)
                total = product if total is None else total + product
            y_ref[at, lanes] = total


def gate_body(state, heads, meta, *refs):
    (
        bc_ref,
        x_ref,
        cols_ref,
        z_ref,
        grad_ref,
        inside_ref,
        state_ref,
        upto_ref,
        incoming,
        skip,
        norm_inner,
        y_ref,
        sums_ref,
    ) = refs
    rows, inner = y_ref.shape
    reach = expand(column(cols_ref, REACH, heads), expander(heads, inner, 2))
    for s in range(rows // SPAN):
        at = slice(s * SPAN, (s + 1) * SPAN)
        high, low = halves_of(state_ref[s] + upto_ref[s, :1] * incoming[...])
        c = bc_ref[at, state:]
        y_ref[at, :] = inside_ref[at, :] + (mm(c, high) + mm(c, low)) * reach[at]
    y = y_ref[...] + skip[...] * x_ref[...].astype(F32)
    z = z_ref[...]
    gated = y * (z * sigmoid(z))
    sums_ref[...] = rows_of_sums(gated * gated, grad_ref[...] * norm_inner[...] * gated)


def norm_body(shards, state, heads, count, meta, *refs):
    sums, refs = refs[:shards], refs[shards:]
    (
        bc_ref,
        x_ref,
        cols_ref,
        z_ref,
        y_ref,
        grad_ref,
        own_ref,
        skip,
        norm_inner,
        y_norm_ref,
        dz_ref,
        dy_ref,
        state_ref,
        after_ref,
        message_ref,
        gain_ref,
        skip_ref,
        carry,
        decay,
    ) = refs
    step = pl.program_id(0)
    rows, inner = dy_ref.shape

    @pl.when(step == 0)
    def _():
        carry[...] = jnp.zeros_like(carry)
        decay[...] = jnp.ones_like(decay)
        gain_ref[...] = jnp.zeros_like(gain_ref)
        skip_ref[...] = jnp.zeros_like(skip_ref)

    full = inner * shards
    all_rows = add_all([one[...] for one in sums])
    inverse = widen(lax.rsqrt(column_of(all_rows, 0) / full + EPSILON), inner)
    share = widen(column_of(all_rows, 1) / full, inner) * inverse * inverse * inverse
    x = x_ref[...].astype(F32)
    y = y_ref[...] + skip[...] * x
    z = z_ref[...]
    sig = sigmoid(z)
    gate = z * sig
    gated = y * gate
    hat = gated * inverse
    grad = grad_ref[...]
    gain_ref[...] += fold_rows(grad * hat)
    y_norm_ref[...] = (hat * norm_inner[...]).astype(BF16)
    d_gated = inverse * (grad * norm_inner[...]) - gated * share
    dz_ref[...] = (d_gated * y * (sig + gate * (1.0 - sig))).astype(BF16)
    dy = d_gated * gate
    skip_ref[...] += fold_rows(dy * x)
    dy_ref[...] = dy

    reach = expand(column(cols_ref, REACH, heads), expander(heads, inner, 2))
    high, low = halves_of(dy * reach)
    for s in reversed(range(rows // SPAN)):
        at = slice(s * SPAN, (s + 1) * SPAN)
        c = bc_ref[at, state:]
        state_ref[s] = carry[...]
        after_ref[s] = decay[...]
        carry[...] = own_ref[s, :1] * carry[...] + (mm_tn(c, high[at]) + mm_tn(c, low[at]))
        decay[...] = decay[...] * own_ref[s]

    @pl.when(step == count - 1)
    def _():
        pack_message(message_ref, carry[...], decay[...])


def write_halves(total, mine, keep_ref, send_ref, columns):
    count, share = keep_ref.shape[:2]
    for j in range(count):
        here = pl.ds(pl.multiple_of((2 * j + mine) * share, share), share)
        there = pl.ds(pl.multiple_of((2 * j + 1 - mine) * share, share), share)
        keep_ref[j, :, columns] = total[here, :].astype(keep_ref.dtype)
        send_ref[j, :, columns] = total[there, :].astype(send_ref.dtype)


def early_body(shards, count, meta, *refs):
    cots, late_cots, refs = refs[:shards], refs[shards : 2 * shards], refs[2 * shards :]
    (normed_ref, y_norm_ref, dz_ref, w_out, w_z), refs = refs[:5], refs[5:]
    outs, refs = refs[:shards], refs[shards:]
    keep_ref, send_ref, gain_ref, cot, total_z, total_out = refs
    step = pl.program_id(0)
    me = meta[1]
    part = cots[0].shape[1]
    inner = dz_ref.shape[1]

    @pl.when(step == 0)
    def _():
        total_z[...] = jnp.zeros_like(total_z)
        total_out[...] = jnp.zeros_like(total_out)

    y_norm = y_norm_ref[...]
    for k in range(shards):
        outs[k][...] = mm(y_norm, w_out[:, block_at(me, k, part)]).astype(BF16)

    @pl.when(step < count // 2)
    def _():
        assemble(cots, me, cot)

    @pl.when(step >= count // 2)
    def _():
        assemble(late_cots, me, cot)

    total_z[...] += mm_tn(normed_ref[...], dz_ref[...])
    total_out[...] += mm_tn(cot[...], y_norm)

    @pl.when(step == count - 1)
    def _():
        mine = meta[2] & 1
        write_halves(total_z, mine, keep_ref, send_ref, slice(0, inner))
        write_halves(total_out, mine, keep_ref, send_ref, slice(inner, 2 * inner))
        gain_ref[...] = row_of_sums(total_z[...] * w_z[...].astype(F32))


def inside_back_body(state, heads, start, meta, begin_row, bc_ref, xdt_ref, dy_ref, cols_ref, runt_ref, dxdt_ref, dbc_ref):
    rows, inner = dxdt_ref.shape
    first = meta[0] + (start + pl.program_id(0)) * rows
    row = lax.broadcasted_iota(jnp.int32, (SPAN, SPAN), 0)
    col = lax.broadcasted_iota(jnp.int32, (SPAN, SPAN), 1)
    size = inner // heads
    lane = lax.broadcasted_iota(jnp.int32, (SPAN, 2 * size), 1)
    for s in range(rows // SPAN):
        at = slice(s * SPAN, (s + 1) * SPAN)
        allowed = (row <= col) & (row + (first + s * SPAN) >= begin_row[:1, at])
        b = bc_ref[at, :state]
        c = bc_ref[at, state:]
        scores = jnp.where(allowed, mm_nt(b, c), 0.0)
        d_scores = None
        for pair in range(heads // 2):
            lanes = slice(pair * 2 * size, (pair + 1) * 2 * size)
            x_both = xdt_ref[at, lanes]
            high, low = halves_of(dy_ref[at, lanes])
            total = None
            for j in range(2):
                h = 2 * pair + j
                lane_at = RUN * heads + h
                spread = runt_ref[h : h + 1, at] - cols_ref[at, lane_at : lane_at + 1]
                fade = jnp.exp(jnp.minimum(spread, 0.0))
                mixing = (scores * fade).astype(BF16)
                mine = (lane < size) == (j == 0)
                high_mine = jnp.where(mine, high, jnp.zeros_like(high))
                low_mine = jnp.where(mine, low, jnp.zeros_like(low))
                product = mm(mixing, high_mine)
                total = product if total is None else total + product
                faded = (mm_nt(x_both, high_mine) + mm_nt(x_both, low_mine)) * fade
                d_scores = faded if d_scores is None else d_scores + faded
            dxdt_ref[at, lanes] = total
        d_scores = jnp.where(allowed, d_scores, 0.0).astype(BF16)
        dbc_ref[at, :state] = mm(d_scores, c)
        dbc_ref[at, state:] = mm_tn(d_scores, b)


def cross_border(fresh, begins, first, edge, taps, taps_ref, lanes):
    reach = taps.shape[0] - 1
    spot = lax.broadcasted_iota(jnp.int32, (8, lanes), 0)
    place = lax.broadcasted_iota(jnp.int32, (8, 128), 0) + (first - 8)
    sent = jnp.zeros((8, lanes), F32)
    for lag in range(1, reach + 1):
        moved = jnp.concatenate([jnp.zeros((8 - lag, lanes), F32), fresh[:lag, :]], axis=0)
        starts = jnp.concatenate([jnp.zeros((8 - lag, 128), jnp.int32), begins[:lag, :]], axis=0)
        valid = widen((place >= starts).astype(F32), lanes)
        moved = jnp.where(spot >= 8 - lag, moved * valid, 0.0)
        sent = sent + taps[reach - lag : reach - lag + 1, :] * moved
        taps_ref[reach - lag] += moved * edge
    return jnp.concatenate([jnp.zeros((EDGE - 8, lanes), F32), sent], axis=0)


def conv_back(ext, begin_ext, place, pre, taps, taps_ref):
    rows, lanes = pre.shape
    reach = taps.shape[0] - 1
    du = ext[:rows, :]
    taps_ref[reach] += fold_rows(du * pre)
    total = taps[reach : reach + 1, :] * du
    for lag in range(1, reach + 1):
        valid = widen((place >= begin_ext[lag : lag + rows, :]).astype(F32), lanes)
        moved = ext[lag : lag + rows, :] * valid
        total = total + taps[reach - lag : reach - lag + 1, :] * moved
        taps_ref[reach - lag] += fold_rows(moved * pre)
    return total


def maps_back_body(state, heads, count, meta, *refs):
    (
        begin_ref,
        bc_ref,
        xdt_ref,
        dy_ref,
        cols_ref,
        slope_ref,
        pre_ref,
        edge_ref,
        normed_ref,
        edge_normed,
        w_bc,
        dbc_ref,
        state_ref,
        upto_ref,
        dstate_ref,
        after_ref,
        own_ref,
        incoming,
        outgoing,
        taps,
        dpre_ref,
        through_ref,
        ds_ref,
        tail_ref,
        left_ref,
        taps_ref,
        bias_ref,
        own_half_ref,
        send_ref,
        gain_ref,
        ext,
        begin_ext,
        weight,
    ) = refs
    step = pl.program_id(0)
    rows, inner = xdt_ref.shape
    at_step = count - 1 - step
    first = meta[0] + at_step * rows
    spread = expander(heads, inner)
    spread_two = expander(heads, inner, 2)

    @pl.when(step == 0)
    def _():
        weight[...] = jnp.zeros_like(weight)
        ext[rows:, :] = jnp.zeros_like(ext[rows:, :])
        begin_ext[rows:, :] = jnp.zeros_like(begin_ext[rows:, :])
        taps_ref[...] = jnp.zeros_like(taps_ref)
        bias_ref[...] = jnp.zeros_like(bias_ref)

    @pl.when(step > 0)
    def _():
        ext[rows:, :] = ext[:8, :]
        begin_ext[rows:, :] = begin_ext[:8, :]

    begin_ext[:rows, :] = begin_ref[...]
    place = row_ids(rows) + first
    keep = expand(column(cols_ref, KEEP, heads), spread_two)
    reach = expand(column(cols_ref, REACH, heads), spread_two)
    x_high, x_low = halves_of(xdt_ref[...].astype(F32) * keep)
    y_high, y_low = halves_of(dy_ref[...] * reach)
    for s in range(rows // SPAN):
        at = slice(s * SPAN, (s + 1) * SPAN)
        s_in = state_ref[s] + upto_ref[s, :1] * incoming[...]
        ds_out = dstate_ref[s] + after_ref[s, :1] * outgoing[...]
        ds_ref[s] = ds_out
        through = jnp.sum((s_in * ds_out).reshape(state // 8, 8, inner), axis=0) * own_ref[s]
        through_ref[s] = jnp.broadcast_to(
            jnp.sum(per_head(through, spread), axis=0, keepdims=True), (8, heads)
        )
        s_high, s_low = halves_of(s_in)
        ds_high, ds_low = halves_of(ds_out)
        d_b = mm_nt(x_high[at], ds_high) + mm_nt(x_low[at], ds_high) + mm_nt(x_high[at], ds_low)
        d_c = mm_nt(y_high[at], s_high) + mm_nt(y_low[at], s_high) + mm_nt(y_high[at], s_low)
        slope = slope_ref[at, :].astype(F32)
        ext[at, :state] = (dbc_ref[at, :state] + d_b) * slope[:, :state]
        ext[at, state:] = (dbc_ref[at, state:] + d_c) * slope[:, state:]
    bias_ref[...] += fold_rows(ext[:rows, :])
    total = conv_back(ext, begin_ext, place, pre_ref[...].astype(F32), taps, taps_ref)
    high, low = halves_of(total)
    dpre_ref[...] = high
    weight[...] += mm_tn(normed_ref[...], high) + mm_tn(normed_ref[...], low)

    @pl.when(step == 0)
    def _():
        tail_ref[...] = total[rows - EDGE :, :]

    @pl.when(step == count - 1)
    def _():
        edge = edge_ref[EDGE - 8 :, inner:].astype(F32)
        left_ref[...] = cross_border(ext, begin_ext, first, edge, taps, taps_ref, 2 * state)
        left_high, left_low = halves_of(left_ref[...])
        weight[...] += mm_tn(edge_normed[...], left_high) + mm_tn(edge_normed[...], left_low)
        half = send_ref.shape[0]
        mine = meta[1] & 1
        here = pl.ds(pl.multiple_of(mine * half, half), half)
        there = pl.ds(pl.multiple_of((1 - mine) * half, half), half)
        own_half_ref[...] = weight[here, :]
        send_ref[...] = weight[there, :]
        gain_ref[...] = row_of_sums(weight[...] * w_bc[...].astype(F32))


def inner_back_body(state, heads, start, fresh_steps, opens, meta, *refs):
    refs = list(refs)

    def take(amount):
        found = refs[:amount]
        del refs[:amount]
        return found

    (
        begin_ref,
        begin_late,
        bc_ref,
        x_ref,
        xdt_ref,
        dy_ref,
        y_ref,
        cols_ref,
        slope_ref,
        pre_late,
        normed_late,
        dxdt_ref,
        through_ref,
        ds_ref,
        skip,
        rate,
        taps,
    ) = take(17)
    if opens:
        (edge_ref,) = take(1)
    else:
        held_in, held_ddt_in, right, taps_in, bias_in, scalar_in, weight_in = take(7)
        w_x, w_dt, scale, gain_z, gain_bc, norm_gain, skip_gain, taps_bc, bias_bc = take(9)
    dpre_ref, ddt_ref = take(2)
    if opens:
        taps_ref, bias_ref, scalar_ref, held_out, held_ddt_out, left_ref, weight = take(7)
    else:
        keep_half_ref, send_ref, owned_ref, shared_ref, taps_ref, bias_ref, scalar_ref, weight = take(8)
    ext, begin_ext, fresh, ddt = take(4)
    step = pl.program_id(0)
    rows, inner = x_ref.shape
    steps = fresh_steps if opens else fresh_steps + 1
    spread = expander(heads, inner)
    spread_two = expander(heads, inner, 2)

    @pl.when(step == 0)
    def _():
        if opens:
            weight[...] = jnp.zeros_like(weight)
            taps_ref[...] = jnp.zeros_like(taps_ref)
            bias_ref[...] = jnp.zeros_like(bias_ref)
            scalar_ref[...] = jnp.zeros_like(scalar_ref)
        else:
            weight[...] = weight_in[...]
            taps_ref[...] = taps_in[...]
            bias_ref[...] = bias_in[...]
            scalar_ref[...] = scalar_in[...]
            ext[:rows, :] = held_in[...]
            ddt[...] = held_ddt_in[...]

    def renew():
        at_block = (start + step) * (rows // SPAN)
        first = meta[0] + at_block * SPAN
        place = row_ids(rows) + first
        suffix = triangle(SPAN, lambda r, c: r <= c)
        prefix = triangle(SPAN, lambda r, c: r > c)
        rate_now = rate[...]
        spans = [slice(s * SPAN, (s + 1) * SPAN) for s in range(rows // SPAN)]
        kept = []
        for s, at in enumerate(spans):
            b = bc_ref[at, :state]
            ds_high, ds_low = halves_of(ds_ref[s])
            kept.append(mm(b, ds_high) + mm(b, ds_low))
        kept = jnp.concatenate(kept, axis=0) * expand(column(cols_ref, KEEP, heads), spread_two)
        dy = dy_ref[...]
        xdt = xdt_ref[...].astype(F32)
        x = x_ref[...].astype(F32)
        dxdt_in = dxdt_ref[...]
        dxdt = dxdt_in + kept
        dt = column(cols_ref, DT, heads)
        d_x = dxdt * expand(dt, spread_two) + skip[...] * dy
        du = d_x * slope_ref[...].astype(F32)
        fresh[...] = du
        bias_ref[...] += fold_rows(du)
        dy_high = dy.astype(BF16).astype(F32)
        later = per_head(dy_high * y_ref[...] - xdt * dxdt_in, spread, 3)
        earlier = per_head(xdt * kept, spread)
        direct = per_head(x * dxdt, spread)
        q = []
        for s, at in enumerate(spans):
            after = [part.astype(F32) for part in pieces(later[at], 3)]
            after = mm(suffix, jnp.concatenate(after, axis=1).astype(BF16))
            before = [part.astype(F32) for part in pieces(earlier[at], 2)]
            before = mm(prefix, jnp.concatenate(before, axis=1).astype(BF16))
            q.append(
                (after[:, :heads] + after[:, heads : 2 * heads] + after[:, 2 * heads :])
                + (before[:, :heads] + before[:, heads:])
                + through_ref[s, :1, :]
            )
        starts = (place == begin_ref[...]).astype(F32)[:, :heads]
        q = jnp.concatenate(q, axis=0) * (1.0 - starts)
        d_raw = (direct + rate_now * q) / (1.0 + jnp.exp(-column(cols_ref, RAW, heads)))
        fresh_ddt[...] = d_raw.astype(BF16)
        scalar_ref[:8, :] += fold_rows(d_raw)
        scalar_ref[8:, :] += fold_rows(rate_now * dt * q)

    fresh_ddt = refs[0]

    def finish(closing=False):
        begin_ext[:rows, :] = begin_late[...]
        first = meta[0] + (start - (0 if opens else 1) + step - (1 if opens else 0)) * rows
        place = row_ids(rows) + first
        total = conv_back(ext, begin_ext, place, pre_late[...].astype(F32), taps, taps_ref)
        dpre_ref[...] = total.astype(BF16)
        if closing:
            dpre_ref[rows - EDGE :, :] = (total[rows - EDGE :, :] + right[...]).astype(BF16)
        ddt_ref[...] = ddt[...]
        held = normed_late[...]
        weight[:, :inner] += mm_tn(held, dpre_ref[...])
        weight[:, inner : inner + heads] += mm_tn(held, ddt[...])

    if opens:
        renew()

        @pl.when(step == 0)
        def _():
            edge = edge_ref[EDGE - 8 :, :inner].astype(F32)
            left_ref[...] = cross_border(fresh, begin_ref, meta[0], edge, taps, taps_ref, inner)

        @pl.when(step > 0)
        def _():
            ext[rows:, :] = fresh[:8, :]
            begin_ext[rows:, :] = begin_ref[:8, :]
            finish()

        ext[:rows, :] = fresh[...]
        ddt[...] = fresh_ddt[...]

        @pl.when(step == steps - 1)
        def _():
            held_out[...] = fresh[...]
            held_ddt_out[...] = fresh_ddt[...]
    else:

        @pl.when(step < steps - 1)
        def _():
            renew()
            ext[rows:, :] = fresh[:8, :]
            begin_ext[rows:, :] = begin_ref[:8, :]
            finish()
            ext[:rows, :] = fresh[...]
            ddt[...] = fresh_ddt[...]

        @pl.when(step == steps - 1)
        def _():
            ext[rows:, :] = jnp.zeros((8, inner), F32)
            begin_ext[rows:, :] = jnp.zeros((8, 128), jnp.int32)
            finish(True)
            write_halves(weight, meta[2] & 1, keep_half_ref, send_ref, slice(0, weight.shape[1]))
            gain = row_of_sums(weight[:, :inner] * w_x[...].astype(F32))
            gain_dt = row_of_sums(weight[:, inner : inner + heads] * w_dt[...].astype(F32))
            owned_ref[...] = jnp.zeros_like(owned_ref)
            shared_ref[...] = jnp.zeros_like(shared_ref)

            def one_row(values):
                return jnp.sum(values, axis=0, keepdims=True)

            for j in range(taps.shape[0]):
                owned_ref[j : j + 1, :] = one_row(taps_ref[j])
                shared_ref[j : j + 1, : 2 * state] = one_row(taps_bc[j])
            owned_ref[4:5, :] = one_row(bias_ref[...])
            shared_ref[4:5, : 2 * state] = one_row(bias_bc[...])
            owned_ref[5:6, :] = one_row(norm_gain[...])
            owned_ref[6:7, :] = one_row(skip_gain[...])
            owned_ref[7:8, :heads] = one_row(scalar_ref[:8, :])
            owned_ref[7:8, 128 : 128 + heads] = one_row(scalar_ref[8:, :])
            shared_ref[:, 2 * state :] = (gain + gain_dt + gain_z[...] + gain_bc[...]) / scale[...]


def input_body(shards, steps, closes, meta, *refs):
    xs, refs = refs[:shards], refs[shards:]
    dz_ref, dpre_ref, dbc_ref, ddt_ref, w_z, w_x, w_bc, w_dt, scale = refs[:9]
    refs = refs[9:]
    if closes:
        (tail_ref, right_ref), refs = refs[:2], refs[2:]
    outs, refs = refs[:shards], refs[shards:]
    dbc_held, sums = refs
    step = pl.program_id(0)
    me = meta[1]
    rows, part = xs[0].shape
    per_step = rows // part
    total_rows = steps * rows

    dbc_held[...] = dbc_ref[...]
    if closes:

        @pl.when(step == steps - 1)
        def _():
            dbc_held[rows - EDGE :, :] = (tail_ref[...] + right_ref[...]).astype(BF16)

    dz, dx, dbc, ddt = dz_ref[...], dpre_ref[...], dbc_held[...], ddt_ref[...]
    products = None
    here = pl.ds(pl.multiple_of(step * rows, rows), rows)
    for k in range(shards):
        at = block_at(me, k, part)
        grad = (
            mm_nt(dz, w_z[at, :])
            + mm_nt(dx, w_x[at, :])
            + mm_nt(dbc, w_bc[at, :])
            + mm_nt(ddt, w_dt[at, :])
        )
        outs[k][here, :] = grad.astype(BF16)
        product = grad * scale[me ^ k] * xs[k][...].astype(F32)
        products = product if products is None else products + product
    row = row_of_sums(products)

    @pl.when(step == 0)
    def _():
        sums[...] = jnp.zeros_like(sums)

    for s in range(steps):

        @pl.when(step == s)
        def _(s=s):
            for j in range(per_step):
                spot = s * per_step + j
                sums[spot : spot + 1, :] = row[:1, j * part : (j + 1) * part]

    @pl.when(step == steps - 1)
    def _():
        for k in range(shards):
            outs[k][total_rows:, :] = sums[...].astype(BF16)


def final_body(shards, heads, steps, meta, *refs):
    refs = list(refs)

    def take(amount):
        found = refs[:amount]
        del refs[:amount]
        return found

    count = shards // 2 + 1
    sets = [(take(count), take(count)) for _ in range(2)]
    mixed = take(count)
    x_ref, cot_ref, cols_ref, scale, out_ref, layer_ref = refs
    step = pl.program_id(0)
    me = meta[1]
    rows, part = x_ref.shape
    width = part * shards
    per_step = rows // part
    layer_ref[...] = add_all([one[...].astype(F32) for one in [x_ref] + mixed]).astype(BF16)

    def finish(parts, tails, row):
        sums = add_all([one[...].astype(F32) for one in tails])
        for j in range(per_step):
            at = slice(j * part, (j + 1) * part)
            spot = INV * heads
            inverse = jnp.broadcast_to(cols_ref[at, spot : spot + 1], (part, part))
            group, line = divmod(row + j, 8)
            total = column_of(sums[8 * group : 8 * group + 8], line)
            share = widen(total / width, part) * inverse * inverse * inverse
            grad = add_all([one[at, :].astype(F32) for one in parts]) * scale[me]
            out_ref[at, :] = cot_ref[at, :].astype(F32) + inverse * grad - x_ref[at, :].astype(F32) * share

    for s in range(steps):
        parts, tails = sets[2 * s // steps]

        @pl.when(step == s)
        def _(s=s, parts=parts, tails=tails):
            finish(parts, tails, (s % (steps // 2)) * per_step)


def weights_body(inner, heads, meta, keep_ref, got_ref, late_keep, late_got, z_ref, out_ref, x_ref, dt_ref):
    total = keep_ref[0].astype(F32) + got_ref[0].astype(F32)
    z_ref[...] = total[:, :inner]
    out_ref[...] = total[:, inner:].T
    total = late_keep[0].astype(F32) + late_got[0].astype(F32)
    x_ref[...] = total[:, :inner]
    dt_ref[...] = total[:, inner : inner + heads]


def swap(shard, axis, flip):
    return lax.ppermute(shard, axis, [(i, i ^ flip) for i in range(lax.axis_size(axis))])


def handed(meta, array, after):
    return call(nothing, (1,), [meta], [], [], (1, 1000), "hand_on", after=after, carry=[array], room=2)[-1]


def nothing(meta):
    pass


def gather_far(shard):
    return {k: swap(shard, "head", k) for k in range(2, lax.axis_size("head"), 2)}


def gather_near(shard, far):
    found = []
    for k in range(0, lax.axis_size("head"), 2):
        one = far[k] if k else shard
        found += [one, swap(one, "head", 1)]
    return found


class Stages:
    def __init__(self, steps):
        self.steps = steps
        self.job = next(steps)

    def terms(self, meta, after=()):
        while self.job[0] is not None:
            run_stages(meta, [self], after)
        return self.job[1]


def run_stages(meta, stages, after):
    stages = [one for one in stages if one.job[0] is not None]
    if not stages:
        return []
    jobs = [one.job for one in stages]

    def body(meta, *refs):
        ins, outs = 0, sum(len(job[1]) for job in jobs)
        for work, arrays, shapes in jobs:
            work(meta, *refs[ins : ins + len(arrays)], *refs[outs : outs + len(shapes)])
            ins, outs = ins + len(arrays), outs + len(shapes)

    made = call(
        body,
        (1,),
        [meta] + [whole_of(array) for job in jobs for array in job[1]],
        [(shape, dtype, whole(shape)) for job in jobs for shape, dtype in job[2]],
        [],
        (1, 1000),
        "sums",
        after=after,
        room=14,
    )
    at = 0
    for one, job in zip(stages, jobs):
        one.job = one.steps.send(made[at : at + len(job[2])])
        at += len(job[2])
    return made[:-1]


def near_body(meta, one_ref, two_ref, out_ref):
    out_ref[...] = (one_ref[...].astype(F32) + two_ref[...].astype(F32)).astype(BF16)


def scatter_near(parts):
    return [swap(parts[k + 1], "head", 1) for k in range(0, len(parts), 2)]


def scatter_far(parts, got):
    found = [parts[0], got[0]]
    for k in range(2, len(parts), 2):
        (near,) = yield near_body, [parts[k], got[k // 2]], [(parts[k].shape, BF16)]
        found.append(swap(near, "head", k))
    yield None, found


def add_body(meta, one_ref, two_ref, out_ref):
    out_ref[...] = one_ref[...] + two_ref[...]


def add_head(values):
    bits = lax.axis_size("head").bit_length() - 1
    for bit in range(bits):
        got = swap(values, "head", 1 << bit)
        if bit == bits - 1:
            yield None, (values, got)
        else:
            (values,) = yield add_body, [values, got], [(values.shape, F32)]


def halve_body(axis, bit, meta, keep_ref, got_ref, kept_ref, sent_ref):
    mine = (meta[axis] >> bit) & 1
    for j in range(kept_ref.shape[0]):
        here, there = 2 * j + mine, 2 * j + 1 - mine
        kept_ref[j] = keep_ref[here].astype(F32) + got_ref[here].astype(F32)
        sent_ref[j] = (keep_ref[there].astype(F32) + got_ref[there].astype(F32)).astype(sent_ref.dtype)


def halve(keep, got, bit):
    count, rows, lanes = keep.shape
    shape = (count // 2, rows, lanes)
    return functools.partial(halve_body, 2, bit), [keep, got], [(shape, F32), (shape, got.dtype)]


def scatter_seq(keep, send):
    bits = lax.axis_size("seq").bit_length() - 1
    for bit in range(bits):
        received = swap(send, "seq", 1 << bit)
        if bit < bits - 1:
            keep, send = yield halve(keep, received, bit + 1)
    yield None, (keep, received)


def sum_rows_everywhere(keep, send):
    got = swap(send, "head", 1)
    for bit in range(1, lax.axis_size("head").bit_length() - 1):
        (keep,) = yield add_body, [keep, got], [(keep.shape, F32)]
        got = swap(keep, "head", 1 << bit)
    for bit in reversed(range(lax.axis_size("seq").bit_length() - 1)):
        rows, lanes = keep.shape
        shape = (2, rows // 2, lanes)
        kept, sent = yield halve(keep.reshape(shape), got.reshape(shape), bit)
        keep, sent = kept.reshape(shape[1:]), sent.reshape(shape[1:])
        got = swap(sent, "seq", 1 << bit)
    yield None, (keep, got)


def pack_small(target, at, values):
    lanes = target.shape[1]
    high, low = halves_of(values)
    for t in range(values.shape[1] // lanes):
        part = slice(t * lanes, (t + 1) * lanes)
        both = jnp.concatenate([high[:, part].astype(F32), low[:, part].astype(F32)], axis=0)
        target[at + 16 * t : at + 16 * t + 16, :] = both.astype(BF16)


def unpack_small(source, at):
    rows = source[at:, :].astype(F32)
    pieces_found = [
        rows[16 * t : 16 * t + 8] + rows[16 * t + 8 : 16 * t + 16] for t in range(rows.shape[0] // 16)
    ]
    return jnp.concatenate(pieces_found, axis=1)


def open_body(meta, keep_ref, got_ref, owned_ref, shared_ref, more_ref, out_ref):
    rows = keep_ref.shape[0]
    out_ref[:rows, :] = (keep_ref[...] + got_ref[...]).astype(BF16)
    shared = shared_ref[...] + more_ref[...]
    pack_small(out_ref, rows, jnp.concatenate([owned_ref[...], shared], axis=1))


def widen_body(bit, rows, last, meta, own_ref, got_ref, out_ref, *small_ref):
    mine = (meta[2] >> bit) & 1
    own, got = own_ref[:rows, :], got_ref[:rows, :]
    out_ref[:rows, :] = jnp.where(mine == 0, own, got)
    out_ref[rows : 2 * rows, :] = jnp.where(mine == 0, got, own)
    small = unpack_small(own_ref, rows) + unpack_small(got_ref, rows)
    if not last:
        pack_small(out_ref, 2 * rows, small)
        return
    taps_x, bias_x, gain_x, skip_x, bias_dt, rate_x, taps_bc, bias_bc, gain_in, held = small_ref
    inner, maps, part = bias_x.shape[1], bias_bc.shape[1], gain_in.shape[1]
    heads = skip_x.shape[1]
    reach = taps_x.shape[0]
    taps_x[...] = small[:reach, :inner]
    bias_x[...] = small[4:5, :inner]
    gain_x[...] = small[5:6, :inner]
    skip_x[...] = per_head(small[:, :inner], expander(heads, inner), 3)[6:7]
    bias_dt[...] = small[7:8, :heads]
    rate_x[...] = small[7:8, 128 : 128 + heads]
    taps_bc[...] = small[:reach, inner : inner + maps]
    bias_bc[...] = small[4:5, inner : inner + maps]
    held[...] = small[:, inner + maps :]
    gain_in[...] = held[:1, pl.ds(pl.multiple_of(meta[1] * part, part), part)]


def end_sums(terms, owned, shared, more, heads, reach, part):
    keep, got = terms
    rows, lanes = keep.shape
    width = owned.shape[1] + shared.shape[1]
    extra = 16 * (width // lanes)
    (held,) = yield open_body, [keep, got, owned, shared, more], [((rows + extra, lanes), BF16)]
    bits = lax.axis_size("seq").bit_length() - 1
    for bit in range(bits):
        got = swap(held, "seq", 1 << bit)
        last = bit == bits - 1
        outs = [((2 * rows + (0 if last else extra), lanes), BF16)]
        if last:
            inner = owned.shape[1]
            small = [(reach, inner), (1, inner), (1, inner), (1, heads), (1, heads), (1, heads)]
            small += [(reach, lanes), (1, lanes), (1, part), (8, width - inner - lanes)]
            outs += [(one, F32) for one in small]
        found = yield functools.partial(widen_body, bit, rows, last), [held, got], outs
        held, rows = found[0], 2 * rows
    mine = lax.axis_index("head") & 1
    other = swap(held, "head", 1)
    low, high = jnp.where(mine == 0, held, other), jnp.where(mine == 0, other, held)
    yield None, (jnp.concatenate([low, high], axis=0).astype(F32), found[1:-1])


def pair_body(forward, meta, own_ref, got_ref, sent_ref, pair):
    state = own_ref.shape[0] - 8
    half = state // 2
    odd = meta[2] & 1
    own_last = odd == (1 if forward else 0)
    own_fade, fade = own_ref[state:, :], got_ref[state:, :]
    own, other = own_ref[:state, :], got_ref[:state, :]
    pair[...] = jnp.where(own_last, own_fade[:1] * other + own, fade[:1] * own + other)
    sent_ref[:half, :] = pair[pl.ds(pl.multiple_of(odd * half, half), half), :]
    sent_ref[half:, :] = own_fade * fade


def fold_body(count, meta, *refs):
    total_ref = refs[count]
    half = total_ref.shape[0]
    total = jnp.zeros(total_ref.shape, F32)
    for one in reversed(refs[:count]):
        total = one[half : half + 1, :] * total + one[:half, :]
    total_ref[...] = total


def join_body(forward, meta, total_ref, rest_ref, got_ref, out_ref):
    state = out_ref.shape[0]
    odd = meta[2] & 1
    own_last = odd == (1 if forward else 0)
    total, rest = total_ref[...], rest_ref[...]
    low, high = jnp.where(odd == 0, total, rest), jnp.where(odd == 0, rest, total)
    total = jnp.concatenate([low, high], axis=0)
    fade, other = got_ref[state : state + 1, :], got_ref[:state, :]
    out_ref[...] = jnp.where(own_last, fade * total + other, total)


def chain(meta, message, forward):
    size = lax.axis_size("seq")
    rows, lanes = message.shape
    state = rows - 8
    half = state // 2

    def small(body, arrays, shape, scratch, name, after=(), carry=()):
        return call(
            body,
            (1,),
            [meta] + [whole_of(one) for one in arrays],
            [(shape, F32, whole(shape))],
            scratch,
            (1, 1000),
            name,
            after=after,
            carry=carry,
            room=8,
        )

    got = swap(message, "seq", 1)
    after = yield None
    sent = small(
        functools.partial(pair_body, forward),
        [message, got],
        (half + 8, lanes),
        [pltpu.VMEM((state, lanes), F32)],
        "pair",
        after,
    )[0]
    found = []
    for by in range(2, size, 2):
        if forward:
            pairs = [(i, i + by) for i in range(size - by)]
        else:
            pairs = [(i + by, i) for i in range(size - by)]
        found.append(lax.ppermute(sent, "seq", pairs))
    after = yield sent
    total = small(
        functools.partial(fold_body, len(found)), found, (half, lanes), [], "fold", after
    )[0]
    rest = swap(total, "seq", 1)
    after, carry = yield total
    body = functools.partial(join_body, forward)
    yield small(body, [total, rest, got], (state, lanes), [], "join", after, carry)


def on_device(
    inputs,
    input_norm_scale,
    w_z,
    w_x,
    w_bc,
    w_dt,
    conv_x_w,
    conv_x_b,
    conv_bc_w,
    conv_bc_b,
    dt_bias,
    a_log,
    d_skip,
    norm_inner,
    w_out,
    cotangent,
    lengths,
    order,
):
    tokens, part = inputs.shape
    shards = lax.axis_size("head")
    seq_size = lax.axis_size("seq")
    me = lax.axis_index("head")
    seq = lax.axis_index("seq")
    width = part * shards
    share = width // seq_size
    inner = w_z.shape[1]
    heads = dt_bias.shape[0]
    size = inner // heads
    state = w_bc.shape[1] // 2
    channels = inner + 2 * state
    taps_count = conv_x_w.shape[0]
    rows = 2 * SPAN
    spans = rows // SPAN
    count = tokens // rows
    half = tokens // 2
    half_count = count // 2
    first = seq * tokens

    number = lengths.shape[0]
    picker = (order[:, None] == jnp.arange(number, dtype=jnp.int32)[None, :]).astype(jnp.int32)
    placed = jnp.sum(picker * lengths[None, :], axis=1)
    starts = jnp.cumsum(placed) - placed
    spots = first + jnp.arange(tokens, dtype=jnp.int32)
    begin = jnp.max(jnp.where(starts[None, :] <= spots[:, None], starts[None, :], 0), axis=1)
    begin = begin.astype(jnp.int32)
    begin_col = jnp.broadcast_to(begin[:, None], (tokens, 128))
    begin_row = jnp.broadcast_to(begin[None, :], (8, tokens))
    ends = begin.reshape(tokens // SPAN, SPAN)[:, -1]
    meta = jnp.concatenate([jnp.stack([first, me, seq]).astype(jnp.int32), ends])

    edge = lax.ppermute(
        inputs[tokens - EDGE :], "seq", [(i, i + 1) for i in range(seq_size - 1)]
    )
    edges = gather_near(edge, gather_far(edge))
    own_halves = [inputs[:half], inputs[half:]]
    xs = [gather_near(own_halves[0], gather_far(own_halves[0]))]
    late_half = handed(meta, own_halves[1], [xs[0][2], edges[2]])
    late_far = gather_far(late_half)
    cots = []

    scale = input_norm_scale.reshape(shards, 1, part)
    taps = jnp.concatenate([conv_x_w, conv_bc_w], axis=1)
    bias = jnp.concatenate([conv_x_b, conv_bc_b])[None, :]
    rate = -jnp.exp(a_log)[None, :]
    w_maps = jnp.concatenate([w_bc, w_dt, jnp.zeros((width, 128 - heads), BF16)], axis=1)
    skip = jnp.repeat(d_skip, size)[None, :]
    inner_gain = norm_inner[None, :]
    scale_row = input_norm_scale[None, :]
    prepared = [begin_row, skip, inner_gain, scale_row, rate]

    def fore(i):
        return i

    def back(i):
        return count - 1 - i

    big = [
        ((tokens, width), BF16, "rows", FAR),
        ((tokens, inner), BF16, "rows", FAR),
        ((tokens, 2 * state), BF16, "rows", FAR),
        ((tokens, inner), BF16, "rows", NEAR),
        ((tokens, inner), BF16, "rows", NEAR),
        ((tokens, 2 * state), BF16, "rows", NEAR),
        ((tokens, inner), BF16, "rows", FAR),
        ((tokens, 2 * state), BF16, "rows", FAR),
        ((tokens, 128), F32, "rows", NEAR),
        ((heads, tokens), F32, "lanes", NEAR),
        ((tokens // SPAN, state, inner), F32, "stack", NEAR),
        ((tokens // SPAN, 8, inner), F32, "stack", NEAR),
        ((tokens // SPAN, 8, inner), F32, "stack", NEAR),
    ]

    def spec_of(shape, kind, step):
        if kind == "rows":
            return rows_at(rows, shape[1], step)
        if kind == "lanes":
            return lanes_at(shape[0], rows, step)
        return stack_at((spans,) + shape[1:], step)

    carried = None
    for chunk in range(2):
        opens, closes = chunk == 0, chunk == 1
        start = chunk * half_count

        def here(i, start=start):
            return start + i

        ins = [meta] + [(one, rows_at(rows, part, fore)) for one in xs[chunk]]
        if opens:
            ins += [whole_of(one) for one in edges]
        else:
            ins += [whole_of(one) for one in carried]
        ins += [(begin_col, rows_at(rows, 128, here))]
        ins += [
            whole_of(one)
            for one in (scale, w_x, w_maps, taps, bias, dt_bias[None, :], rate)
        ]
        outs = [
            (shape, dtype, spec_of(shape, kind, here), space) for shape, dtype, kind, space in big
        ]
        if opens:
            extra = [((EDGE, channels), BF16), ((EDGE, width), BF16)]
        else:
            extra = []
        if closes:
            extra += [((state + 8, inner), F32)]
        else:
            extra += [((EDGE, channels), BF16), ((state, inner), F32), ((8, inner), F32)]
        outs += [(shape, dtype, whole(shape)) for shape, dtype in extra]
        found = call(
            functools.partial(
                project_body, shards, inner, state, heads, start, half_count, opens, closes
            ),
            (half_count,),
            ins,
            outs,
            [
                pltpu.VMEM((rows + 8, channels), F32),
                pltpu.VMEM((state, inner), F32),
                pltpu.VMEM((8, inner), F32),
            ],
            (12, 1000000),
            "project",
            room=ROOM_PROJECT,
            after=prepared if opens else [],
            carry=[cotangent[chunk * half : (chunk + 1) * half]],
            kept=None if opens else dict(enumerate(held)),
        )
        held = found[: len(big)]
        if opens:
            late_far = {k: handed(meta, one, [found[-2]]) for k, one in late_far.items()}
            xs.append(gather_near(late_half, late_far))
            early_cot, early_cot_far = found[-1], gather_far(found[-1])
        else:
            late_cot, late_cot_far = found[-1], gather_far(found[-1])
            early_cot_far = {k: handed(meta, one, [found[-2]]) for k, one in early_cot_far.items()}
            cots.append(gather_near(early_cot, early_cot_far))
        if opens:
            pre_edge, edge_normed = found[len(big) : len(big) + 2]
            carried = found[len(big) + 2 : -2]
        else:
            message = found[len(big)]
    (
        normed,
        pre_x,
        pre_bc,
        x,
        xdt,
        bc,
        slope_x,
        slope_bc,
        cols,
        runt,
        states,
        upto,
        own,
    ) = held

    links = chain(meta, message, True)
    next(links)
    found = None
    for chunk in range(2):
        start = chunk * half_count
        if chunk == 1:
            sent = links.send([found[-1]])
            late_cot_far = {k: handed(meta, one, [sent]) for k, one in late_cot_far.items()}
            cots.append(gather_near(late_cot, late_cot_far))

        def here(i, start=start):
            return start + i

        found = call(
            functools.partial(inside_body, shards, state, heads, start),
            (half_count,),
            [meta]
            + [(one, rows_at(rows, part, fore)) for one in cots[chunk]]
            + [
                (begin_col, rows_at(rows, 128, here)),
                (bc, rows_at(rows, 2 * state, here)),
                (xdt, rows_at(rows, inner, here)),
                (cols, rows_at(rows, 128, here)),
                (runt, lanes_at(heads, rows, here)),
                (normed, rows_at(rows, width, here)),
                whole_of(w_z),
                whole_of(w_out),
            ],
            [((tokens, inner), F32, rows_at(rows, inner, here), NEAR)] * 3,
            [pltpu.VMEM((rows, width), BF16)],
            (8, 1000000),
            "inside",
            room=ROOM_INSIDE,
            kept=None if found is None else dict(enumerate(found[:3])),
            after=() if found is None else [sent],
        )
    inside, z, grad_y, done = found
    links.send([done])
    incoming, _ = links.send(((), ()))

    y, sums, done = call(
        functools.partial(gate_body, state, heads),
        (count,),
        [meta]
        + [
            (bc, rows_at(rows, 2 * state, fore)),
            (x, rows_at(rows, inner, fore)),
            (cols, rows_at(rows, 128, fore)),
            (z, rows_at(rows, inner, fore)),
            (grad_y, rows_at(rows, inner, fore)),
            (inside, rows_at(rows, inner, fore)),
            (states, stack_at((spans, state, inner), fore)),
            (upto, stack_at((spans, 8, inner), fore)),
            whole_of(incoming),
            whole_of(skip),
            whole_of(inner_gain),
        ],
        [
            ((tokens, inner), F32, rows_at(rows, inner, fore), NEAR),
            ((8, tokens), F32, lanes_at(8, rows, fore)),
        ],
        [],
        (9, 1000000),
        "gate",
        room=ROOM_GATE,
    )

    all_sums = [sums] + [swap(sums, "head", k) for k in range(1, shards)]

    y_norm, dz, dy, dstates, after, message, g_norm_inner, g_skip, done = call(
        functools.partial(norm_body, shards, state, heads, count),
        (count,),
        [meta]
        + [(one, lanes_at(8, rows, back)) for one in all_sums]
        + [
            (bc, rows_at(rows, 2 * state, back)),
            (x, rows_at(rows, inner, back)),
            (cols, rows_at(rows, 128, back)),
            (z, rows_at(rows, inner, back)),
            (y, rows_at(rows, inner, back)),
            (grad_y, rows_at(rows, inner, back)),
            (own, stack_at((spans, 8, inner), back)),
            whole_of(skip),
            whole_of(inner_gain),
        ],
        [
            ((tokens, inner), BF16, rows_at(rows, inner, back), NEAR),
            ((tokens, inner), BF16, rows_at(rows, inner, back), NEAR),
            ((tokens, inner), F32, rows_at(rows, inner, back), NEAR),
            ((tokens // SPAN, state, inner), F32, stack_at((spans, state, inner), back), NEAR),
            ((tokens // SPAN, 8, inner), F32, stack_at((spans, 8, inner), back), NEAR),
            ((state + 8, inner), F32, whole((state + 8, inner))),
            ((8, inner), F32, whole((8, inner))),
            ((8, inner), F32, whole((8, inner))),
        ],
        [pltpu.VMEM((state, inner), F32), pltpu.VMEM((8, inner), F32)],
        (12, 1000000),
        "norm",
        room=ROOM_NORM,
    )


    def inside_back(chunk, kept, after):
        def here(i):
            return chunk * half_count + i

        return call(
            functools.partial(inside_back_body, state, heads, chunk * half_count),
            (half_count,),
            [
                meta,
                (begin_row, lanes_at(8, rows, here)),
                (bc, rows_at(rows, 2 * state, here)),
                (xdt, rows_at(rows, inner, here)),
                (dy, rows_at(rows, inner, here)),
                (cols, rows_at(rows, 128, here)),
                (runt, lanes_at(heads, rows, here)),
            ],
            [
                ((tokens, inner), F32, rows_at(rows, inner, here), NEAR),
                ((tokens, 2 * state), F32, rows_at(rows, 2 * state, here), NEAR),
            ],
            [],
            (7, 1000000),
            "inside_back",
            room=ROOM_INSIDE,
            kept=None if kept is None else dict(enumerate(kept[:2])),
            after=after,
        )

    links = chain(meta, message, False)
    next(links)
    held = inside_back(0, None, [])
    sent = links.send([held[-1]])

    pair_shape = (seq_size // 2, share, 2 * inner)
    found = call(
        functools.partial(early_body, shards, count),
        (count,),
        [meta]
        + [
            (one, rows_at(rows, part, lambda i: jnp.minimum(i, half_count - 1)))
            for one in cots[0]
        ]
        + [
            (one, rows_at(rows, part, lambda i: jnp.maximum(i - half_count, 0)))
            for one in cots[1]
        ]
        + [
            (normed, rows_at(rows, width, fore)),
            (y_norm, rows_at(rows, inner, fore)),
            (dz, rows_at(rows, inner, fore)),
            whole_of(w_out),
            whole_of(w_z),
        ],
        [((tokens, part), BF16, rows_at(rows, part, fore), FAR)] * shards
        + [
            (pair_shape, BF16, whole(pair_shape), FAR),
            (pair_shape, BF16, whole(pair_shape), FAR),
            ((8, width), F32, whole((8, width))),
        ],
        [
            pltpu.VMEM((rows, width), BF16),
            pltpu.VMEM((width, inner), F32),
            pltpu.VMEM((width, inner), F32),
        ],
        (12, 1000000),
        "early",
        after=[held[-1], sent],
        room=ROOM_EARLY,
    )
    out_parts, (early_keep, early_send, gain_z, done) = found[:shards], found[shards:]
    out_parts = [bare(one) for one in out_parts]
    total = links.send(())
    dxdt, dbc, done = inside_back(1, held, [total])
    sent_late = [bare(early_send)] + out_parts[1::2]
    outgoing, token, early_send, *odd_parts = links.send(([done], sent_late))
    out_parts[1::2] = odd_parts
    out_near = scatter_near(out_parts)
    early = Stages(scatter_seq(bare(early_keep), early_send))


    found = call(
        functools.partial(maps_back_body, state, heads, count),
        (count,),
        [
            meta,
            (begin_col, rows_at(rows, 128, back)),
            (bc, rows_at(rows, 2 * state, back)),
            (xdt, rows_at(rows, inner, back)),
            (dy, rows_at(rows, inner, back)),
            (cols, rows_at(rows, 128, back)),
            (slope_bc, rows_at(rows, 2 * state, back)),
            (pre_bc, rows_at(rows, 2 * state, back)),
            whole_of(pre_edge),
            (normed, rows_at(rows, width, back)),
            whole_of(edge_normed),
            whole_of(w_bc),
            (dbc, rows_at(rows, 2 * state, back)),
            (states, stack_at((spans, state, inner), back)),
            (upto, stack_at((spans, 8, inner), back)),
            (dstates, stack_at((spans, state, inner), back)),
            (after, stack_at((spans, 8, inner), back)),
            (own, stack_at((spans, 8, inner), back)),
            whole_of(incoming),
            whole_of(outgoing),
            whole_of(conv_bc_w),
        ],
        [
            ((tokens, 2 * state), BF16, rows_at(rows, 2 * state, back), NEAR),
            ((tokens // SPAN, 8, heads), F32, stack_at((spans, 8, heads), back), NEAR),
            ((tokens // SPAN, state, inner), F32, stack_at((spans, state, inner), back), NEAR),
            ((EDGE, 2 * state), F32, whole((EDGE, 2 * state))),
            ((EDGE, 2 * state), F32, whole((EDGE, 2 * state))),
            ((taps_count, 8, 2 * state), F32, whole((taps_count, 8, 2 * state))),
            ((8, 2 * state), F32, whole((8, 2 * state))),
            ((width // 2, 2 * state), F32, whole((width // 2, 2 * state))),
            ((width // 2, 2 * state), F32, whole((width // 2, 2 * state))),
            ((8, width), F32, whole((8, width))),
        ],
        [
            pltpu.VMEM((rows + 8, 2 * state), F32),
            pltpu.VMEM((rows + 8, 128), jnp.int32),
            pltpu.VMEM((width, 2 * state), F32),
        ],
        (12, 1000000),
        "maps_back",
        room=ROOM_MAPS,
    )
    dpre_bc, through, ds_all, tail_bc, left_bc, taps_bc, bias_bc = found[:7]
    bc_keep, bc_send, gain_bc, done = found[7:]
    left_pairs = [(i + 1, i) for i in range(seq_size - 1)]
    right_bc = lax.ppermute(left_bc, "seq", left_pairs)
    bc_sums = Stages(sum_rows_everywhere(bc_keep, bc_send))
    out_sums = Stages(scatter_far(out_parts, out_near))
    sent = run_stages(meta, [bc_sums, out_sums], [done])

    late_width = inner + 128
    late_shape = (seq_size // 2, share, late_width)

    def inner_back(opens, start, fresh_steps, extra, after):
        steps = fresh_steps if opens else fresh_steps + 1

        def now(i):
            return start + jnp.minimum(i, fresh_steps - 1)

        def late(i):
            return jnp.maximum(i - 1, 0) if opens else start - 1 + i

        def written(i):
            return jnp.maximum(i - 1, 0) if opens else i

        outs = [
            ((half, inner), BF16, rows_at(rows, inner, written), NEAR),
            ((half, heads), BF16, rows_at(rows, heads, written)),
        ]
        sums = [
            ((taps_count, 8, inner), F32, whole((taps_count, 8, inner))),
            ((8, inner), F32, whole((8, inner))),
            ((16, heads), F32, whole((16, heads))),
        ]
        sums_scratch = []
        if opens:
            outs += sums + [
                ((rows, inner), F32, whole((rows, inner)), NEAR),
                ((rows, heads), BF16, whole((rows, heads))),
                ((EDGE, inner), F32, whole((EDGE, inner))),
                ((width, late_width), F32, whole((width, late_width)), NEAR),
            ]
        else:
            outs += [
                (late_shape, BF16, whole(late_shape), FAR),
                (late_shape, BF16, whole(late_shape), FAR),
                ((8, inner), F32, whole((8, inner))),
                ((8, 2 * state + width), F32, whole((8, 2 * state + width))),
            ]
            sums_scratch = [pltpu.VMEM(shape, F32) for shape, _, _ in sums]
            sums_scratch += [pltpu.VMEM((width, late_width), F32)]
        return call(
            functools.partial(inner_back_body, state, heads, start, fresh_steps, opens),
            (steps,),
            [
                meta,
                (begin_col, rows_at(rows, 128, now)),
                (begin_col, rows_at(rows, 128, late)),
                (bc, rows_at(rows, 2 * state, now)),
                (Held(bare(x), FAR), rows_at(rows, inner, now)),
                (xdt, rows_at(rows, inner, now)),
                (dy, rows_at(rows, inner, now)),
                (Held(bare(y), FAR), rows_at(rows, inner, now)),
                (cols, rows_at(rows, 128, now)),
                (slope_x, rows_at(rows, inner, now)),
                (pre_x, rows_at(rows, inner, late)),
                (normed, rows_at(rows, width, late)),
                (dxdt, rows_at(rows, inner, now)),
                (through, stack_at((spans, 8, heads), now)),
                (ds_all, stack_at((spans, state, inner), now)),
                whole_of(skip),
                whole_of(rate),
                whole_of(conv_x_w),
            ]
            + [whole_of(one) for one in extra],
            outs,
            sums_scratch
            + [
                pltpu.VMEM((rows + 8, inner), F32),
                pltpu.VMEM((rows + 8, 128), jnp.int32),
                pltpu.VMEM((rows, inner), F32),
                pltpu.VMEM((rows, heads), BF16),
                pltpu.VMEM((rows, heads), BF16),
            ],
            (6 * fresh_steps, 1000000),
            "inner_back",
            after=after,
            room=ROOM_INNER,
        )

    found = inner_back(True, 0, count - 1, [pre_edge], sent + [right_bc])
    sent = run_stages(meta, [early, bc_sums, out_sums], [found[-1]])
    dpre_low, ddt_low, taps_x, bias_x, scalars, held_du, held_ddt, left_x, weight_x, done = found
    right_x = lax.ppermute(left_x, "seq", left_pairs)

    def input_grad(chunk, dpre, ddt, extra, after, carry=()):
        start = chunk * half_count

        def here(i):
            return start + i

        whole_rows = half + EDGE
        return call(
            functools.partial(input_body, shards, half_count, chunk == 1),
            (half_count,),
            [meta]
            + [(Held(one, FAR), rows_at(rows, part, fore)) for one in xs[chunk]]
            + [
                (Held(bare(dz), FAR), rows_at(rows, inner, here)),
                (dpre, rows_at(rows, inner, fore)),
                (Held(bare(dpre_bc), FAR), rows_at(rows, 2 * state, here)),
                (ddt, rows_at(rows, heads, fore)),
            ]
            + [whole_of(one) for one in [w_z, w_x, w_bc, w_dt, scale] + extra],
            [((whole_rows, part), BF16, whole((whole_rows, part)))] * shards,
            [pltpu.VMEM((rows, 2 * state), BF16), pltpu.VMEM((EDGE, part), F32)],
            (8, 1000000),
            "input_grad",
            room=ROOM_INPUT,
            after=after,
            carry=carry,
        )

    found = inner_back(
        False,
        count - 1,
        1,
        [held_du, held_ddt, right_x, taps_x, bias_x, scalars, weight_x]
        + [w_x, w_dt, scale_row, gain_z, gain_bc]
        + [g_norm_inner, g_skip, taps_bc, bias_bc],
        sent,
    )
    dpre_high, ddt_high, late_keep, late_send, owned, shared, done = found
    late = Stages(scatter_seq(bare(late_keep), bare(late_send)))
    shared_sums = Stages(add_head(shared))
    sent = run_stages(meta, [bc_sums, out_sums], [done])
    sent += out_sums.terms(meta)[2:] + [early.job[1][1]]
    *parts_low, done = input_grad(0, dpre_low, ddt_low, [], sent)
    low_sums = Stages(scatter_far(parts_low, scatter_near(parts_low)))
    sent = run_stages(meta, [bc_sums, shared_sums, low_sums, early], [done])
    early_terms, mixed = early.terms(meta), out_sums.terms(meta)
    results = input_grad(
        1,
        dpre_high,
        ddt_high,
        [tail_bc, right_bc],
        sent,
        [mixed[0], early_terms[0]],
    )
    parts_high, (done, *own_terms) = results[:shards], results[shards:]
    mixed[0], early_keep = own_terms
    high_sums = Stages(scatter_far(parts_high, scatter_near(parts_high)))
    ends = Stages(
        end_sums(
            bc_sums.terms(meta), owned, *shared_sums.terms(meta), heads, taps_count, part
        )
    )
    far_low = low_sums.terms(meta)
    run_stages(meta, [late, ends], [done, far_low[-1], early_terms[1]])
    run_stages(meta, [late, high_sums, ends], ())
    far_high = high_sums.terms(meta)
    run_stages(meta, [late, ends], ())

    def low(i):
        return jnp.minimum(i, half_count - 1)

    def high(i):
        return jnp.maximum(i - half_count, 0)

    ins = []
    for terms, step in ((far_low, low), (far_high, high)):
        ins += [(one, rows_at(rows, part, step)) for one in terms]
        ins += [(one, pl.BlockSpec((EDGE, part), lambda i, meta: (half // EDGE, 0))) for one in terms]
    grad_input, output, done = call(
        functools.partial(final_body, shards, heads, count),
        (count,),
        [meta]
        + ins
        + [(one, rows_at(rows, part, fore)) for one in mixed]
        + [
            (Held(inputs, FAR), rows_at(rows, part, fore)),
            (Held(cotangent, FAR), rows_at(rows, part, fore)),
            (cols, rows_at(rows, 128, fore)),
            whole_of(scale),
        ],
        [
            ((tokens, part), F32, rows_at(rows, part, fore)),
            ((tokens, part), BF16, rows_at(rows, part, fore)),
        ],
        [],
        (5, 1000000),
        "finals",
        room=10,
    )
    grad_w_z, grad_w_out, grad_w_x, grad_w_dt, _ = call(
        functools.partial(weights_body, inner, heads),
        (1,),
        [meta] + [whole_of(one) for one in (early_keep, early_terms[1]) + late.terms(meta)],
        [
            ((share, inner), F32, whole((share, inner))),
            ((inner, share), F32, whole((inner, share))),
            ((share, inner), F32, whole((share, inner))),
            ((share, heads), F32, whole((share, heads))),
        ],
        [],
        (2, 1000000),
        "weights",
        room=10,
    )
    grad_w_bc, small = ends.terms(meta, [done])
    taps_x, bias_x, gain_x, skip_x, bias_dt, rate_x, taps_bc, bias_bc, gain_in = small
    return (
        output,
        grad_input,
        gain_in.reshape(-1),
        grad_w_z,
        grad_w_x,
        grad_w_bc,
        grad_w_dt,
        taps_x,
        bias_x.reshape(-1),
        taps_bc,
        bias_bc.reshape(-1),
        bias_dt.reshape(-1),
        rate_x.reshape(-1),
        skip_x.reshape(-1),
        gain_x.reshape(-1),
        grad_w_out,
    )


def solution(mesh):
    placed = (
        P("seq", "head"),
        P(),
        P(None, "head"),
        P(None, "head"),
        P(),
        P(None, "head"),
        P(None, "head"),
        P("head"),
        P(),
        P(),
        P("head"),
        P("head"),
        P("head"),
        P("head"),
        P("head", None),
        P("seq", "head"),
        P(),
        P(),
    )
    return jax.shard_map(
        on_device,
        mesh=mesh,
        in_specs=placed,
        out_specs=(
            P("seq", "head"),
            P("seq", "head"),
            P("head"),
            P("seq", "head"),
            P("seq", "head"),
            P(),
            P("seq", "head"),
            P(None, "head"),
            P("head"),
            P(),
            P(),
            P("head"),
            P("head"),
            P("head"),
            P("head"),
            P("head", "seq"),
        ),
        check_vma=False,
    )
```

```python
import functools

import jax
import jax.numpy as jnp
from jax import lax
from jax.experimental import pallas as pl
from jax.experimental.pallas import tpu as pltpu
from jax.sharding import PartitionSpec as P

SPAN = 256
EDGE = 16
EPSILON = 1e-05
F32 = jnp.float32
BF16 = jnp.bfloat16
NEAR, FAR = pltpu.VMEM, pltpu.HBM
ROOM_PROJECT, ROOM_INSIDE, ROOM_GATE, ROOM_NORM = 14, 8, 6, 8
ROOM_EARLY, ROOM_MAPS, ROOM_INNER, ROOM_INPUT = 20, 12, 22, 12


def mm(left, right):
    return lax.dot_general(left, right, (((1,), (0,)), ((), ())), preferred_element_type=F32)


def mm_nt(left, right):
    return lax.dot_general(left, right, (((1,), (1,)), ((), ())), preferred_element_type=F32)


def mm_tn(left, right):
    return lax.dot_general(left, right, (((0,), (0,)), ((), ())), preferred_element_type=F32)


def pieces(values, count):
    found = []
    for _ in range(count):
        part = values.astype(BF16)
        found.append(part)
        values = values - part.astype(F32)
    return found


def add_all(terms):
    total = terms[0]
    for term in terms[1:]:
        total = total + term
    return total


def triangle(size, keep):
    rows = lax.broadcasted_iota(jnp.int32, (size, size), 0)
    cols = lax.broadcasted_iota(jnp.int32, (size, size), 1)
    return keep(rows, cols).astype(F32).astype(BF16)


def expander(heads, width, copies=1):
    rows = lax.broadcasted_iota(jnp.int32, (copies * heads, width), 0) & (heads - 1)
    cols = lax.broadcasted_iota(jnp.int32, (copies * heads, width), 1)
    size = width // heads
    return ((cols >= rows * size) & (cols < (rows + 1) * size)).astype(F32).astype(BF16)


def expand(values, spread):
    count = spread.shape[0] // values.shape[1]
    parts = [part.astype(F32) for part in pieces(values, count)]
    return mm(jnp.concatenate(parts, axis=1).astype(BF16), spread)


def per_head(values, spread, count=2):
    return add_all([mm_nt(part, spread) for part in pieces(values, count)])


def widen(column, width):
    lanes = column.shape[1]
    if width <= lanes:
        return column[:, :width]
    return jnp.concatenate([column] * (width // lanes), axis=1)


def row_ids(rows, lanes=128):
    return lax.broadcasted_iota(jnp.int32, (rows, lanes), 0)


def sigmoid(values):
    return 0.5 * jnp.tanh(0.5 * values) + 0.5


def softplus(values):
    return jnp.maximum(values, 0.0) + jnp.log1p(jnp.exp(-jnp.abs(values)))


def rows_of_sums(first, second):
    lane = lax.broadcasted_iota(jnp.int32, (first.shape[0], 128), 1)
    one = jnp.sum(first, axis=1, keepdims=True)
    two = jnp.sum(second, axis=1, keepdims=True)
    return jnp.where(lane == 0, one, jnp.where(lane == 1, two, 0.0)).T[:8]


def row_of_sums(values):
    lane = lax.broadcasted_iota(jnp.int32, (values.shape[0], 128), 1)
    return jnp.where(lane == 0, jnp.sum(values, axis=1, keepdims=True), 0.0).T[:8]


def column_of(rows, at):
    picks = (lax.broadcasted_iota(jnp.int32, (8, 128), 0) == at).astype(F32).astype(BF16)
    return add_all([mm_tn(part, picks) for part in pieces(rows, 3)])


def fold_rows(values):
    rows, lanes = values.shape
    return jnp.sum(values.reshape(rows // 8, 8, lanes), axis=0)


def halves_of(values):
    high = values.astype(BF16)
    return high, (values - high.astype(F32)).astype(BF16)


class Held:
    def __init__(self, array, space):
        self.array, self.space, self.shape = array, space, array.shape


def bare(one):
    return one.array if isinstance(one, Held) else one


def stays(one):
    return pltpu.with_memory_space_constraint(one.array, one.space) if isinstance(one, Held) else one


class Place:
    def __init__(self, tokens, ends):
        self.tokens, self.ends = tokens, ends

    def __getitem__(self, which):
        index = lax.axis_index("head" if which == 1 else "seq")
        return index * self.tokens if which == 0 else index


def call(body, grid, ins, outs, scratch, work, name, kept=None, after=(), carry=(), room=24):
    place = ins[0]
    prefetched = [] if isinstance(place, Place) else [place]
    arrays = prefetched + [stays(one[0]) for one in ins[1:]]
    specs = [one[1] for one in ins[1:]]
    aliases = {}
    own = len(arrays)
    for at, array in (kept or {}).items():
        aliases[len(arrays)] = at
        arrays.append(stays(array))
        specs.append(pl.BlockSpec(memory_space=pl.ANY))
    for array in after:
        arrays.append(stays(array))
        specs.append(pl.BlockSpec(memory_space=pl.ANY))
    for at, array in enumerate(carry):
        aliases[len(arrays)] = len(outs) + 1 + at
        arrays.append(array)
        specs.append(pl.BlockSpec(memory_space=pl.ANY))
    total = len(arrays)
    spaces = [one[3] if len(one) > 3 else None for one in outs]

    def only_own(*refs):
        token = refs[total + len(outs)]
        token[...] = jnp.zeros_like(token)
        where = [] if prefetched else [place]
        body(*where, *refs[:own], *refs[total : total + len(outs)], *refs[total + len(outs) + 1 + len(carry) :])

    found = pl.pallas_call(
        only_own,
        out_shape=[
            space(one[0], one[1]) if space else jax.ShapeDtypeStruct(one[0], one[1])
            for one, space in zip(outs, spaces)
        ]
        + [NEAR((8, 128), F32)]
        + [jax.ShapeDtypeStruct(one.shape, one.dtype) for one in carry],
        grid_spec=pltpu.PrefetchScalarGridSpec(
            num_scalar_prefetch=len(prefetched),
            grid=grid,
            in_specs=specs,
            out_specs=[one[2] for one in outs]
            + [whole((8, 128))]
            + [pl.BlockSpec(memory_space=pl.ANY)] * len(carry),
            scratch_shapes=scratch,
        ),
        input_output_aliases=aliases,
        compiler_params=pltpu.CompilerParams(
            dimension_semantics=("arbitrary",) * len(grid), vmem_limit_bytes=room * 1024 * 1024
        ),
        cost_estimate=pl.CostEstimate(
            flops=int(work[0] * 1e9), bytes_accessed=int(work[1]), transcendentals=0
        ),
        name=name,
    )(*arrays)
    made = [Held(one, space) if space else one for one, space in zip(found, spaces)]
    return made + [Held(found[len(outs)], NEAR)] + list(found[len(outs) + 1 :])


def rows_at(rows, lanes, step):
    return pl.BlockSpec((rows, lanes), lambda i, *meta: (step(i), 0))


def lanes_at(rows, lanes, step):
    return pl.BlockSpec((rows, lanes), lambda i, *meta: (0, step(i)))


def stack_at(shape, step):
    return pl.BlockSpec(shape, lambda i, *meta: (step(i),) + (0,) * (len(shape) - 1))


def whole(shape):
    return pl.BlockSpec(shape, lambda i, *meta: (0,) * len(shape))


def whole_of(array):
    return (array, whole(array.shape))


def block_at(me, k, size):
    return pl.ds(pl.multiple_of((me ^ k) * size, size), size)


LAST = 3
DT, RAW, RUN, REACH, KEEP, INV = range(6)


def column(ref, which, heads):
    return ref[:, which * heads : (which + 1) * heads]


def project_body(shards, inner, state, heads, start, steps, opens, closes, meta, *refs):
    refs = list(refs)

    def take(amount):
        found = refs[:amount]
        del refs[:amount]
        return found

    xs = take(shards)
    if opens:
        edges = take(shards)
    else:
        tail_in, carry_in, decay_in = take(3)
    begin_ref, scale, w_x, w_maps, taps, bias, dt_bias, rate = take(8)
    (
        normed_ref,
        pre_x_ref,
        pre_bc_ref,
        x_ref,
        xdt_ref,
        bc_ref,
        slope_x_ref,
        slope_bc_ref,
        cols_ref,
        runt_ref,
        state_ref,
        upto_ref,
        own_ref,
    ) = take(13)
    if opens:
        edge_ref, edge_normed = take(2)
    if closes:
        (message_ref,) = take(1)
    else:
        tail_ref, carry_out, decay_out = take(3)
    ext, carry, decay = take(3)
    step = pl.program_id(0)
    me = meta[1]
    rows = x_ref.shape[0]
    part = xs[0].shape[1]
    width = part * shards
    maps = 2 * state
    at_block = (start + step) * (rows // SPAN)
    first = meta[0] + at_block * SPAN

    def normalise(sources, target):
        loaded = [source[...].astype(F32) for source in sources]
        total = jnp.sum(add_all([one * one for one in loaded]), axis=1, keepdims=True)
        inverse = lax.rsqrt(total / width + EPSILON)
        for k, one in enumerate(loaded):
            target[:, block_at(me, k, part)] = (one * inverse * scale[me ^ k]).astype(BF16)
        return inverse

    @pl.when(step == 0)
    def _():
        if opens:
            normalise(edges, edge_normed)
            held = edge_normed[...]
            edge_ref[:, :inner] = mm(held, w_x[...]).astype(BF16)
            edge_ref[:, inner:] = mm(held, w_maps[:, :maps]).astype(BF16)
            ext[:8, :] = edge_ref[EDGE - 8 :, :].astype(F32)
            carry[...] = jnp.zeros_like(carry)
            decay[...] = jnp.ones_like(decay)
        else:
            ext[:8, :] = tail_in[EDGE - 8 :, :].astype(F32)
            carry[...] = carry_in[...]
            decay[...] = decay_in[...]

    @pl.when(step > 0)
    def _():
        ext[:8, :] = ext[rows : rows + 8, :]

    inverse = normalise(xs, normed_ref)
    held = normed_ref[...]
    pre_x_ref[...] = mm(held, w_x[...]).astype(BF16)
    both = mm(held, w_maps[...])
    pre_bc_ref[...] = both[:, :maps].astype(BF16)
    ext[8:, :inner] = pre_x_ref[...].astype(F32)
    ext[8:, inner:] = pre_bc_ref[...].astype(F32)
    raw = both[:, maps : maps + heads] + dt_bias[...]
    dt = softplus(raw)

    begin = begin_ref[...]
    place = row_ids(rows) + first
    reach = taps.shape[0] - 1
    channels = ext.shape[1]
    total = bias[...] + taps[reach : reach + 1, :] * ext[8:, :]
    for lag in range(1, reach + 1):
        valid = widen((place - lag >= begin).astype(F32), channels)
        lagged = ext[8 - lag : 8 - lag + rows, :] * valid
        total = total + taps[reach - lag : reach - lag + 1, :] * lagged
    sig = sigmoid(total)
    conv = total * sig
    slope = (sig * (1.0 + total * (1.0 - sig))).astype(BF16)
    slope_x_ref[...] = slope[:, :inner]
    slope_bc_ref[...] = slope[:, inner:]
    x = conv[:, :inner]
    x_ref[...] = x.astype(BF16)
    bc = conv[:, inner:].astype(BF16)
    bc_ref[...] = bc

    spread = expander(heads, inner, 2)
    xdt_ref[...] = (x * expand(dt, spread)).astype(BF16)
    log_decay = dt * rate[...]
    lower = triangle(SPAN, lambda r, c: r >= c)
    upper = triangle(SPAN, lambda r, c: r <= c)
    spans = [slice(s * SPAN, (s + 1) * SPAN) for s in range(rows // SPAN)]
    runs, tails, reaches, keeps, owns = [], [], [], [], []
    for s, at in enumerate(spans):
        parts = [part.astype(F32) for part in pieces(log_decay[at], 3)]
        parts = jnp.concatenate(parts, axis=1).astype(BF16)
        sums = mm(lower, parts)
        runs.append(sums[:, :heads] + sums[:, heads : 2 * heads] + sums[:, 2 * heads :])
        sums = mm_tn(parts, upper)
        runt_ref[:, at] = sums[:heads] + sums[heads : 2 * heads] + sums[2 * heads :]
    for s, at in enumerate(spans):
        run = runs[s]
        tail = run[SPAN - 1 : SPAN, :]
        last = meta[LAST + at_block + s]
        keeps.append(jnp.exp(tail - run) * (place[at] >= last).astype(F32)[:, :heads])
        reaches.append(jnp.exp(run) * (begin[at] < first + s * SPAN).astype(F32)[:, :heads])
        alive = (last < first + s * SPAN).astype(F32)
        owns.append(jnp.broadcast_to(jnp.exp(tail) * alive, (8, heads)))
    keep = jnp.concatenate(keeps, axis=0)
    run, reached = jnp.concatenate(runs, axis=0), jnp.concatenate(reaches, axis=0)
    columns = [dt, raw, run, reached, keep, jnp.broadcast_to(inverse, (rows, heads))]
    rest = cols_ref.shape[1] - len(columns) * heads
    cols_ref[...] = jnp.concatenate(columns + [jnp.zeros((rows, rest), F32)], axis=1)
    high, low = halves_of(x * expand(keep * dt, spread))
    own_all = expand(jnp.concatenate(owns, axis=0), expander(heads, inner, 3))
    for s, at in enumerate(spans):
        own = own_all[8 * s : 8 * s + 8]
        state_ref[s] = carry[...]
        upto_ref[s] = decay[...]
        own_ref[s] = own
        b = bc[at, :state]
        carry[...] = own[:1] * carry[...] + (mm_tn(b, high[at]) + mm_tn(b, low[at]))
        decay[...] = decay[...] * own

    @pl.when(step == steps - 1)
    def _():
        if closes:
            pack_message(message_ref, carry[...], decay[...])
        else:
            tail_ref[:, :inner] = pre_x_ref[rows - EDGE :, :]
            tail_ref[:, inner:] = pre_bc_ref[rows - EDGE :, :]
            carry_out[...] = carry[...]
            decay_out[...] = decay[...]


def pack_message(target, carry, decay):
    state = carry.shape[0]
    target[:state, :] = carry
    target[state:, :] = decay


def assemble(sources, me, target):
    part = sources[0].shape[1]
    for k, source in enumerate(sources):
        target[:, block_at(me, k, part)] = source[...]


def inside_body(shards, state, heads, start, meta, *refs):
    cots, refs = refs[:shards], refs[shards:]
    begin_ref, bc_ref, xdt_ref, cols_ref, runt_ref, normed_ref, w_z, w_out = refs[:8]
    y_ref, z_ref, grad_ref, cot = refs[8:]
    z_ref[...] = mm(normed_ref[...], w_z[...])
    assemble(cots, meta[1], cot)
    grad_ref[...] = mm_nt(cot[...], w_out[...])
    rows, inner = y_ref.shape
    first = meta[0] + (start + pl.program_id(0)) * rows
    row = lax.broadcasted_iota(jnp.int32, (SPAN, SPAN), 0)
    col = lax.broadcasted_iota(jnp.int32, (SPAN, SPAN), 1)
    size = inner // heads
    lane = lax.broadcasted_iota(jnp.int32, (SPAN, 2 * size), 1)
    for s in range(rows // SPAN):
        at = slice(s * SPAN, (s + 1) * SPAN)
        begin = widen(begin_ref[at, :], SPAN)
        allowed = (col <= row) & (col + (first + s * SPAN) >= begin)
        scores = mm_nt(bc_ref[at, state:], bc_ref[at, :state])
        scores = jnp.where(allowed, scores, 0.0)
        for pair in range(heads // 2):
            lanes = slice(pair * 2 * size, (pair + 1) * 2 * size)
            both = xdt_ref[at, lanes]
            total = None
            for j in range(2):
                h = 2 * pair + j
                lane_at = RUN * heads + h
                spread = cols_ref[at, lane_at : lane_at + 1] - runt_ref[h : h + 1, at]
                mixing = (scores * jnp.exp(jnp.minimum(spread, 0.0))).astype(BF16)
                mine = jnp.where((lane < size) == (j == 0), both, jnp.zeros_like(both))
                product = mm(mixing, mine)
                total = product if total is None else total + product
            y_ref[at, lanes] = total


def gate_body(state, heads, meta, *refs):
    (
        bc_ref,
        x_ref,
        cols_ref,
        z_ref,
        grad_ref,
        inside_ref,
        state_ref,
        upto_ref,
        incoming,
        skip,
        norm_inner,
        y_ref,
        sums_ref,
    ) = refs
    rows, inner = y_ref.shape
    reach = expand(column(cols_ref, REACH, heads), expander(heads, inner, 2))
    for s in range(rows // SPAN):
        at = slice(s * SPAN, (s + 1) * SPAN)
        high, low = halves_of(state_ref[s] + upto_ref[s, :1] * incoming[...])
        c = bc_ref[at, state:]
        y_ref[at, :] = inside_ref[at, :] + (mm(c, high) + mm(c, low)) * reach[at]
    y = y_ref[...] + skip[...] * x_ref[...].astype(F32)
    z = z_ref[...]
    gated = y * (z * sigmoid(z))
    sums_ref[...] = rows_of_sums(gated * gated, grad_ref[...] * norm_inner[...] * gated)


def norm_body(shards, state, heads, count, meta, *refs):
    sums, refs = refs[:shards], refs[shards:]
    (
        bc_ref,
        x_ref,
        cols_ref,
        z_ref,
        y_ref,
        grad_ref,
        own_ref,
        skip,
        norm_inner,
        y_norm_ref,
        dz_ref,
        dy_ref,
        state_ref,
        after_ref,
        message_ref,
        gain_ref,
        skip_ref,
        carry,
        decay,
    ) = refs
    step = pl.program_id(0)
    rows, inner = dy_ref.shape

    @pl.when(step == 0)
    def _():
        carry[...] = jnp.zeros_like(carry)
        decay[...] = jnp.ones_like(decay)
        gain_ref[...] = jnp.zeros_like(gain_ref)
        skip_ref[...] = jnp.zeros_like(skip_ref)

    full = inner * shards
    all_rows = add_all([one[...] for one in sums])
    inverse = widen(lax.rsqrt(column_of(all_rows, 0) / full + EPSILON), inner)
    share = widen(column_of(all_rows, 1) / full, inner) * inverse * inverse * inverse
    x = x_ref[...].astype(F32)
    y = y_ref[...] + skip[...] * x
    z = z_ref[...]
    sig = sigmoid(z)
    gate = z * sig
    gated = y * gate
    hat = gated * inverse
    grad = grad_ref[...]
    gain_ref[...] += fold_rows(grad * hat)
    y_norm_ref[...] = (hat * norm_inner[...]).astype(BF16)
    d_gated = inverse * (grad * norm_inner[...]) - gated * share
    dz_ref[...] = (d_gated * y * (sig + gate * (1.0 - sig))).astype(BF16)
    dy = d_gated * gate
    skip_ref[...] += fold_rows(dy * x)
    dy_ref[...] = dy

    reach = expand(column(cols_ref, REACH, heads), expander(heads, inner, 2))
    high, low = halves_of(dy * reach)
    for s in reversed(range(rows // SPAN)):
        at = slice(s * SPAN, (s + 1) * SPAN)
        c = bc_ref[at, state:]
        state_ref[s] = carry[...]
        after_ref[s] = decay[...]
        carry[...] = own_ref[s, :1] * carry[...] + (mm_tn(c, high[at]) + mm_tn(c, low[at]))
        decay[...] = decay[...] * own_ref[s]

    @pl.when(step == count - 1)
    def _():
        pack_message(message_ref, carry[...], decay[...])


def write_halves(total, mine, keep_ref, send_ref, columns):
    count, share = keep_ref.shape[:2]
    for j in range(count):
        here = pl.ds(pl.multiple_of((2 * j + mine) * share, share), share)
        there = pl.ds(pl.multiple_of((2 * j + 1 - mine) * share, share), share)
        keep_ref[j, :, columns] = total[here, :].astype(keep_ref.dtype)
        send_ref[j, :, columns] = total[there, :].astype(send_ref.dtype)


def early_body(shards, count, meta, *refs):
    cots, late_cots, refs = refs[:shards], refs[shards : 2 * shards], refs[2 * shards :]
    (normed_ref, y_norm_ref, dz_ref, w_out, w_z), refs = refs[:5], refs[5:]
    outs, refs = refs[:shards], refs[shards:]
    keep_ref, send_ref, gain_ref, cot, total_z, total_out = refs
    step = pl.program_id(0)
    me = meta[1]
    part = cots[0].shape[1]
    inner = dz_ref.shape[1]

    @pl.when(step == 0)
    def _():
        total_z[...] = jnp.zeros_like(total_z)
        total_out[...] = jnp.zeros_like(total_out)

    y_norm = y_norm_ref[...]
    for k in range(shards):
        outs[k][...] = mm(y_norm, w_out[:, block_at(me, k, part)]).astype(BF16)

    @pl.when(step < count // 2)
    def _():
        assemble(cots, me, cot)

    @pl.when(step >= count // 2)
    def _():
        assemble(late_cots, me, cot)

    total_z[...] += mm_tn(normed_ref[...], dz_ref[...])
    total_out[...] += mm_tn(cot[...], y_norm)

    @pl.when(step == count - 1)
    def _():
        mine = meta[2] & 1
        write_halves(total_z, mine, keep_ref, send_ref, slice(0, inner))
        write_halves(total_out, mine, keep_ref, send_ref, slice(inner, 2 * inner))
        gain_ref[...] = row_of_sums(total_z[...] * w_z[...].astype(F32))


def inside_back_body(state, heads, start, meta, begin_row, bc_ref, xdt_ref, dy_ref, cols_ref, runt_ref, dxdt_ref, dbc_ref):
    rows, inner = dxdt_ref.shape
    first = meta[0] + (start + pl.program_id(0)) * rows
    row = lax.broadcasted_iota(jnp.int32, (SPAN, SPAN), 0)
    col = lax.broadcasted_iota(jnp.int32, (SPAN, SPAN), 1)
    size = inner // heads
    lane = lax.broadcasted_iota(jnp.int32, (SPAN, 2 * size), 1)
    for s in range(rows // SPAN):
        at = slice(s * SPAN, (s + 1) * SPAN)
        allowed = (row <= col) & (row + (first + s * SPAN) >= begin_row[:1, at])
        b = bc_ref[at, :state]
        c = bc_ref[at, state:]
        scores = jnp.where(allowed, mm_nt(b, c), 0.0)
        d_scores = None
        for pair in range(heads // 2):
            lanes = slice(pair * 2 * size, (pair + 1) * 2 * size)
            x_both = xdt_ref[at, lanes]
            high, low = halves_of(dy_ref[at, lanes])
            total = None
            for j in range(2):
                h = 2 * pair + j
                lane_at = RUN * heads + h
                spread = runt_ref[h : h + 1, at] - cols_ref[at, lane_at : lane_at + 1]
                fade = jnp.exp(jnp.minimum(spread, 0.0))
                mixing = (scores * fade).astype(BF16)
                mine = (lane < size) == (j == 0)
                high_mine = jnp.where(mine, high, jnp.zeros_like(high))
                low_mine = jnp.where(mine, low, jnp.zeros_like(low))
                product = mm(mixing, high_mine)
                total = product if total is None else total + product
                faded = (mm_nt(x_both, high_mine) + mm_nt(x_both, low_mine)) * fade
                d_scores = faded if d_scores is None else d_scores + faded
            dxdt_ref[at, lanes] = total
        d_scores = jnp.where(allowed, d_scores, 0.0).astype(BF16)
        dbc_ref[at, :state] = mm(d_scores, c)
        dbc_ref[at, state:] = mm_tn(d_scores, b)


def cross_border(fresh, begins, first, edge, taps, taps_ref, lanes):
    reach = taps.shape[0] - 1
    spot = lax.broadcasted_iota(jnp.int32, (8, lanes), 0)
    place = lax.broadcasted_iota(jnp.int32, (8, 128), 0) + (first - 8)
    sent = jnp.zeros((8, lanes), F32)
    for lag in range(1, reach + 1):
        moved = jnp.concatenate([jnp.zeros((8 - lag, lanes), F32), fresh[:lag, :]], axis=0)
        starts = jnp.concatenate([jnp.zeros((8 - lag, 128), jnp.int32), begins[:lag, :]], axis=0)
        valid = widen((place >= starts).astype(F32), lanes)
        moved = jnp.where(spot >= 8 - lag, moved * valid, 0.0)
        sent = sent + taps[reach - lag : reach - lag + 1, :] * moved
        taps_ref[reach - lag] += moved * edge
    return jnp.concatenate([jnp.zeros((EDGE - 8, lanes), F32), sent], axis=0)


def conv_back(ext, begin_ext, place, pre, taps, taps_ref):
    rows, lanes = pre.shape
    reach = taps.shape[0] - 1
    du = ext[:rows, :]
    taps_ref[reach] += fold_rows(du * pre)
    total = taps[reach : reach + 1, :] * du
    for lag in range(1, reach + 1):
        valid = widen((place >= begin_ext[lag : lag + rows, :]).astype(F32), lanes)
        moved = ext[lag : lag + rows, :] * valid
        total = total + taps[reach - lag : reach - lag + 1, :] * moved
        taps_ref[reach - lag] += fold_rows(moved * pre)
    return total


def maps_back_body(state, heads, count, meta, *refs):
    (
        begin_ref,
        bc_ref,
        xdt_ref,
        dy_ref,
        cols_ref,
        slope_ref,
        pre_ref,
        edge_ref,
        normed_ref,
        edge_normed,
        w_bc,
        dbc_ref,
        state_ref,
        upto_ref,
        dstate_ref,
        after_ref,
        own_ref,
        incoming,
        outgoing,
        taps,
        dpre_ref,
        through_ref,
        ds_ref,
        tail_ref,
        left_ref,
        taps_ref,
        bias_ref,
        own_half_ref,
        send_ref,
        gain_ref,
        ext,
        begin_ext,
        weight,
    ) = refs
    step = pl.program_id(0)
    rows, inner = xdt_ref.shape
    at_step = count - 1 - step
    first = meta[0] + at_step * rows
    spread = expander(heads, inner)
    spread_two = expander(heads, inner, 2)

    @pl.when(step == 0)
    def _():
        weight[...] = jnp.zeros_like(weight)
        ext[rows:, :] = jnp.zeros_like(ext[rows:, :])
        begin_ext[rows:, :] = jnp.zeros_like(begin_ext[rows:, :])
        taps_ref[...] = jnp.zeros_like(taps_ref)
        bias_ref[...] = jnp.zeros_like(bias_ref)

    @pl.when(step > 0)
    def _():
        ext[rows:, :] = ext[:8, :]
        begin_ext[rows:, :] = begin_ext[:8, :]

    begin_ext[:rows, :] = begin_ref[...]
    place = row_ids(rows) + first
    keep = expand(column(cols_ref, KEEP, heads), spread_two)
    reach = expand(column(cols_ref, REACH, heads), spread_two)
    x_high, x_low = halves_of(xdt_ref[...].astype(F32) * keep)
    y_high, y_low = halves_of(dy_ref[...] * reach)
    for s in range(rows // SPAN):
        at = slice(s * SPAN, (s + 1) * SPAN)
        s_in = state_ref[s] + upto_ref[s, :1] * incoming[...]
        ds_out = dstate_ref[s] + after_ref[s, :1] * outgoing[...]
        ds_ref[s] = ds_out
        through = jnp.sum((s_in * ds_out).reshape(state // 8, 8, inner), axis=0) * own_ref[s]
        through_ref[s] = jnp.broadcast_to(
            jnp.sum(per_head(through, spread), axis=0, keepdims=True), (8, heads)
        )
        s_high, s_low = halves_of(s_in)
        ds_high, ds_low = halves_of(ds_out)
        d_b = mm_nt(x_high[at], ds_high) + mm_nt(x_low[at], ds_high) + mm_nt(x_high[at], ds_low)
        d_c = mm_nt(y_high[at], s_high) + mm_nt(y_low[at], s_high) + mm_nt(y_high[at], s_low)
        slope = slope_ref[at, :].astype(F32)
        ext[at, :state] = (dbc_ref[at, :state] + d_b) * slope[:, :state]
        ext[at, state:] = (dbc_ref[at, state:] + d_c) * slope[:, state:]
    bias_ref[...] += fold_rows(ext[:rows, :])
    total = conv_back(ext, begin_ext, place, pre_ref[...].astype(F32), taps, taps_ref)
    high, low = halves_of(total)
    dpre_ref[...] = high
    weight[...] += mm_tn(normed_ref[...], high) + mm_tn(normed_ref[...], low)

    @pl.when(step == 0)
    def _():
        tail_ref[...] = total[rows - EDGE :, :]

    @pl.when(step == count - 1)
    def _():
        edge = edge_ref[EDGE - 8 :, inner:].astype(F32)
        left_ref[...] = cross_border(ext, begin_ext, first, edge, taps, taps_ref, 2 * state)
        left_high, left_low = halves_of(left_ref[...])
        weight[...] += mm_tn(edge_normed[...], left_high) + mm_tn(edge_normed[...], left_low)
        half = send_ref.shape[0]
        mine = meta[1] & 1
        here = pl.ds(pl.multiple_of(mine * half, half), half)
        there = pl.ds(pl.multiple_of((1 - mine) * half, half), half)
        own_half_ref[...] = weight[here, :]
        send_ref[...] = weight[there, :]
        gain_ref[...] = row_of_sums(weight[...] * w_bc[...].astype(F32))


def inner_back_body(state, heads, start, fresh_steps, opens, meta, *refs):
    refs = list(refs)

    def take(amount):
        found = refs[:amount]
        del refs[:amount]
        return found

    (
        begin_ref,
        begin_late,
        bc_ref,
        x_ref,
        xdt_ref,
        dy_ref,
        y_ref,
        cols_ref,
        slope_ref,
        pre_late,
        normed_late,
        dxdt_ref,
        through_ref,
        ds_ref,
        skip,
        rate,
        taps,
    ) = take(17)
    if opens:
        (edge_ref,) = take(1)
    else:
        held_in, held_ddt_in, right, taps_in, bias_in, scalar_in, weight_in = take(7)
        w_x, w_dt, scale, gain_z, gain_bc, norm_gain, skip_gain, taps_bc, bias_bc = take(9)
    dpre_ref, ddt_ref = take(2)
    if opens:
        taps_ref, bias_ref, scalar_ref, held_out, held_ddt_out, left_ref, weight = take(7)
    else:
        keep_half_ref, send_ref, owned_ref, shared_ref, taps_ref, bias_ref, scalar_ref, weight = take(8)
    ext, begin_ext, fresh, ddt = take(4)
    step = pl.program_id(0)
    rows, inner = x_ref.shape
    steps = fresh_steps if opens else fresh_steps + 1
    spread = expander(heads, inner)
    spread_two = expander(heads, inner, 2)

    @pl.when(step == 0)
    def _():
        if opens:
            weight[...] = jnp.zeros_like(weight)
            taps_ref[...] = jnp.zeros_like(taps_ref)
            bias_ref[...] = jnp.zeros_like(bias_ref)
            scalar_ref[...] = jnp.zeros_like(scalar_ref)
        else:
            weight[...] = weight_in[...]
            taps_ref[...] = taps_in[...]
            bias_ref[...] = bias_in[...]
            scalar_ref[...] = scalar_in[...]
            ext[:rows, :] = held_in[...]
            ddt[...] = held_ddt_in[...]

    def renew():
        at_block = (start + step) * (rows // SPAN)
        first = meta[0] + at_block * SPAN
        place = row_ids(rows) + first
        suffix = triangle(SPAN, lambda r, c: r <= c)
        prefix = triangle(SPAN, lambda r, c: r > c)
        rate_now = rate[...]
        spans = [slice(s * SPAN, (s + 1) * SPAN) for s in range(rows // SPAN)]
        kept = []
        for s, at in enumerate(spans):
            b = bc_ref[at, :state]
            ds_high, ds_low = halves_of(ds_ref[s])
            kept.append(mm(b, ds_high) + mm(b, ds_low))
        kept = jnp.concatenate(kept, axis=0) * expand(column(cols_ref, KEEP, heads), spread_two)
        dy = dy_ref[...]
        xdt = xdt_ref[...].astype(F32)
        x = x_ref[...].astype(F32)
        dxdt_in = dxdt_ref[...]
        dxdt = dxdt_in + kept
        dt = column(cols_ref, DT, heads)
        d_x = dxdt * expand(dt, spread_two) + skip[...] * dy
        du = d_x * slope_ref[...].astype(F32)
        fresh[...] = du
        bias_ref[...] += fold_rows(du)
        dy_high = dy.astype(BF16).astype(F32)
        later = per_head(dy_high * y_ref[...] - xdt * dxdt_in, spread, 3)
        earlier = per_head(xdt * kept, spread)
        direct = per_head(x * dxdt, spread)
        q = []
        for s, at in enumerate(spans):
            after = [part.astype(F32) for part in pieces(later[at], 3)]
            after = mm(suffix, jnp.concatenate(after, axis=1).astype(BF16))
            before = [part.astype(F32) for part in pieces(earlier[at], 2)]
            before = mm(prefix, jnp.concatenate(before, axis=1).astype(BF16))
            q.append(
                (after[:, :heads] + after[:, heads : 2 * heads] + after[:, 2 * heads :])
                + (before[:, :heads] + before[:, heads:])
                + through_ref[s, :1, :]
            )
        starts = (place == begin_ref[...]).astype(F32)[:, :heads]
        q = jnp.concatenate(q, axis=0) * (1.0 - starts)
        d_raw = (direct + rate_now * q) / (1.0 + jnp.exp(-column(cols_ref, RAW, heads)))
        fresh_ddt[...] = d_raw.astype(BF16)
        scalar_ref[:8, :] += fold_rows(d_raw)
        scalar_ref[8:, :] += fold_rows(rate_now * dt * q)

    fresh_ddt = refs[0]

    def finish(closing=False):
        begin_ext[:rows, :] = begin_late[...]
        first = meta[0] + (start - (0 if opens else 1) + step - (1 if opens else 0)) * rows
        place = row_ids(rows) + first
        total = conv_back(ext, begin_ext, place, pre_late[...].astype(F32), taps, taps_ref)
        dpre_ref[...] = total.astype(BF16)
        if closing:
            dpre_ref[rows - EDGE :, :] = (total[rows - EDGE :, :] + right[...]).astype(BF16)
        ddt_ref[...] = ddt[...]
        held = normed_late[...]
        weight[:, :inner] += mm_tn(held, dpre_ref[...])
        weight[:, inner : inner + heads] += mm_tn(held, ddt[...])

    if opens:
        renew()

        @pl.when(step == 0)
        def _():
            edge = edge_ref[EDGE - 8 :, :inner].astype(F32)
            left_ref[...] = cross_border(fresh, begin_ref, meta[0], edge, taps, taps_ref, inner)

        @pl.when(step > 0)
        def _():
            ext[rows:, :] = fresh[:8, :]
            begin_ext[rows:, :] = begin_ref[:8, :]
            finish()

        ext[:rows, :] = fresh[...]
        ddt[...] = fresh_ddt[...]

        @pl.when(step == steps - 1)
        def _():
            held_out[...] = fresh[...]
            held_ddt_out[...] = fresh_ddt[...]
    else:

        @pl.when(step < steps - 1)
        def _():
            renew()
            ext[rows:, :] = fresh[:8, :]
            begin_ext[rows:, :] = begin_ref[:8, :]
            finish()
            ext[:rows, :] = fresh[...]
            ddt[...] = fresh_ddt[...]

        @pl.when(step == steps - 1)
        def _():
            ext[rows:, :] = jnp.zeros((8, inner), F32)
            begin_ext[rows:, :] = jnp.zeros((8, 128), jnp.int32)
            finish(True)
            write_halves(weight, meta[2] & 1, keep_half_ref, send_ref, slice(0, weight.shape[1]))
            gain = row_of_sums(weight[:, :inner] * w_x[...].astype(F32))
            gain_dt = row_of_sums(weight[:, inner : inner + heads] * w_dt[...].astype(F32))
            owned_ref[...] = jnp.zeros_like(owned_ref)
            shared_ref[...] = jnp.zeros_like(shared_ref)

            def one_row(values):
                return jnp.sum(values, axis=0, keepdims=True)

            for j in range(taps.shape[0]):
                owned_ref[j : j + 1, :] = one_row(taps_ref[j])
                shared_ref[j : j + 1, : 2 * state] = one_row(taps_bc[j])
            owned_ref[4:5, :] = one_row(bias_ref[...])
            shared_ref[4:5, : 2 * state] = one_row(bias_bc[...])
            owned_ref[5:6, :] = one_row(norm_gain[...])
            owned_ref[6:7, :] = one_row(skip_gain[...])
            owned_ref[7:8, :heads] = one_row(scalar_ref[:8, :])
            owned_ref[7:8, 128 : 128 + heads] = one_row(scalar_ref[8:, :])
            shared_ref[:, 2 * state :] = (gain + gain_dt + gain_z[...] + gain_bc[...]) / scale[...]


def input_body(shards, steps, closes, meta, *refs):
    xs, refs = refs[:shards], refs[shards:]
    dz_ref, dpre_ref, dbc_ref, ddt_ref, w_z, w_x, w_bc, w_dt, scale = refs[:9]
    refs = refs[9:]
    if closes:
        (tail_ref, right_ref), refs = refs[:2], refs[2:]
    outs, refs = refs[:shards], refs[shards:]
    dbc_held, sums = refs
    step = pl.program_id(0)
    me = meta[1]
    rows, part = xs[0].shape
    per_step = rows // part
    total_rows = steps * rows

    dbc_held[...] = dbc_ref[...]
    if closes:

        @pl.when(step == steps - 1)
        def _():
            dbc_held[rows - EDGE :, :] = (tail_ref[...] + right_ref[...]).astype(BF16)

    dz, dx, dbc, ddt = dz_ref[...], dpre_ref[...], dbc_held[...], ddt_ref[...]
    products = None
    here = pl.ds(pl.multiple_of(step * rows, rows), rows)
    for k in range(shards):
        at = block_at(me, k, part)
        grad = (
            mm_nt(dz, w_z[at, :])
            + mm_nt(dx, w_x[at, :])
            + mm_nt(dbc, w_bc[at, :])
            + mm_nt(ddt, w_dt[at, :])
        )
        outs[k][here, :] = grad.astype(BF16)
        product = grad * scale[me ^ k] * xs[k][...].astype(F32)
        products = product if products is None else products + product
    row = row_of_sums(products)

    @pl.when(step == 0)
    def _():
        sums[...] = jnp.zeros_like(sums)

    for s in range(steps):

        @pl.when(step == s)
        def _(s=s):
            for j in range(per_step):
                spot = s * per_step + j
                sums[spot : spot + 1, :] = row[:1, j * part : (j + 1) * part]

    @pl.when(step == steps - 1)
    def _():
        for k in range(shards):
            outs[k][total_rows:, :] = sums[...].astype(BF16)


def final_body(shards, heads, steps, meta, *refs):
    refs = list(refs)

    def take(amount):
        found = refs[:amount]
        del refs[:amount]
        return found

    count = shards // 2 + 1
    sets = [(take(count), take(count)) for _ in range(2)]
    mixed = take(count)
    x_ref, cot_ref, cols_ref, scale, out_ref, layer_ref = refs
    step = pl.program_id(0)
    me = meta[1]
    rows, part = x_ref.shape
    width = part * shards
    per_step = rows // part
    layer_ref[...] = add_all([one[...].astype(F32) for one in [x_ref] + mixed]).astype(BF16)

    def finish(parts, tails, row):
        sums = add_all([one[...].astype(F32) for one in tails])
        for j in range(per_step):
            at = slice(j * part, (j + 1) * part)
            spot = INV * heads
            inverse = jnp.broadcast_to(cols_ref[at, spot : spot + 1], (part, part))
            group, line = divmod(row + j, 8)
            total = column_of(sums[8 * group : 8 * group + 8], line)
            share = widen(total / width, part) * inverse * inverse * inverse
            grad = add_all([one[at, :].astype(F32) for one in parts]) * scale[me]
            out_ref[at, :] = cot_ref[at, :].astype(F32) + inverse * grad - x_ref[at, :].astype(F32) * share

    for s in range(steps):
        parts, tails = sets[2 * s // steps]

        @pl.when(step == s)
        def _(s=s, parts=parts, tails=tails):
            finish(parts, tails, (s % (steps // 2)) * per_step)


def weights_body(inner, heads, meta, keep_ref, got_ref, late_keep, late_got, z_ref, out_ref, x_ref, dt_ref):
    total = keep_ref[0].astype(F32) + got_ref[0].astype(F32)
    z_ref[...] = total[:, :inner]
    out_ref[...] = total[:, inner:].T
    total = late_keep[0].astype(F32) + late_got[0].astype(F32)
    x_ref[...] = total[:, :inner]
    dt_ref[...] = total[:, inner : inner + heads]


def swap(shard, axis, flip):
    return lax.ppermute(shard, axis, [(i, i ^ flip) for i in range(lax.axis_size(axis))])


def handed(meta, array, after):
    return call(nothing, (1,), [meta], [], [], (1, 1000), "hand_on", after=after, carry=[array], room=2)[-1]


def nothing(meta):
    pass


def gather_far(shard):
    return {k: swap(shard, "head", k) for k in range(2, lax.axis_size("head"), 2)}


def gather_near(shard, far):
    found = []
    for k in range(0, lax.axis_size("head"), 2):
        one = far[k] if k else shard
        found += [one, swap(one, "head", 1)]
    return found


class Stages:
    def __init__(self, steps):
        self.steps = steps
        self.job = next(steps)

    def terms(self, meta, after=()):
        while self.job[0] is not None:
            run_stages(meta, [self], after)
        return self.job[1]


def run_stages(meta, stages, after):
    stages = [one for one in stages if one.job[0] is not None]
    if not stages:
        return []
    jobs = [one.job for one in stages]

    def body(meta, *refs):
        ins, outs = 0, sum(len(job[1]) for job in jobs)
        for work, arrays, shapes in jobs:
            work(meta, *refs[ins : ins + len(arrays)], *refs[outs : outs + len(shapes)])
            ins, outs = ins + len(arrays), outs + len(shapes)

    made = call(
        body,
        (1,),
        [meta] + [whole_of(array) for job in jobs for array in job[1]],
        [(shape, dtype, whole(shape)) for job in jobs for shape, dtype in job[2]],
        [],
        (1, 1000),
        "sums",
        after=after,
        room=14,
    )
    at = 0
    for one, job in zip(stages, jobs):
        one.job = one.steps.send(made[at : at + len(job[2])])
        at += len(job[2])
    return made[:-1]


def near_body(meta, one_ref, two_ref, out_ref):
    out_ref[...] = (one_ref[...].astype(F32) + two_ref[...].astype(F32)).astype(BF16)


def scatter_near(parts):
    return [swap(parts[k + 1], "head", 1) for k in range(0, len(parts), 2)]


def scatter_far(parts, got):
    found = [parts[0], got[0]]
    for k in range(2, len(parts), 2):
        (near,) = yield near_body, [parts[k], got[k // 2]], [(parts[k].shape, BF16)]
        found.append(swap(near, "head", k))
    yield None, found


def add_body(meta, one_ref, two_ref, out_ref):
    out_ref[...] = one_ref[...] + two_ref[...]


def add_head(values):
    bits = lax.axis_size("head").bit_length() - 1
    for bit in range(bits):
        got = swap(values, "head", 1 << bit)
        if bit == bits - 1:
            yield None, (values, got)
        else:
            (values,) = yield add_body, [values, got], [(values.shape, F32)]


def halve_body(axis, bit, meta, keep_ref, got_ref, kept_ref, sent_ref):
    mine = (meta[axis] >> bit) & 1
    for j in range(kept_ref.shape[0]):
        here, there = 2 * j + mine, 2 * j + 1 - mine
        kept_ref[j] = keep_ref[here].astype(F32) + got_ref[here].astype(F32)
        sent_ref[j] = (keep_ref[there].astype(F32) + got_ref[there].astype(F32)).astype(sent_ref.dtype)


def halve(keep, got, bit):
    count, rows, lanes = keep.shape
    shape = (count // 2, rows, lanes)
    return functools.partial(halve_body, 2, bit), [keep, got], [(shape, F32), (shape, got.dtype)]


def scatter_seq(keep, send):
    bits = lax.axis_size("seq").bit_length() - 1
    for bit in range(bits):
        received = swap(send, "seq", 1 << bit)
        if bit < bits - 1:
            keep, send = yield halve(keep, received, bit + 1)
    yield None, (keep, received)


def sum_rows_everywhere(keep, send):
    got = swap(send, "head", 1)
    for bit in range(1, lax.axis_size("head").bit_length() - 1):
        (keep,) = yield add_body, [keep, got], [(keep.shape, F32)]
        got = swap(keep, "head", 1 << bit)
    for bit in reversed(range(lax.axis_size("seq").bit_length() - 1)):
        rows, lanes = keep.shape
        shape = (2, rows // 2, lanes)
        kept, sent = yield halve(keep.reshape(shape), got.reshape(shape), bit)
        keep, sent = kept.reshape(shape[1:]), sent.reshape(shape[1:])
        got = swap(sent, "seq", 1 << bit)
    yield None, (keep, got)


def pack_small(target, at, values):
    lanes = target.shape[1]
    high, low = halves_of(values)
    for t in range(values.shape[1] // lanes):
        part = slice(t * lanes, (t + 1) * lanes)
        both = jnp.concatenate([high[:, part].astype(F32), low[:, part].astype(F32)], axis=0)
        target[at + 16 * t : at + 16 * t + 16, :] = both.astype(BF16)


def unpack_small(source, at):
    rows = source[at:, :].astype(F32)
    pieces_found = [
        rows[16 * t : 16 * t + 8] + rows[16 * t + 8 : 16 * t + 16] for t in range(rows.shape[0] // 16)
    ]
    return jnp.concatenate(pieces_found, axis=1)


def open_body(meta, keep_ref, got_ref, owned_ref, shared_ref, more_ref, out_ref):
    rows = keep_ref.shape[0]
    out_ref[:rows, :] = (keep_ref[...] + got_ref[...]).astype(BF16)
    shared = shared_ref[...] + more_ref[...]
    pack_small(out_ref, rows, jnp.concatenate([owned_ref[...], shared], axis=1))


def widen_body(bit, rows, last, meta, own_ref, got_ref, out_ref, *small_ref):
    mine = (meta[2] >> bit) & 1
    own, got = own_ref[:rows, :], got_ref[:rows, :]
    out_ref[:rows, :] = jnp.where(mine == 0, own, got)
    out_ref[rows : 2 * rows, :] = jnp.where(mine == 0, got, own)
    small = unpack_small(own_ref, rows) + unpack_small(got_ref, rows)
    if not last:
        pack_small(out_ref, 2 * rows, small)
        return
    taps_x, bias_x, gain_x, skip_x, bias_dt, rate_x, taps_bc, bias_bc, gain_in, held = small_ref
    inner, maps, part = bias_x.shape[1], bias_bc.shape[1], gain_in.shape[1]
    heads = skip_x.shape[1]
    reach = taps_x.shape[0]
    taps_x[...] = small[:reach, :inner]
    bias_x[...] = small[4:5, :inner]
    gain_x[...] = small[5:6, :inner]
    skip_x[...] = per_head(small[:, :inner], expander(heads, inner), 3)[6:7]
    bias_dt[...] = small[7:8, :heads]
    rate_x[...] = small[7:8, 128 : 128 + heads]
    taps_bc[...] = small[:reach, inner : inner + maps]
    bias_bc[...] = small[4:5, inner : inner + maps]
    held[...] = small[:, inner + maps :]
    gain_in[...] = held[:1, pl.ds(pl.multiple_of(meta[1] * part, part), part)]


def end_sums(terms, owned, shared, more, heads, reach, part):
    keep, got = terms
    rows, lanes = keep.shape
    width = owned.shape[1] + shared.shape[1]
    extra = 16 * (width // lanes)
    (held,) = yield open_body, [keep, got, owned, shared, more], [((rows + extra, lanes), BF16)]
    bits = lax.axis_size("seq").bit_length() - 1
    for bit in range(bits):
        got = swap(held, "seq", 1 << bit)
        last = bit == bits - 1
        outs = [((2 * rows + (0 if last else extra), lanes), BF16)]
        if last:
            inner = owned.shape[1]
            small = [(reach, inner), (1, inner), (1, inner), (1, heads), (1, heads), (1, heads)]
            small += [(reach, lanes), (1, lanes), (1, part), (8, width - inner - lanes)]
            outs += [(one, F32) for one in small]
        found = yield functools.partial(widen_body, bit, rows, last), [held, got], outs
        held, rows = found[0], 2 * rows
    mine = lax.axis_index("head") & 1
    other = swap(held, "head", 1)
    low, high = jnp.where(mine == 0, held, other), jnp.where(mine == 0, other, held)
    yield None, (jnp.concatenate([low, high], axis=0).astype(F32), found[1:-1])


def pair_of(forward, meta, own_ref, got_ref):
    state = own_ref.shape[0] - 8
    own_last = (meta[2] & 1) == (1 if forward else 0)
    own_fade, fade = own_ref[state:, :], got_ref[state:, :]
    own, other = own_ref[:state, :], got_ref[:state, :]
    pair = jnp.where(own_last, own_fade[:1] * other + own, fade[:1] * own + other)
    return pair, own_fade * fade


def pair_body(forward, meta, own_ref, got_ref, sent_ref, pair):
    half = pair.shape[0] // 2
    pair[...], fade = pair_of(forward, meta, own_ref, got_ref)
    sent_ref[:half, :] = pair[pl.ds(pl.multiple_of((meta[2] & 1) * half, half), half), :]
    sent_ref[half:, :] = fade


def whole_pair_body(forward, meta, own_ref, got_ref, sent_ref):
    state = sent_ref.shape[0] - 16
    pair, fade = pair_of(forward, meta, own_ref, got_ref)
    sent_ref[:state, :] = pair.astype(BF16)
    sent_ref[state:, :] = jnp.concatenate(
        [part.astype(F32) for part in halves_of(fade)], axis=0
    ).astype(BF16)


def whole_join_body(forward, count, meta, *refs):
    got_ref, out_ref = refs[count:]
    state = out_ref.shape[0]
    total = jnp.zeros(out_ref.shape, F32)
    for one in reversed(refs[:count]):
        tail = one[state:, :].astype(F32)
        total = (tail[:1] + tail[8:9]) * total + one[:state, :].astype(F32)
    own_last = (meta[2] & 1) == (1 if forward else 0)
    fade, other = got_ref[state : state + 1, :], got_ref[:state, :]
    out_ref[...] = jnp.where(own_last, fade * total + other, total)


def fold_body(count, meta, *refs):
    total_ref = refs[count]
    half = total_ref.shape[0]
    total = jnp.zeros(total_ref.shape, F32)
    for one in reversed(refs[:count]):
        total = one[half : half + 1, :] * total + one[:half, :]
    total_ref[...] = total


def join_body(forward, meta, total_ref, rest_ref, got_ref, out_ref):
    state = out_ref.shape[0]
    odd = meta[2] & 1
    own_last = odd == (1 if forward else 0)
    total, rest = total_ref[...], rest_ref[...]
    low, high = jnp.where(odd == 0, total, rest), jnp.where(odd == 0, rest, total)
    total = jnp.concatenate([low, high], axis=0)
    fade, other = got_ref[state : state + 1, :], got_ref[:state, :]
    out_ref[...] = jnp.where(own_last, fade * total + other, total)


def chain(meta, message, forward):
    size = lax.axis_size("seq")
    rows, lanes = message.shape
    state = rows - 8
    half = state // 2

    def small(body, arrays, shape, scratch, name, after=(), carry=(), dtype=F32):
        return call(
            body,
            (1,),
            [meta] + [whole_of(one) for one in arrays],
            [(shape, dtype, whole(shape))],
            scratch,
            (1, 1000),
            name,
            after=after,
            carry=carry,
            room=8,
        )

    got = swap(message, "seq", 1)
    after = yield None
    if forward:
        body = functools.partial(whole_pair_body, forward)
        sent = small(body, [message, got], (state + 16, lanes), [], "pair", after, dtype=BF16)[0]
    else:
        sent = small(
            functools.partial(pair_body, forward),
            [message, got],
            (half + 8, lanes),
            [pltpu.VMEM((state, lanes), F32)],
            "pair",
            after,
        )[0]
    found = []
    for by in range(2, size, 2):
        if forward:
            pairs = [(i, i + by) for i in range(size - by)]
        else:
            pairs = [(i + by, i) for i in range(size - by)]
        found.append(lax.ppermute(sent, "seq", pairs))
    after = yield sent
    if forward:
        body = functools.partial(whole_join_body, forward, len(found))
        yield small(body, found + [got], (state, lanes), [], "join", after)
    total = small(
        functools.partial(fold_body, len(found)), found, (half, lanes), [], "fold", after
    )[0]
    rest = swap(total, "seq", 1)
    after, carry = yield total
    body = functools.partial(join_body, forward)
    yield small(body, [total, rest, got], (state, lanes), [], "join", after, carry)


def on_device(
    inputs,
    input_norm_scale,
    w_z,
    w_x,
    w_bc,
    w_dt,
    conv_x_w,
    conv_x_b,
    conv_bc_w,
    conv_bc_b,
    dt_bias,
    a_log,
    d_skip,
    norm_inner,
    w_out,
    cotangent,
    lengths,
    order,
):
    tokens, part = inputs.shape
    shards = lax.axis_size("head")
    seq_size = lax.axis_size("seq")
    me = lax.axis_index("head")
    seq = lax.axis_index("seq")
    width = part * shards
    share = width // seq_size
    inner = w_z.shape[1]
    heads = dt_bias.shape[0]
    size = inner // heads
    state = w_bc.shape[1] // 2
    channels = inner + 2 * state
    taps_count = conv_x_w.shape[0]
    rows = 2 * SPAN
    spans = rows // SPAN
    count = tokens // rows
    half = tokens // 2
    half_count = count // 2
    first = seq * tokens

    number = lengths.shape[0]
    picker = (order[:, None] == jnp.arange(number, dtype=jnp.int32)[None, :]).astype(jnp.int32)
    placed = jnp.sum(picker * lengths[None, :], axis=1)
    starts = jnp.cumsum(placed) - placed
    spots = first + jnp.arange(tokens, dtype=jnp.int32)
    begin = jnp.max(jnp.where(starts[None, :] <= spots[:, None], starts[None, :], 0), axis=1)
    begin = begin.astype(jnp.int32)
    begin_col = jnp.broadcast_to(begin[:, None], (tokens, 128))
    begin_row = jnp.broadcast_to(begin[None, :], (8, tokens))
    ends = begin.reshape(tokens // SPAN, SPAN)[:, -1]
    ends = jnp.concatenate([jnp.stack([first, me, seq]).astype(jnp.int32), ends])
    meta = Place(tokens, ends)

    edge = lax.ppermute(
        inputs[tokens - EDGE :], "seq", [(i, i + 1) for i in range(seq_size - 1)]
    )
    edges = gather_near(edge, gather_far(edge))
    own_halves = [inputs[:half], inputs[half:]]
    xs = [gather_near(own_halves[0], gather_far(own_halves[0]))]
    late_half = handed(meta, own_halves[1], [xs[0][2], edges[2]])
    late_far = gather_far(late_half)
    cots = []

    scale = input_norm_scale.reshape(shards, 1, part)
    taps = jnp.concatenate([conv_x_w, conv_bc_w], axis=1)
    bias = jnp.concatenate([conv_x_b, conv_bc_b])[None, :]
    rate = -jnp.exp(a_log)[None, :]
    w_maps = jnp.concatenate([w_bc, w_dt, jnp.zeros((width, 128 - heads), BF16)], axis=1)
    skip = jnp.repeat(d_skip, size)[None, :]
    inner_gain = norm_inner[None, :]
    scale_row = input_norm_scale[None, :]
    prepared = [begin_row, skip, inner_gain, scale_row, rate]

    def fore(i):
        return i

    def back(i):
        return count - 1 - i

    big = [
        ((tokens, width), BF16, "rows", FAR),
        ((tokens, inner), BF16, "rows", FAR),
        ((tokens, 2 * state), BF16, "rows", FAR),
        ((tokens, inner), BF16, "rows", NEAR),
        ((tokens, inner), BF16, "rows", NEAR),
        ((tokens, 2 * state), BF16, "rows", NEAR),
        ((tokens, inner), BF16, "rows", FAR),
        ((tokens, 2 * state), BF16, "rows", FAR),
        ((tokens, 128), F32, "rows", NEAR),
        ((heads, tokens), F32, "lanes", NEAR),
        ((tokens // SPAN, state, inner), F32, "stack", NEAR),
        ((tokens // SPAN, 8, inner), F32, "stack", NEAR),
        ((tokens // SPAN, 8, inner), F32, "stack", NEAR),
    ]

    def spec_of(shape, kind, step):
        if kind == "rows":
            return rows_at(rows, shape[1], step)
        if kind == "lanes":
            return lanes_at(shape[0], rows, step)
        return stack_at((spans,) + shape[1:], step)

    carried = None
    for chunk in range(2):
        opens, closes = chunk == 0, chunk == 1
        start = chunk * half_count

        def here(i, start=start):
            return start + i

        ins = [ends] + [(one, rows_at(rows, part, fore)) for one in xs[chunk]]
        if opens:
            ins += [whole_of(one) for one in edges]
        else:
            ins += [whole_of(one) for one in carried]
        ins += [(begin_col, rows_at(rows, 128, here))]
        ins += [
            whole_of(one)
            for one in (scale, w_x, w_maps, taps, bias, dt_bias[None, :], rate)
        ]
        outs = [
            (shape, dtype, spec_of(shape, kind, here), space) for shape, dtype, kind, space in big
        ]
        if opens:
            extra = [((EDGE, channels), BF16), ((EDGE, width), BF16)]
        else:
            extra = []
        if closes:
            extra += [((state + 8, inner), F32)]
        else:
            extra += [((EDGE, channels), BF16), ((state, inner), F32), ((8, inner), F32)]
        outs += [(shape, dtype, whole(shape)) for shape, dtype in extra]
        found = call(
            functools.partial(
                project_body, shards, inner, state, heads, start, half_count, opens, closes
            ),
            (half_count,),
            ins,
            outs,
            [
                pltpu.VMEM((rows + 8, channels), F32),
                pltpu.VMEM((state, inner), F32),
                pltpu.VMEM((8, inner), F32),
            ],
            (12, 1000000),
            "project",
            room=ROOM_PROJECT,
            after=prepared if opens else [],
            carry=[cotangent[chunk * half : (chunk + 1) * half]],
            kept=None if opens else dict(enumerate(held)),
        )
        held = found[: len(big)]
        if opens:
            late_far = {k: handed(meta, one, [found[-2]]) for k, one in late_far.items()}
            xs.append(gather_near(late_half, late_far))
            early_cot, early_cot_far = found[-1], gather_far(found[-1])
        else:
            late_cot, late_cot_far = found[-1], gather_far(found[-1])
            early_cot_far = {k: handed(meta, one, [found[-2]]) for k, one in early_cot_far.items()}
            cots.append(gather_near(early_cot, early_cot_far))
        if opens:
            pre_edge, edge_normed = found[len(big) : len(big) + 2]
            carried = found[len(big) + 2 : -2]
        else:
            message = found[len(big)]
    (
        normed,
        pre_x,
        pre_bc,
        x,
        xdt,
        bc,
        slope_x,
        slope_bc,
        cols,
        runt,
        states,
        upto,
        own,
    ) = held

    links = chain(meta, message, True)
    next(links)
    found = None
    for chunk in range(2):
        start = chunk * half_count
        if chunk == 1:
            sent = links.send([found[-1]])
            late_cot_far = {k: handed(meta, one, [sent]) for k, one in late_cot_far.items()}
            cots.append(gather_near(late_cot, late_cot_far))

        def here(i, start=start):
            return start + i

        found = call(
            functools.partial(inside_body, shards, state, heads, start),
            (half_count,),
            [meta]
            + [(one, rows_at(rows, part, fore)) for one in cots[chunk]]
            + [
                (begin_col, rows_at(rows, 128, here)),
                (bc, rows_at(rows, 2 * state, here)),
                (xdt, rows_at(rows, inner, here)),
                (cols, rows_at(rows, 128, here)),
                (runt, lanes_at(heads, rows, here)),
                (normed, rows_at(rows, width, here)),
                whole_of(w_z),
                whole_of(w_out),
            ],
            [((tokens, inner), F32, rows_at(rows, inner, here), NEAR)] * 3,
            [pltpu.VMEM((rows, width), BF16)],
            (8, 1000000),
            "inside",
            room=ROOM_INSIDE,
            kept=None if found is None else dict(enumerate(found[:3])),
            after=() if found is None else [sent],
        )
    inside, z, grad_y, done = found
    incoming, _ = links.send([done])

    y, sums, done = call(
        functools.partial(gate_body, state, heads),
        (count,),
        [meta]
        + [
            (bc, rows_at(rows, 2 * state, fore)),
            (x, rows_at(rows, inner, fore)),
            (cols, rows_at(rows, 128, fore)),
            (z, rows_at(rows, inner, fore)),
            (grad_y, rows_at(rows, inner, fore)),
            (inside, rows_at(rows, inner, fore)),
            (states, stack_at((spans, state, inner), fore)),
            (upto, stack_at((spans, 8, inner), fore)),
            whole_of(incoming),
            whole_of(skip),
            whole_of(inner_gain),
        ],
        [
            ((tokens, inner), F32, rows_at(rows, inner, fore), NEAR),
            ((8, tokens), F32, lanes_at(8, rows, fore)),
        ],
        [],
        (9, 1000000),
        "gate",
        room=ROOM_GATE,
    )

    all_sums = [sums] + [swap(sums, "head", k) for k in range(1, shards)]

    y_norm, dz, dy, dstates, after, message, g_norm_inner, g_skip, done = call(
        functools.partial(norm_body, shards, state, heads, count),
        (count,),
        [meta]
        + [(one, lanes_at(8, rows, back)) for one in all_sums]
        + [
            (bc, rows_at(rows, 2 * state, back)),
            (x, rows_at(rows, inner, back)),
            (cols, rows_at(rows, 128, back)),
            (z, rows_at(rows, inner, back)),
            (y, rows_at(rows, inner, back)),
            (grad_y, rows_at(rows, inner, back)),
            (own, stack_at((spans, 8, inner), back)),
            whole_of(skip),
            whole_of(inner_gain),
        ],
        [
            ((tokens, inner), BF16, rows_at(rows, inner, back), NEAR),
            ((tokens, inner), BF16, rows_at(rows, inner, back), NEAR),
            ((tokens, inner), F32, rows_at(rows, inner, back), NEAR),
            ((tokens // SPAN, state, inner), F32, stack_at((spans, state, inner), back), NEAR),
            ((tokens // SPAN, 8, inner), F32, stack_at((spans, 8, inner), back), NEAR),
            ((state + 8, inner), F32, whole((state + 8, inner))),
            ((8, inner), F32, whole((8, inner))),
            ((8, inner), F32, whole((8, inner))),
        ],
        [pltpu.VMEM((state, inner), F32), pltpu.VMEM((8, inner), F32)],
        (12, 1000000),
        "norm",
        room=ROOM_NORM,
    )


    def inside_back(chunk, kept, after):
        def here(i):
            return chunk * half_count + i

        return call(
            functools.partial(inside_back_body, state, heads, chunk * half_count),
            (half_count,),
            [
                meta,
                (begin_row, lanes_at(8, rows, here)),
                (bc, rows_at(rows, 2 * state, here)),
                (xdt, rows_at(rows, inner, here)),
                (dy, rows_at(rows, inner, here)),
                (cols, rows_at(rows, 128, here)),
                (runt, lanes_at(heads, rows, here)),
            ],
            [
                ((tokens, inner), F32, rows_at(rows, inner, here), NEAR),
                ((tokens, 2 * state), F32, rows_at(rows, 2 * state, here), NEAR),
            ],
            [],
            (7, 1000000),
            "inside_back",
            room=ROOM_INSIDE,
            kept=None if kept is None else dict(enumerate(kept[:2])),
            after=after,
        )

    links = chain(meta, message, False)
    next(links)
    held = inside_back(0, None, [])
    sent = links.send([held[-1]])

    pair_shape = (seq_size // 2, share, 2 * inner)
    found = call(
        functools.partial(early_body, shards, count),
        (count,),
        [meta]
        + [
            (one, rows_at(rows, part, lambda i: jnp.minimum(i, half_count - 1)))
            for one in cots[0]
        ]
        + [
            (one, rows_at(rows, part, lambda i: jnp.maximum(i - half_count, 0)))
            for one in cots[1]
        ]
        + [
            (normed, rows_at(rows, width, fore)),
            (y_norm, rows_at(rows, inner, fore)),
            (dz, rows_at(rows, inner, fore)),
            whole_of(w_out),
            whole_of(w_z),
        ],
        [((tokens, part), BF16, rows_at(rows, part, fore), FAR)] * shards
        + [
            (pair_shape, BF16, whole(pair_shape), FAR),
            (pair_shape, BF16, whole(pair_shape), FAR),
            ((8, width), F32, whole((8, width))),
        ],
        [
            pltpu.VMEM((rows, width), BF16),
            pltpu.VMEM((width, inner), F32),
            pltpu.VMEM((width, inner), F32),
        ],
        (12, 1000000),
        "early",
        after=[held[-1], sent],
        room=ROOM_EARLY,
    )
    out_parts, (early_keep, early_send, gain_z, done) = found[:shards], found[shards:]
    out_parts = [bare(one) for one in out_parts]
    total = links.send(())
    dxdt, dbc, done = inside_back(1, held, [total])
    sent_late = [bare(early_send)] + out_parts[1::2]
    outgoing, token, early_send, *odd_parts = links.send(([done], sent_late))
    out_parts[1::2] = odd_parts
    out_near = scatter_near(out_parts)
    early = Stages(scatter_seq(bare(early_keep), early_send))


    found = call(
        functools.partial(maps_back_body, state, heads, count),
        (count,),
        [
            meta,
            (begin_col, rows_at(rows, 128, back)),
            (bc, rows_at(rows, 2 * state, back)),
            (xdt, rows_at(rows, inner, back)),
            (dy, rows_at(rows, inner, back)),
            (cols, rows_at(rows, 128, back)),
            (slope_bc, rows_at(rows, 2 * state, back)),
            (pre_bc, rows_at(rows, 2 * state, back)),
            whole_of(pre_edge),
            (normed, rows_at(rows, width, back)),
            whole_of(edge_normed),
            whole_of(w_bc),
            (dbc, rows_at(rows, 2 * state, back)),
            (states, stack_at((spans, state, inner), back)),
            (upto, stack_at((spans, 8, inner), back)),
            (dstates, stack_at((spans, state, inner), back)),
            (after, stack_at((spans, 8, inner), back)),
            (own, stack_at((spans, 8, inner), back)),
            whole_of(incoming),
            whole_of(outgoing),
            whole_of(conv_bc_w),
        ],
        [
            ((tokens, 2 * state), BF16, rows_at(rows, 2 * state, back), NEAR),
            ((tokens // SPAN, 8, heads), F32, stack_at((spans, 8, heads), back), NEAR),
            ((tokens // SPAN, state, inner), F32, stack_at((spans, state, inner), back), NEAR),
            ((EDGE, 2 * state), F32, whole((EDGE, 2 * state))),
            ((EDGE, 2 * state), F32, whole((EDGE, 2 * state))),
            ((taps_count, 8, 2 * state), F32, whole((taps_count, 8, 2 * state))),
            ((8, 2 * state), F32, whole((8, 2 * state))),
            ((width // 2, 2 * state), F32, whole((width // 2, 2 * state))),
            ((width // 2, 2 * state), F32, whole((width // 2, 2 * state))),
            ((8, width), F32, whole((8, width))),
        ],
        [
            pltpu.VMEM((rows + 8, 2 * state), F32),
            pltpu.VMEM((rows + 8, 128), jnp.int32),
            pltpu.VMEM((width, 2 * state), F32),
        ],
        (12, 1000000),
        "maps_back",
        room=ROOM_MAPS,
    )
    dpre_bc, through, ds_all, tail_bc, left_bc, taps_bc, bias_bc = found[:7]
    bc_keep, bc_send, gain_bc, done = found[7:]
    left_pairs = [(i + 1, i) for i in range(seq_size - 1)]
    right_bc = lax.ppermute(left_bc, "seq", left_pairs)
    bc_sums = Stages(sum_rows_everywhere(bc_keep, bc_send))
    out_sums = Stages(scatter_far(out_parts, out_near))
    sent = run_stages(meta, [bc_sums, out_sums], [done])

    late_width = inner + 128
    late_shape = (seq_size // 2, share, late_width)

    def inner_back(opens, start, fresh_steps, extra, after):
        steps = fresh_steps if opens else fresh_steps + 1

        def now(i):
            return start + jnp.minimum(i, fresh_steps - 1)

        def late(i):
            return jnp.maximum(i - 1, 0) if opens else start - 1 + i

        def written(i):
            return jnp.maximum(i - 1, 0) if opens else i

        outs = [
            ((half, inner), BF16, rows_at(rows, inner, written), NEAR),
            ((half, heads), BF16, rows_at(rows, heads, written)),
        ]
        sums = [
            ((taps_count, 8, inner), F32, whole((taps_count, 8, inner))),
            ((8, inner), F32, whole((8, inner))),
            ((16, heads), F32, whole((16, heads))),
        ]
        sums_scratch = []
        if opens:
            outs += sums + [
                ((rows, inner), F32, whole((rows, inner)), NEAR),
                ((rows, heads), BF16, whole((rows, heads))),
                ((EDGE, inner), F32, whole((EDGE, inner))),
                ((width, late_width), F32, whole((width, late_width)), NEAR),
            ]
        else:
            outs += [
                (late_shape, BF16, whole(late_shape), FAR),
                (late_shape, BF16, whole(late_shape), FAR),
                ((8, inner), F32, whole((8, inner))),
                ((8, 2 * state + width), F32, whole((8, 2 * state + width))),
            ]
            sums_scratch = [pltpu.VMEM(shape, F32) for shape, _, _ in sums]
            sums_scratch += [pltpu.VMEM((width, late_width), F32)]
        return call(
            functools.partial(inner_back_body, state, heads, start, fresh_steps, opens),
            (steps,),
            [
                meta,
                (begin_col, rows_at(rows, 128, now)),
                (begin_col, rows_at(rows, 128, late)),
                (bc, rows_at(rows, 2 * state, now)),
                (Held(bare(x), FAR), rows_at(rows, inner, now)),
                (xdt, rows_at(rows, inner, now)),
                (dy, rows_at(rows, inner, now)),
                (Held(bare(y), FAR), rows_at(rows, inner, now)),
                (cols, rows_at(rows, 128, now)),
                (slope_x, rows_at(rows, inner, now)),
                (pre_x, rows_at(rows, inner, late)),
                (normed, rows_at(rows, width, late)),
                (dxdt, rows_at(rows, inner, now)),
                (through, stack_at((spans, 8, heads), now)),
                (ds_all, stack_at((spans, state, inner), now)),
                whole_of(skip),
                whole_of(rate),
                whole_of(conv_x_w),
            ]
            + [whole_of(one) for one in extra],
            outs,
            sums_scratch
            + [
                pltpu.VMEM((rows + 8, inner), F32),
                pltpu.VMEM((rows + 8, 128), jnp.int32),
                pltpu.VMEM((rows, inner), F32),
                pltpu.VMEM((rows, heads), BF16),
                pltpu.VMEM((rows, heads), BF16),
            ],
            (6 * fresh_steps, 1000000),
            "inner_back",
            after=after,
            room=ROOM_INNER,
        )

    found = inner_back(True, 0, count - 1, [pre_edge], sent + [right_bc])
    sent = run_stages(meta, [early, bc_sums, out_sums], [found[-1]])
    dpre_low, ddt_low, taps_x, bias_x, scalars, held_du, held_ddt, left_x, weight_x, done = found
    right_x = lax.ppermute(left_x, "seq", left_pairs)

    def input_grad(chunk, dpre, ddt, extra, after, carry=()):
        start = chunk * half_count

        def here(i):
            return start + i

        whole_rows = half + EDGE
        return call(
            functools.partial(input_body, shards, half_count, chunk == 1),
            (half_count,),
            [meta]
            + [(Held(one, FAR), rows_at(rows, part, fore)) for one in xs[chunk]]
            + [
                (Held(bare(dz), FAR), rows_at(rows, inner, here)),
                (dpre, rows_at(rows, inner, fore)),
                (Held(bare(dpre_bc), FAR), rows_at(rows, 2 * state, here)),
                (ddt, rows_at(rows, heads, fore)),
            ]
            + [whole_of(one) for one in [w_z, w_x, w_bc, w_dt, scale] + extra],
            [((whole_rows, part), BF16, whole((whole_rows, part)))] * shards,
            [pltpu.VMEM((rows, 2 * state), BF16), pltpu.VMEM((EDGE, part), F32)],
            (8, 1000000),
            "input_grad",
            room=ROOM_INPUT,
            after=after,
            carry=carry,
        )

    found = inner_back(
        False,
        count - 1,
        1,
        [held_du, held_ddt, right_x, taps_x, bias_x, scalars, weight_x]
        + [w_x, w_dt, scale_row, gain_z, gain_bc]
        + [g_norm_inner, g_skip, taps_bc, bias_bc],
        sent,
    )
    dpre_high, ddt_high, late_keep, late_send, owned, shared, done = found
    late = Stages(scatter_seq(bare(late_keep), bare(late_send)))
    shared_sums = Stages(add_head(shared))
    sent = run_stages(meta, [bc_sums, out_sums], [done])
    sent += out_sums.terms(meta)[2:] + [early.job[1][1]]
    *parts_low, done = input_grad(0, dpre_low, ddt_low, [], sent)
    low_sums = Stages(scatter_far(parts_low, scatter_near(parts_low)))
    sent = run_stages(meta, [bc_sums, shared_sums, low_sums, early], [done])
    early_terms, mixed = early.terms(meta), out_sums.terms(meta)
    results = input_grad(
        1,
        dpre_high,
        ddt_high,
        [tail_bc, right_bc],
        sent,
        [mixed[0], early_terms[0]],
    )
    parts_high, (done, *own_terms) = results[:shards], results[shards:]
    mixed[0], early_keep = own_terms
    high_sums = Stages(scatter_far(parts_high, scatter_near(parts_high)))
    ends = Stages(
        end_sums(
            bc_sums.terms(meta), owned, *shared_sums.terms(meta), heads, taps_count, part
        )
    )
    far_low = low_sums.terms(meta)
    run_stages(meta, [late, ends], [done, far_low[-1], early_terms[1]])
    run_stages(meta, [late, high_sums, ends], ())
    far_high = high_sums.terms(meta)
    run_stages(meta, [late, ends], ())

    def low(i):
        return jnp.minimum(i, half_count - 1)

    def high(i):
        return jnp.maximum(i - half_count, 0)

    ins = []
    for terms, step in ((far_low, low), (far_high, high)):
        ins += [(one, rows_at(rows, part, step)) for one in terms]
        ins += [(one, pl.BlockSpec((EDGE, part), lambda i, *meta: (half // EDGE, 0))) for one in terms]
    grad_input, output, done = call(
        functools.partial(final_body, shards, heads, count),
        (count,),
        [meta]
        + ins
        + [(one, rows_at(rows, part, fore)) for one in mixed]
        + [
            (Held(inputs, FAR), rows_at(rows, part, fore)),
            (Held(cotangent, FAR), rows_at(rows, part, fore)),
            (cols, rows_at(rows, 128, fore)),
            whole_of(scale),
        ],
        [
            ((tokens, part), F32, rows_at(rows, part, fore)),
            ((tokens, part), BF16, rows_at(rows, part, fore)),
        ],
        [],
        (5, 1000000),
        "finals",
        room=10,
    )
    grad_w_z, grad_w_out, grad_w_x, grad_w_dt, _ = call(
        functools.partial(weights_body, inner, heads),
        (1,),
        [meta] + [whole_of(one) for one in (early_keep, early_terms[1]) + late.terms(meta)],
        [
            ((share, inner), F32, whole((share, inner))),
            ((inner, share), F32, whole((inner, share))),
            ((share, inner), F32, whole((share, inner))),
            ((share, heads), F32, whole((share, heads))),
        ],
        [],
        (2, 1000000),
        "weights",
        room=10,
    )
    grad_w_bc, small = ends.terms(meta, [done])
    taps_x, bias_x, gain_x, skip_x, bias_dt, rate_x, taps_bc, bias_bc, gain_in = small
    return (
        output,
        grad_input,
        gain_in.reshape(-1),
        grad_w_z,
        grad_w_x,
        grad_w_bc,
        grad_w_dt,
        taps_x,
        bias_x.reshape(-1),
        taps_bc,
        bias_bc.reshape(-1),
        bias_dt.reshape(-1),
        rate_x.reshape(-1),
        skip_x.reshape(-1),
        gain_x.reshape(-1),
        grad_w_out,
    )


def solution(mesh):
    placed = (
        P("seq", "head"),
        P(),
        P(None, "head"),
        P(None, "head"),
        P(),
        P(None, "head"),
        P(None, "head"),
        P("head"),
        P(),
        P(),
        P("head"),
        P("head"),
        P("head"),
        P("head"),
        P("head", None),
        P("seq", "head"),
        P(),
        P(),
    )
    return jax.shard_map(
        on_device,
        mesh=mesh,
        in_specs=placed,
        out_specs=(
            P("seq", "head"),
            P("seq", "head"),
            P("head"),
            P("seq", "head"),
            P("seq", "head"),
            P(),
            P("seq", "head"),
            P(None, "head"),
            P("head"),
            P(),
            P(),
            P("head"),
            P("head"),
            P("head"),
            P("head"),
            P("head", "seq"),
        ),
        check_vma=False,
    )
```

```python
import functools

import jax
import jax.numpy as jnp
from jax import lax
from jax.experimental import pallas as pl
from jax.experimental.pallas import tpu as pltpu
from jax.sharding import PartitionSpec as P

SPAN = 256
EDGE = 16
EPSILON = 1e-05
F32 = jnp.float32
BF16 = jnp.bfloat16
NEAR, FAR = pltpu.VMEM, pltpu.HBM
ROOM_PROJECT, ROOM_INSIDE, ROOM_GATE, ROOM_NORM = 14, 8, 6, 8
ROOM_EARLY, ROOM_MAPS, ROOM_INNER, ROOM_INPUT = 20, 12, 22, 12


def mm(left, right):
    return lax.dot_general(left, right, (((1,), (0,)), ((), ())), preferred_element_type=F32)


def mm_nt(left, right):
    return lax.dot_general(left, right, (((1,), (1,)), ((), ())), preferred_element_type=F32)


def mm_tn(left, right):
    return lax.dot_general(left, right, (((0,), (0,)), ((), ())), preferred_element_type=F32)


def pieces(values, count):
    found = []
    for _ in range(count):
        part = values.astype(BF16)
        found.append(part)
        values = values - part.astype(F32)
    return found


def add_all(terms):
    total = terms[0]
    for term in terms[1:]:
        total = total + term
    return total


def triangle(size, keep):
    rows = lax.broadcasted_iota(jnp.int32, (size, size), 0)
    cols = lax.broadcasted_iota(jnp.int32, (size, size), 1)
    return keep(rows, cols).astype(F32).astype(BF16)


def expander(heads, width, copies=1):
    rows = lax.broadcasted_iota(jnp.int32, (copies * heads, width), 0) & (heads - 1)
    cols = lax.broadcasted_iota(jnp.int32, (copies * heads, width), 1)
    size = width // heads
    return ((cols >= rows * size) & (cols < (rows + 1) * size)).astype(F32).astype(BF16)


def expand(values, spread):
    count = spread.shape[0] // values.shape[1]
    parts = [part.astype(F32) for part in pieces(values, count)]
    return mm(jnp.concatenate(parts, axis=1).astype(BF16), spread)


def per_head(values, spread, count=2):
    return add_all([mm_nt(part, spread) for part in pieces(values, count)])


def widen(column, width):
    lanes = column.shape[1]
    if width <= lanes:
        return column[:, :width]
    return jnp.concatenate([column] * (width // lanes), axis=1)


def row_ids(rows, lanes=128):
    return lax.broadcasted_iota(jnp.int32, (rows, lanes), 0)


def sigmoid(values):
    return 0.5 * jnp.tanh(0.5 * values) + 0.5


def softplus(values):
    return jnp.maximum(values, 0.0) + jnp.log1p(jnp.exp(-jnp.abs(values)))


def rows_of_sums(first, second):
    lane = lax.broadcasted_iota(jnp.int32, (first.shape[0], 128), 1)
    one = jnp.sum(first, axis=1, keepdims=True)
    two = jnp.sum(second, axis=1, keepdims=True)
    return jnp.where(lane == 0, one, jnp.where(lane == 1, two, 0.0)).T[:8]


def row_of_sums(values):
    lane = lax.broadcasted_iota(jnp.int32, (values.shape[0], 128), 1)
    return jnp.where(lane == 0, jnp.sum(values, axis=1, keepdims=True), 0.0).T[:8]


def column_of(rows, at):
    picks = (lax.broadcasted_iota(jnp.int32, (8, 128), 0) == at).astype(F32).astype(BF16)
    return add_all([mm_tn(part, picks) for part in pieces(rows, 3)])


def fold_rows(values):
    rows, lanes = values.shape
    return jnp.sum(values.reshape(rows // 8, 8, lanes), axis=0)


def halves_of(values):
    high = values.astype(BF16)
    return high, (values - high.astype(F32)).astype(BF16)


class Held:
    def __init__(self, array, space):
        self.array, self.space, self.shape = array, space, array.shape


def bare(one):
    return one.array if isinstance(one, Held) else one


def stays(one):
    return pltpu.with_memory_space_constraint(one.array, one.space) if isinstance(one, Held) else one


class Place:
    def __init__(self, tokens):
        self.tokens = tokens

    def __getitem__(self, which):
        index = lax.axis_index("head" if which == 1 else "seq")
        return index * self.tokens if which == 0 else index


def call(body, grid, ins, outs, scratch, work, name, kept=None, after=(), carry=(), room=24):
    place = ins[0]
    arrays = [stays(one[0]) for one in ins[1:]]
    specs = [one[1] for one in ins[1:]]
    aliases = {}
    own = len(arrays)
    for at, array in (kept or {}).items():
        aliases[len(arrays)] = at
        arrays.append(stays(array))
        specs.append(pl.BlockSpec(memory_space=pl.ANY))
    for array in after:
        arrays.append(stays(array))
        specs.append(pl.BlockSpec(memory_space=pl.ANY))
    for at, array in enumerate(carry):
        aliases[len(arrays)] = len(outs) + 1 + at
        arrays.append(array)
        specs.append(pl.BlockSpec(memory_space=pl.ANY))
    total = len(arrays)
    spaces = [one[3] if len(one) > 3 else None for one in outs]

    def only_own(*refs):
        token = refs[total + len(outs)]
        token[...] = jnp.zeros_like(token)
        body(place, *refs[:own], *refs[total : total + len(outs)], *refs[total + len(outs) + 1 + len(carry) :])

    found = pl.pallas_call(
        only_own,
        out_shape=[
            space(one[0], one[1]) if space else jax.ShapeDtypeStruct(one[0], one[1])
            for one, space in zip(outs, spaces)
        ]
        + [NEAR((8, 128), F32)]
        + [jax.ShapeDtypeStruct(one.shape, one.dtype) for one in carry],
        grid_spec=pltpu.PrefetchScalarGridSpec(
            num_scalar_prefetch=0,
            grid=grid,
            in_specs=specs,
            out_specs=[one[2] for one in outs]
            + [whole((8, 128))]
            + [pl.BlockSpec(memory_space=pl.ANY)] * len(carry),
            scratch_shapes=scratch,
        ),
        input_output_aliases=aliases,
        compiler_params=pltpu.CompilerParams(
            dimension_semantics=("arbitrary",) * len(grid), vmem_limit_bytes=room * 1024 * 1024
        ),
        cost_estimate=pl.CostEstimate(
            flops=int(work[0] * 1e9), bytes_accessed=int(work[1]), transcendentals=0
        ),
        name=name,
    )(*arrays)
    made = [Held(one, space) if space else one for one, space in zip(found, spaces)]
    return made + [Held(found[len(outs)], NEAR)] + list(found[len(outs) + 1 :])


def rows_at(rows, lanes, step):
    return pl.BlockSpec((rows, lanes), lambda i, *meta: (step(i), 0))


def lanes_at(rows, lanes, step):
    return pl.BlockSpec((rows, lanes), lambda i, *meta: (0, step(i)))


def stack_at(shape, step):
    return pl.BlockSpec(shape, lambda i, *meta: (step(i),) + (0,) * (len(shape) - 1))


def whole(shape):
    return pl.BlockSpec(shape, lambda i, *meta: (0,) * len(shape))


def whole_of(array):
    return (array, whole(array.shape))


def block_at(me, k, size):
    return pl.ds(pl.multiple_of((me ^ k) * size, size), size)


DT, RAW, RUN, REACH, KEEP, INV = range(6)


def column(ref, which, heads):
    return ref[:, which * heads : (which + 1) * heads]


def project_body(shards, inner, state, heads, start, steps, opens, closes, meta, *refs):
    refs = list(refs)

    def take(amount):
        found = refs[:amount]
        del refs[:amount]
        return found

    xs = take(shards)
    if opens:
        edges = take(shards)
    else:
        tail_in, carry_in, decay_in = take(3)
    begin_ref, scale, w_x, w_maps, taps, bias, dt_bias, rate = take(8)
    (
        normed_ref,
        pre_x_ref,
        pre_bc_ref,
        x_ref,
        xdt_ref,
        bc_ref,
        slope_x_ref,
        slope_bc_ref,
        cols_ref,
        runt_ref,
        state_ref,
        upto_ref,
        own_ref,
    ) = take(13)
    if opens:
        edge_ref, edge_normed = take(2)
    if closes:
        (message_ref,) = take(1)
    else:
        tail_ref, carry_out, decay_out = take(3)
    ext, carry, decay = take(3)
    step = pl.program_id(0)
    me = meta[1]
    rows = x_ref.shape[0]
    part = xs[0].shape[1]
    width = part * shards
    maps = 2 * state
    at_block = (start + step) * (rows // SPAN)
    first = meta[0] + at_block * SPAN

    def normalise(sources, target):
        loaded = [source[...].astype(F32) for source in sources]
        total = jnp.sum(add_all([one * one for one in loaded]), axis=1, keepdims=True)
        inverse = lax.rsqrt(total / width + EPSILON)
        for k, one in enumerate(loaded):
            target[:, block_at(me, k, part)] = (one * inverse * scale[me ^ k]).astype(BF16)
        return inverse

    @pl.when(step == 0)
    def _():
        if opens:
            normalise(edges, edge_normed)
            held = edge_normed[...]
            edge_ref[:, :inner] = mm(held, w_x[...]).astype(BF16)
            edge_ref[:, inner:] = mm(held, w_maps[:, :maps]).astype(BF16)
            ext[:8, :] = edge_ref[EDGE - 8 :, :].astype(F32)
            carry[...] = jnp.zeros_like(carry)
            decay[...] = jnp.ones_like(decay)
        else:
            ext[:8, :] = tail_in[EDGE - 8 :, :].astype(F32)
            carry[...] = carry_in[...]
            decay[...] = decay_in[...]

    @pl.when(step > 0)
    def _():
        ext[:8, :] = ext[rows : rows + 8, :]

    inverse = normalise(xs, normed_ref)
    held = normed_ref[...]
    pre_x_ref[...] = mm(held, w_x[...]).astype(BF16)
    both = mm(held, w_maps[...])
    pre_bc_ref[...] = both[:, :maps].astype(BF16)
    ext[8:, :inner] = pre_x_ref[...].astype(F32)
    ext[8:, inner:] = pre_bc_ref[...].astype(F32)
    raw = both[:, maps : maps + heads] + dt_bias[...]
    dt = softplus(raw)

    begin = begin_ref[...]
    place = row_ids(rows) + first
    reach = taps.shape[0] - 1
    channels = ext.shape[1]
    total = bias[...] + taps[reach : reach + 1, :] * ext[8:, :]
    for lag in range(1, reach + 1):
        valid = widen((place - lag >= begin).astype(F32), channels)
        lagged = ext[8 - lag : 8 - lag + rows, :] * valid
        total = total + taps[reach - lag : reach - lag + 1, :] * lagged
    sig = sigmoid(total)
    conv = total * sig
    slope = (sig * (1.0 + total * (1.0 - sig))).astype(BF16)
    slope_x_ref[...] = slope[:, :inner]
    slope_bc_ref[...] = slope[:, inner:]
    x = conv[:, :inner]
    x_ref[...] = x.astype(BF16)
    bc = conv[:, inner:].astype(BF16)
    bc_ref[...] = bc

    spread = expander(heads, inner, 2)
    xdt_ref[...] = (x * expand(dt, spread)).astype(BF16)
    log_decay = dt * rate[...]
    lower = triangle(SPAN, lambda r, c: r >= c)
    upper = triangle(SPAN, lambda r, c: r <= c)
    spans = [slice(s * SPAN, (s + 1) * SPAN) for s in range(rows // SPAN)]
    runs, tails, reaches, keeps, owns = [], [], [], [], []
    for s, at in enumerate(spans):
        parts = [part.astype(F32) for part in pieces(log_decay[at], 3)]
        parts = jnp.concatenate(parts, axis=1).astype(BF16)
        sums = mm(lower, parts)
        runs.append(sums[:, :heads] + sums[:, heads : 2 * heads] + sums[:, 2 * heads :])
        sums = mm_tn(parts, upper)
        runt_ref[:, at] = sums[:heads] + sums[heads : 2 * heads] + sums[2 * heads :]
    for s, at in enumerate(spans):
        run = runs[s]
        tail = run[SPAN - 1 : SPAN, :]
        last = begin[(s + 1) * SPAN - 1 : (s + 1) * SPAN, :]
        keeps.append(jnp.exp(tail - run) * (place[at] >= last).astype(F32)[:, :heads])
        reaches.append(jnp.exp(run) * (begin[at] < first + s * SPAN).astype(F32)[:, :heads])
        alive = (last < first + s * SPAN).astype(F32)[:, :heads]
        owns.append(jnp.broadcast_to(jnp.exp(tail) * alive, (8, heads)))
    keep = jnp.concatenate(keeps, axis=0)
    run, reached = jnp.concatenate(runs, axis=0), jnp.concatenate(reaches, axis=0)
    columns = [dt, raw, run, reached, keep, jnp.broadcast_to(inverse, (rows, heads))]
    rest = cols_ref.shape[1] - len(columns) * heads
    cols_ref[...] = jnp.concatenate(columns + [jnp.zeros((rows, rest), F32)], axis=1)
    high, low = halves_of(x * expand(keep * dt, spread))
    own_all = expand(jnp.concatenate(owns, axis=0), expander(heads, inner, 3))
    for s, at in enumerate(spans):
        own = own_all[8 * s : 8 * s + 8]
        state_ref[s] = carry[...]
        upto_ref[s] = decay[...]
        own_ref[s] = own
        b = bc[at, :state]
        carry[...] = own[:1] * carry[...] + (mm_tn(b, high[at]) + mm_tn(b, low[at]))
        decay[...] = decay[...] * own

    @pl.when(step == steps - 1)
    def _():
        if closes:
            pack_message(message_ref, carry[...], decay[...])
        else:
            tail_ref[:, :inner] = pre_x_ref[rows - EDGE :, :]
            tail_ref[:, inner:] = pre_bc_ref[rows - EDGE :, :]
            carry_out[...] = carry[...]
            decay_out[...] = decay[...]


def pack_message(target, carry, decay):
    state = carry.shape[0]
    target[:state, :] = carry
    target[state:, :] = decay


def assemble(sources, me, target):
    part = sources[0].shape[1]
    for k, source in enumerate(sources):
        target[:, block_at(me, k, part)] = source[...]


def inside_body(shards, state, heads, start, meta, *refs):
    cots, refs = refs[:shards], refs[shards:]
    begin_ref, bc_ref, xdt_ref, cols_ref, runt_ref, normed_ref, w_z, w_out = refs[:8]
    y_ref, z_ref, grad_ref, cot = refs[8:]
    z_ref[...] = mm(normed_ref[...], w_z[...])
    assemble(cots, meta[1], cot)
    grad_ref[...] = mm_nt(cot[...], w_out[...])
    rows, inner = y_ref.shape
    first = meta[0] + (start + pl.program_id(0)) * rows
    row = lax.broadcasted_iota(jnp.int32, (SPAN, SPAN), 0)
    col = lax.broadcasted_iota(jnp.int32, (SPAN, SPAN), 1)
    size = inner // heads
    lane = lax.broadcasted_iota(jnp.int32, (SPAN, 2 * size), 1)
    for s in range(rows // SPAN):
        at = slice(s * SPAN, (s + 1) * SPAN)
        begin = widen(begin_ref[at, :], SPAN)
        allowed = (col <= row) & (col + (first + s * SPAN) >= begin)
        scores = mm_nt(bc_ref[at, state:], bc_ref[at, :state])
        scores = jnp.where(allowed, scores, 0.0)
        for pair in range(heads // 2):
            lanes = slice(pair * 2 * size, (pair + 1) * 2 * size)
            both = xdt_ref[at, lanes]
            total = None
            for j in range(2):
                h = 2 * pair + j
                lane_at = RUN * heads + h
                spread = cols_ref[at, lane_at : lane_at + 1] - runt_ref[h : h + 1, at]
                mixing = (scores * jnp.exp(jnp.minimum(spread, 0.0))).astype(BF16)
                mine = jnp.where((lane < size) == (j == 0), both, jnp.zeros_like(both))
                product = mm(mixing, mine)
                total = product if total is None else total + product
            y_ref[at, lanes] = total


def gate_body(state, heads, meta, *refs):
    (
        bc_ref,
        x_ref,
        cols_ref,
        z_ref,
        grad_ref,
        inside_ref,
        state_ref,
        upto_ref,
        incoming,
        skip,
        norm_inner,
        y_ref,
        sums_ref,
    ) = refs
    rows, inner = y_ref.shape
    reach = expand(column(cols_ref, REACH, heads), expander(heads, inner, 2))
    for s in range(rows // SPAN):
        at = slice(s * SPAN, (s + 1) * SPAN)
        high, low = halves_of(state_ref[s] + upto_ref[s, :1] * incoming[...])
        c = bc_ref[at, state:]
        y_ref[at, :] = inside_ref[at, :] + (mm(c, high) + mm(c, low)) * reach[at]
    y = y_ref[...] + skip[...] * x_ref[...].astype(F32)
    z = z_ref[...]
    gated = y * (z * sigmoid(z))
    sums_ref[...] = rows_of_sums(gated * gated, grad_ref[...] * norm_inner[...] * gated)


def norm_body(shards, state, heads, count, meta, *refs):
    sums, refs = refs[:shards], refs[shards:]
    (
        bc_ref,
        x_ref,
        cols_ref,
        z_ref,
        y_ref,
        grad_ref,
        own_ref,
        skip,
        norm_inner,
        y_norm_ref,
        dz_ref,
        dy_ref,
        state_ref,
        after_ref,
        message_ref,
        gain_ref,
        skip_ref,
        carry,
        decay,
    ) = refs
    step = pl.program_id(0)
    rows, inner = dy_ref.shape

    @pl.when(step == 0)
    def _():
        carry[...] = jnp.zeros_like(carry)
        decay[...] = jnp.ones_like(decay)
        gain_ref[...] = jnp.zeros_like(gain_ref)
        skip_ref[...] = jnp.zeros_like(skip_ref)

    full = inner * shards
    all_rows = add_all([one[...] for one in sums])
    inverse = widen(lax.rsqrt(column_of(all_rows, 0) / full + EPSILON), inner)
    share = widen(column_of(all_rows, 1) / full, inner) * inverse * inverse * inverse
    x = x_ref[...].astype(F32)
    y = y_ref[...] + skip[...] * x
    z = z_ref[...]
    sig = sigmoid(z)
    gate = z * sig
    gated = y * gate
    hat = gated * inverse
    grad = grad_ref[...]
    gain_ref[...] += fold_rows(grad * hat)
    y_norm_ref[...] = (hat * norm_inner[...]).astype(BF16)
    d_gated = inverse * (grad * norm_inner[...]) - gated * share
    dz_ref[...] = (d_gated * y * (sig + gate * (1.0 - sig))).astype(BF16)
    dy = d_gated * gate
    skip_ref[...] += fold_rows(dy * x)
    dy_ref[...] = dy

    reach = expand(column(cols_ref, REACH, heads), expander(heads, inner, 2))
    high, low = halves_of(dy * reach)
    for s in reversed(range(rows // SPAN)):
        at = slice(s * SPAN, (s + 1) * SPAN)
        c = bc_ref[at, state:]
        state_ref[s] = carry[...]
        after_ref[s] = decay[...]
        carry[...] = own_ref[s, :1] * carry[...] + (mm_tn(c, high[at]) + mm_tn(c, low[at]))
        decay[...] = decay[...] * own_ref[s]

    @pl.when(step == count - 1)
    def _():
        pack_message(message_ref, carry[...], decay[...])


def write_halves(total, mine, keep_ref, send_ref, columns):
    count, share = keep_ref.shape[:2]
    for j in range(count):
        here = pl.ds(pl.multiple_of((2 * j + mine) * share, share), share)
        there = pl.ds(pl.multiple_of((2 * j + 1 - mine) * share, share), share)
        keep_ref[j, :, columns] = total[here, :].astype(keep_ref.dtype)
        send_ref[j, :, columns] = total[there, :].astype(send_ref.dtype)


def early_body(shards, count, meta, *refs):
    cots, late_cots, refs = refs[:shards], refs[shards : 2 * shards], refs[2 * shards :]
    (normed_ref, y_norm_ref, dz_ref, w_out, w_z), refs = refs[:5], refs[5:]
    outs, refs = refs[:shards], refs[shards:]
    keep_ref, send_ref, gain_ref, cot, total_z, total_out = refs
    step = pl.program_id(0)
    me = meta[1]
    part = cots[0].shape[1]
    inner = dz_ref.shape[1]

    @pl.when(step == 0)
    def _():
        total_z[...] = jnp.zeros_like(total_z)
        total_out[...] = jnp.zeros_like(total_out)

    y_norm = y_norm_ref[...]
    for k in range(shards):
        outs[k][...] = mm(y_norm, w_out[:, block_at(me, k, part)]).astype(BF16)

    @pl.when(step < count // 2)
    def _():
        assemble(cots, me, cot)

    @pl.when(step >= count // 2)
    def _():
        assemble(late_cots, me, cot)

    total_z[...] += mm_tn(normed_ref[...], dz_ref[...])
    total_out[...] += mm_tn(cot[...], y_norm)

    @pl.when(step == count - 1)
    def _():
        mine = meta[2] & 1
        write_halves(total_z, mine, keep_ref, send_ref, slice(0, inner))
        write_halves(total_out, mine, keep_ref, send_ref, slice(inner, 2 * inner))
        gain_ref[...] = row_of_sums(total_z[...] * w_z[...].astype(F32))


def inside_back_body(state, heads, start, meta, begin_row, bc_ref, xdt_ref, dy_ref, cols_ref, runt_ref, dxdt_ref, dbc_ref):
    rows, inner = dxdt_ref.shape
    first = meta[0] + (start + pl.program_id(0)) * rows
    row = lax.broadcasted_iota(jnp.int32, (SPAN, SPAN), 0)
    col = lax.broadcasted_iota(jnp.int32, (SPAN, SPAN), 1)
    size = inner // heads
    lane = lax.broadcasted_iota(jnp.int32, (SPAN, 2 * size), 1)
    for s in range(rows // SPAN):
        at = slice(s * SPAN, (s + 1) * SPAN)
        allowed = (row <= col) & (row + (first + s * SPAN) >= begin_row[:1, at])
        b = bc_ref[at, :state]
        c = bc_ref[at, state:]
        scores = jnp.where(allowed, mm_nt(b, c), 0.0)
        d_scores = None
        for pair in range(heads // 2):
            lanes = slice(pair * 2 * size, (pair + 1) * 2 * size)
            x_both = xdt_ref[at, lanes]
            high, low = halves_of(dy_ref[at, lanes])
            total = None
            for j in range(2):
                h = 2 * pair + j
                lane_at = RUN * heads + h
                spread = runt_ref[h : h + 1, at] - cols_ref[at, lane_at : lane_at + 1]
                fade = jnp.exp(jnp.minimum(spread, 0.0))
                mixing = (scores * fade).astype(BF16)
                mine = (lane < size) == (j == 0)
                high_mine = jnp.where(mine, high, jnp.zeros_like(high))
                low_mine = jnp.where(mine, low, jnp.zeros_like(low))
                product = mm(mixing, high_mine)
                total = product if total is None else total + product
                faded = (mm_nt(x_both, high_mine) + mm_nt(x_both, low_mine)) * fade
                d_scores = faded if d_scores is None else d_scores + faded
            dxdt_ref[at, lanes] = total
        d_scores = jnp.where(allowed, d_scores, 0.0).astype(BF16)
        dbc_ref[at, :state] = mm(d_scores, c)
        dbc_ref[at, state:] = mm_tn(d_scores, b)


def cross_border(fresh, begins, first, edge, taps, taps_ref, lanes):
    reach = taps.shape[0] - 1
    spot = lax.broadcasted_iota(jnp.int32, (8, lanes), 0)
    place = lax.broadcasted_iota(jnp.int32, (8, 128), 0) + (first - 8)
    sent = jnp.zeros((8, lanes), F32)
    for lag in range(1, reach + 1):
        moved = jnp.concatenate([jnp.zeros((8 - lag, lanes), F32), fresh[:lag, :]], axis=0)
        starts = jnp.concatenate([jnp.zeros((8 - lag, 128), jnp.int32), begins[:lag, :]], axis=0)
        valid = widen((place >= starts).astype(F32), lanes)
        moved = jnp.where(spot >= 8 - lag, moved * valid, 0.0)
        sent = sent + taps[reach - lag : reach - lag + 1, :] * moved
        taps_ref[reach - lag] += moved * edge
    return jnp.concatenate([jnp.zeros((EDGE - 8, lanes), F32), sent], axis=0)


def conv_back(ext, begin_ext, place, pre, taps, taps_ref):
    rows, lanes = pre.shape
    reach = taps.shape[0] - 1
    du = ext[:rows, :]
    taps_ref[reach] += fold_rows(du * pre)
    total = taps[reach : reach + 1, :] * du
    for lag in range(1, reach + 1):
        valid = widen((place >= begin_ext[lag : lag + rows, :]).astype(F32), lanes)
        moved = ext[lag : lag + rows, :] * valid
        total = total + taps[reach - lag : reach - lag + 1, :] * moved
        taps_ref[reach - lag] += fold_rows(moved * pre)
    return total


def maps_back_body(state, heads, count, meta, *refs):
    (
        begin_ref,
        bc_ref,
        xdt_ref,
        dy_ref,
        cols_ref,
        slope_ref,
        pre_ref,
        edge_ref,
        normed_ref,
        edge_normed,
        w_bc,
        dbc_ref,
        state_ref,
        upto_ref,
        dstate_ref,
        after_ref,
        own_ref,
        incoming,
        outgoing,
        taps,
        dpre_ref,
        through_ref,
        ds_ref,
        tail_ref,
        left_ref,
        taps_ref,
        bias_ref,
        own_half_ref,
        send_ref,
        gain_ref,
        ext,
        begin_ext,
        weight,
    ) = refs
    step = pl.program_id(0)
    rows, inner = xdt_ref.shape
    at_step = count - 1 - step
    first = meta[0] + at_step * rows
    spread = expander(heads, inner)
    spread_two = expander(heads, inner, 2)

    @pl.when(step == 0)
    def _():
        weight[...] = jnp.zeros_like(weight)
        ext[rows:, :] = jnp.zeros_like(ext[rows:, :])
        begin_ext[rows:, :] = jnp.zeros_like(begin_ext[rows:, :])
        taps_ref[...] = jnp.zeros_like(taps_ref)
        bias_ref[...] = jnp.zeros_like(bias_ref)

    @pl.when(step > 0)
    def _():
        ext[rows:, :] = ext[:8, :]
        begin_ext[rows:, :] = begin_ext[:8, :]

    begin_ext[:rows, :] = begin_ref[...]
    place = row_ids(rows) + first
    keep = expand(column(cols_ref, KEEP, heads), spread_two)
    reach = expand(column(cols_ref, REACH, heads), spread_two)
    x_high, x_low = halves_of(xdt_ref[...].astype(F32) * keep)
    y_high, y_low = halves_of(dy_ref[...] * reach)
    for s in range(rows // SPAN):
        at = slice(s * SPAN, (s + 1) * SPAN)
        s_in = state_ref[s] + upto_ref[s, :1] * incoming[...]
        ds_out = dstate_ref[s] + after_ref[s, :1] * outgoing[...]
        ds_ref[s] = ds_out
        through = jnp.sum((s_in * ds_out).reshape(state // 8, 8, inner), axis=0) * own_ref[s]
        through_ref[s] = jnp.broadcast_to(
            jnp.sum(per_head(through, spread), axis=0, keepdims=True), (8, heads)
        )
        s_high, s_low = halves_of(s_in)
        ds_high, ds_low = halves_of(ds_out)
        d_b = mm_nt(x_high[at], ds_high) + mm_nt(x_low[at], ds_high) + mm_nt(x_high[at], ds_low)
        d_c = mm_nt(y_high[at], s_high) + mm_nt(y_low[at], s_high) + mm_nt(y_high[at], s_low)
        slope = slope_ref[at, :].astype(F32)
        ext[at, :state] = (dbc_ref[at, :state] + d_b) * slope[:, :state]
        ext[at, state:] = (dbc_ref[at, state:] + d_c) * slope[:, state:]
    bias_ref[...] += fold_rows(ext[:rows, :])
    total = conv_back(ext, begin_ext, place, pre_ref[...].astype(F32), taps, taps_ref)
    high, low = halves_of(total)
    dpre_ref[...] = high
    weight[...] += mm_tn(normed_ref[...], high) + mm_tn(normed_ref[...], low)

    @pl.when(step == 0)
    def _():
        tail_ref[...] = total[rows - EDGE :, :]

    @pl.when(step == count - 1)
    def _():
        edge = edge_ref[EDGE - 8 :, inner:].astype(F32)
        left_ref[...] = cross_border(ext, begin_ext, first, edge, taps, taps_ref, 2 * state)
        left_high, left_low = halves_of(left_ref[...])
        weight[...] += mm_tn(edge_normed[...], left_high) + mm_tn(edge_normed[...], left_low)
        half = send_ref.shape[0]
        mine = meta[1] & 1
        here = pl.ds(pl.multiple_of(mine * half, half), half)
        there = pl.ds(pl.multiple_of((1 - mine) * half, half), half)
        own_half_ref[...] = weight[here, :]
        send_ref[...] = weight[there, :]
        gain_ref[...] = row_of_sums(weight[...] * w_bc[...].astype(F32))


def inner_back_body(state, heads, start, fresh_steps, opens, meta, *refs):
    refs = list(refs)

    def take(amount):
        found = refs[:amount]
        del refs[:amount]
        return found

    (
        begin_ref,
        begin_late,
        bc_ref,
        x_ref,
        xdt_ref,
        dy_ref,
        y_ref,
        cols_ref,
        slope_ref,
        pre_late,
        normed_late,
        dxdt_ref,
        through_ref,
        ds_ref,
        skip,
        rate,
        taps,
    ) = take(17)
    if opens:
        (edge_ref,) = take(1)
    else:
        held_in, held_ddt_in, right, taps_in, bias_in, scalar_in, weight_in = take(7)
        w_x, w_dt, scale, gain_z, gain_bc, norm_gain, skip_gain, taps_bc, bias_bc = take(9)
    dpre_ref, ddt_ref = take(2)
    if opens:
        taps_ref, bias_ref, scalar_ref, held_out, held_ddt_out, left_ref, weight = take(7)
    else:
        keep_half_ref, send_ref, owned_ref, shared_ref, taps_ref, bias_ref, scalar_ref, weight = take(8)
    ext, begin_ext, fresh, ddt = take(4)
    step = pl.program_id(0)
    rows, inner = x_ref.shape
    steps = fresh_steps if opens else fresh_steps + 1
    spread = expander(heads, inner)
    spread_two = expander(heads, inner, 2)

    @pl.when(step == 0)
    def _():
        if opens:
            weight[...] = jnp.zeros_like(weight)
            taps_ref[...] = jnp.zeros_like(taps_ref)
            bias_ref[...] = jnp.zeros_like(bias_ref)
            scalar_ref[...] = jnp.zeros_like(scalar_ref)
        else:
            weight[...] = weight_in[...]
            taps_ref[...] = taps_in[...]
            bias_ref[...] = bias_in[...]
            scalar_ref[...] = scalar_in[...]
            ext[:rows, :] = held_in[...]
            ddt[...] = held_ddt_in[...]

    def renew():
        at_block = (start + step) * (rows // SPAN)
        first = meta[0] + at_block * SPAN
        place = row_ids(rows) + first
        suffix = triangle(SPAN, lambda r, c: r <= c)
        prefix = triangle(SPAN, lambda r, c: r > c)
        rate_now = rate[...]
        spans = [slice(s * SPAN, (s + 1) * SPAN) for s in range(rows // SPAN)]
        kept = []
        for s, at in enumerate(spans):
            b = bc_ref[at, :state]
            ds_high, ds_low = halves_of(ds_ref[s])
            kept.append(mm(b, ds_high) + mm(b, ds_low))
        kept = jnp.concatenate(kept, axis=0) * expand(column(cols_ref, KEEP, heads), spread_two)
        dy = dy_ref[...]
        xdt = xdt_ref[...].astype(F32)
        x = x_ref[...].astype(F32)
        dxdt_in = dxdt_ref[...]
        dxdt = dxdt_in + kept
        dt = column(cols_ref, DT, heads)
        d_x = dxdt * expand(dt, spread_two) + skip[...] * dy
        du = d_x * slope_ref[...].astype(F32)
        fresh[...] = du
        bias_ref[...] += fold_rows(du)
        dy_high = dy.astype(BF16).astype(F32)
        later = per_head(dy_high * y_ref[...] - xdt * dxdt_in, spread, 3)
        earlier = per_head(xdt * kept, spread)
        direct = per_head(x * dxdt, spread)
        q = []
        for s, at in enumerate(spans):
            after = [part.astype(F32) for part in pieces(later[at], 3)]
            after = mm(suffix, jnp.concatenate(after, axis=1).astype(BF16))
            before = [part.astype(F32) for part in pieces(earlier[at], 2)]
            before = mm(prefix, jnp.concatenate(before, axis=1).astype(BF16))
            q.append(
                (after[:, :heads] + after[:, heads : 2 * heads] + after[:, 2 * heads :])
                + (before[:, :heads] + before[:, heads:])
                + through_ref[s, :1, :]
            )
        starts = (place == begin_ref[...]).astype(F32)[:, :heads]
        q = jnp.concatenate(q, axis=0) * (1.0 - starts)
        d_raw = (direct + rate_now * q) / (1.0 + jnp.exp(-column(cols_ref, RAW, heads)))
        fresh_ddt[...] = d_raw.astype(BF16)
        scalar_ref[:8, :] += fold_rows(d_raw)
        scalar_ref[8:, :] += fold_rows(rate_now * dt * q)

    fresh_ddt = refs[0]

    def finish(closing=False):
        begin_ext[:rows, :] = begin_late[...]
        first = meta[0] + (start - (0 if opens else 1) + step - (1 if opens else 0)) * rows
        place = row_ids(rows) + first
        total = conv_back(ext, begin_ext, place, pre_late[...].astype(F32), taps, taps_ref)
        dpre_ref[...] = total.astype(BF16)
        if closing:
            dpre_ref[rows - EDGE :, :] = (total[rows - EDGE :, :] + right[...]).astype(BF16)
        ddt_ref[...] = ddt[...]
        held = normed_late[...]
        weight[:, :inner] += mm_tn(held, dpre_ref[...])
        weight[:, inner : inner + heads] += mm_tn(held, ddt[...])

    if opens:
        renew()

        @pl.when(step == 0)
        def _():
            edge = edge_ref[EDGE - 8 :, :inner].astype(F32)
            left_ref[...] = cross_border(fresh, begin_ref, meta[0], edge, taps, taps_ref, inner)

        @pl.when(step > 0)
        def _():
            ext[rows:, :] = fresh[:8, :]
            begin_ext[rows:, :] = begin_ref[:8, :]
            finish()

        ext[:rows, :] = fresh[...]
        ddt[...] = fresh_ddt[...]

        @pl.when(step == steps - 1)
        def _():
            held_out[...] = fresh[...]
            held_ddt_out[...] = fresh_ddt[...]
    else:

        @pl.when(step < steps - 1)
        def _():
            renew()
            ext[rows:, :] = fresh[:8, :]
            begin_ext[rows:, :] = begin_ref[:8, :]
            finish()
            ext[:rows, :] = fresh[...]
            ddt[...] = fresh_ddt[...]

        @pl.when(step == steps - 1)
        def _():
            ext[rows:, :] = jnp.zeros((8, inner), F32)
            begin_ext[rows:, :] = jnp.zeros((8, 128), jnp.int32)
            finish(True)
            write_halves(weight, meta[2] & 1, keep_half_ref, send_ref, slice(0, weight.shape[1]))
            gain = row_of_sums(weight[:, :inner] * w_x[...].astype(F32))
            gain_dt = row_of_sums(weight[:, inner : inner + heads] * w_dt[...].astype(F32))
            owned_ref[...] = jnp.zeros_like(owned_ref)
            shared_ref[...] = jnp.zeros_like(shared_ref)

            def one_row(values):
                return jnp.sum(values, axis=0, keepdims=True)

            for j in range(taps.shape[0]):
                owned_ref[j : j + 1, :] = one_row(taps_ref[j])
                shared_ref[j : j + 1, : 2 * state] = one_row(taps_bc[j])
            owned_ref[4:5, :] = one_row(bias_ref[...])
            shared_ref[4:5, : 2 * state] = one_row(bias_bc[...])
            owned_ref[5:6, :] = one_row(norm_gain[...])
            owned_ref[6:7, :] = one_row(skip_gain[...])
            owned_ref[7:8, :heads] = one_row(scalar_ref[:8, :])
            owned_ref[7:8, 128 : 128 + heads] = one_row(scalar_ref[8:, :])
            shared_ref[:, 2 * state :] = (gain + gain_dt + gain_z[...] + gain_bc[...]) / scale[...]


def input_body(shards, steps, closes, meta, *refs):
    xs, refs = refs[:shards], refs[shards:]
    dz_ref, dpre_ref, dbc_ref, ddt_ref, w_z, w_x, w_bc, w_dt, scale = refs[:9]
    refs = refs[9:]
    if closes:
        (tail_ref, right_ref), refs = refs[:2], refs[2:]
    outs, refs = refs[:shards], refs[shards:]
    dbc_held, sums = refs
    step = pl.program_id(0)
    me = meta[1]
    rows, part = xs[0].shape
    per_step = rows // part
    total_rows = steps * rows

    dbc_held[...] = dbc_ref[...]
    if closes:

        @pl.when(step == steps - 1)
        def _():
            dbc_held[rows - EDGE :, :] = (tail_ref[...] + right_ref[...]).astype(BF16)

    dz, dx, dbc, ddt = dz_ref[...], dpre_ref[...], dbc_held[...], ddt_ref[...]
    products = None
    here = pl.ds(pl.multiple_of(step * rows, rows), rows)
    for k in range(shards):
        at = block_at(me, k, part)
        grad = (
            mm_nt(dz, w_z[at, :])
            + mm_nt(dx, w_x[at, :])
            + mm_nt(dbc, w_bc[at, :])
            + mm_nt(ddt, w_dt[at, :])
        )
        outs[k][here, :] = grad.astype(BF16)
        product = grad * scale[me ^ k] * xs[k][...].astype(F32)
        products = product if products is None else products + product
    row = row_of_sums(products)

    @pl.when(step == 0)
    def _():
        sums[...] = jnp.zeros_like(sums)

    for s in range(steps):

        @pl.when(step == s)
        def _(s=s):
            for j in range(per_step):
                spot = s * per_step + j
                sums[spot : spot + 1, :] = row[:1, j * part : (j + 1) * part]

    @pl.when(step == steps - 1)
    def _():
        for k in range(shards):
            outs[k][total_rows:, :] = sums[...].astype(BF16)


def final_body(shards, heads, steps, meta, *refs):
    refs = list(refs)

    def take(amount):
        found = refs[:amount]
        del refs[:amount]
        return found

    count = shards // 2 + 1
    sets = [(take(count), take(count)) for _ in range(2)]
    mixed = take(count)
    x_ref, cot_ref, cols_ref, scale, out_ref, layer_ref = refs
    step = pl.program_id(0)
    me = meta[1]
    rows, part = x_ref.shape
    width = part * shards
    per_step = rows // part
    layer_ref[...] = add_all([one[...].astype(F32) for one in [x_ref] + mixed]).astype(BF16)

    def finish(parts, tails, row):
        sums = add_all([one[...].astype(F32) for one in tails])
        for j in range(per_step):
            at = slice(j * part, (j + 1) * part)
            spot = INV * heads
            inverse = jnp.broadcast_to(cols_ref[at, spot : spot + 1], (part, part))
            group, line = divmod(row + j, 8)
            total = column_of(sums[8 * group : 8 * group + 8], line)
            share = widen(total / width, part) * inverse * inverse * inverse
            grad = add_all([one[at, :].astype(F32) for one in parts]) * scale[me]
            out_ref[at, :] = cot_ref[at, :].astype(F32) + inverse * grad - x_ref[at, :].astype(F32) * share

    for s in range(steps):
        parts, tails = sets[2 * s // steps]

        @pl.when(step == s)
        def _(s=s, parts=parts, tails=tails):
            finish(parts, tails, (s % (steps // 2)) * per_step)


def weights_body(inner, heads, meta, keep_ref, got_ref, late_keep, late_got, z_ref, out_ref, x_ref, dt_ref):
    total = keep_ref[0].astype(F32) + got_ref[0].astype(F32)
    z_ref[...] = total[:, :inner]
    out_ref[...] = total[:, inner:].T
    total = late_keep[0].astype(F32) + late_got[0].astype(F32)
    x_ref[...] = total[:, :inner]
    dt_ref[...] = total[:, inner:].T[:heads]


def swap(shard, axis, flip):
    return lax.ppermute(shard, axis, [(i, i ^ flip) for i in range(lax.axis_size(axis))])


def handed(meta, array, after):
    return call(nothing, (1,), [meta], [], [], (1, 1000), "hand_on", after=after, carry=[array], room=2)[-1]


def nothing(meta):
    pass


def gather_far(shard):
    return {k: swap(shard, "head", k) for k in range(2, lax.axis_size("head"), 2)}


def gather_near(shard, far):
    found = []
    for k in range(0, lax.axis_size("head"), 2):
        one = far[k] if k else shard
        found += [one, swap(one, "head", 1)]
    return found


class Stages:
    def __init__(self, steps):
        self.steps = steps
        self.job = next(steps)

    def terms(self, meta, after=()):
        while self.job[0] is not None:
            run_stages(meta, [self], after)
        return self.job[1]


def run_stages(meta, stages, after, carry=()):
    stages = [one for one in stages if one.job[0] is not None]
    if not stages:
        return [], list(carry)
    jobs = [one.job for one in stages]

    def body(meta, *refs):
        ins, outs = 0, sum(len(job[1]) for job in jobs)
        for work, arrays, shapes in jobs:
            work(meta, *refs[ins : ins + len(arrays)], *refs[outs : outs + len(shapes)])
            ins, outs = ins + len(arrays), outs + len(shapes)

    made = call(
        body,
        (1,),
        [meta] + [whole_of(array) for job in jobs for array in job[1]],
        [(shape, dtype, whole(shape)) for job in jobs for shape, dtype in job[2]],
        [],
        (1, 1000),
        "sums",
        after=after,
        carry=carry,
        room=14,
    )
    at = 0
    for one, job in zip(stages, jobs):
        one.job = one.steps.send(made[at : at + len(job[2])])
        at += len(job[2])
    return made[:at], made[at + 1 :]


def near_body(meta, one_ref, two_ref, out_ref):
    out_ref[...] = (one_ref[...].astype(F32) + two_ref[...].astype(F32)).astype(BF16)


def scatter_near(parts):
    return [swap(parts[k + 1], "head", 1) for k in range(0, len(parts), 2)]


def scatter_far(parts, got):
    found = [parts[0], got[0]]
    for k in range(2, len(parts), 2):
        (near,) = yield near_body, [parts[k], got[k // 2]], [(parts[k].shape, BF16)]
        found.append(swap(near, "head", k))
    yield None, found


def add_body(meta, one_ref, two_ref, out_ref):
    out_ref[...] = one_ref[...] + two_ref[...]


def add_head(values):
    bits = lax.axis_size("head").bit_length() - 1
    for bit in range(bits):
        got = swap(values, "head", 1 << bit)
        if bit == bits - 1:
            yield None, (values, got)
        else:
            (values,) = yield add_body, [values, got], [(values.shape, F32)]


def halve_body(axis, bit, meta, keep_ref, got_ref, kept_ref, sent_ref):
    mine = (meta[axis] >> bit) & 1
    for j in range(kept_ref.shape[0]):
        here, there = 2 * j + mine, 2 * j + 1 - mine
        kept_ref[j] = keep_ref[here].astype(F32) + got_ref[here].astype(F32)
        sent_ref[j] = (keep_ref[there].astype(F32) + got_ref[there].astype(F32)).astype(sent_ref.dtype)


def halve(keep, got, bit):
    count, rows, lanes = keep.shape
    shape = (count // 2, rows, lanes)
    return functools.partial(halve_body, 2, bit), [keep, got], [(shape, F32), (shape, got.dtype)]


def scatter_seq(keep, send):
    bits = lax.axis_size("seq").bit_length() - 1
    for bit in range(bits):
        received = swap(send, "seq", 1 << bit)
        if bit < bits - 1:
            keep, send = yield halve(keep, received, bit + 1)
    yield None, (keep, received)


def sum_rows_everywhere(keep, send):
    got = swap(send, "head", 1)
    for bit in range(1, lax.axis_size("head").bit_length() - 1):
        (keep,) = yield add_body, [keep, got], [(keep.shape, F32)]
        got = swap(keep, "head", 1 << bit)
    for bit in reversed(range(lax.axis_size("seq").bit_length() - 1)):
        rows, lanes = keep.shape
        shape = (2, rows // 2, lanes)
        kept, sent = yield halve(keep.reshape(shape), got.reshape(shape), bit)
        keep, sent = kept.reshape(shape[1:]), sent.reshape(shape[1:])
        got = swap(sent, "seq", 1 << bit)
    yield None, (keep, got)


def pack_small(target, at, values):
    lanes = target.shape[1]
    high, low = halves_of(values)
    for t in range(values.shape[1] // lanes):
        part = slice(t * lanes, (t + 1) * lanes)
        both = jnp.concatenate([high[:, part].astype(F32), low[:, part].astype(F32)], axis=0)
        target[at + 16 * t : at + 16 * t + 16, :] = both.astype(BF16)


def unpack_small(source, at):
    rows = source[at:, :].astype(F32)
    pieces_found = [
        rows[16 * t : 16 * t + 8] + rows[16 * t + 8 : 16 * t + 16] for t in range(rows.shape[0] // 16)
    ]
    return jnp.concatenate(pieces_found, axis=1)


def open_body(meta, keep_ref, got_ref, owned_ref, shared_ref, more_ref, out_ref):
    rows = keep_ref.shape[0]
    out_ref[:rows, :] = (keep_ref[...] + got_ref[...]).astype(BF16)
    shared = shared_ref[...] + more_ref[...]
    pack_small(out_ref, rows, jnp.concatenate([owned_ref[...], shared], axis=1))


def widen_body(bit, rows, last, meta, own_ref, got_ref, out_ref, *small_ref):
    mine = (meta[2] >> bit) & 1
    own, got = own_ref[:rows, :], got_ref[:rows, :]
    out_ref[:rows, :] = jnp.where(mine == 0, own, got)
    out_ref[rows : 2 * rows, :] = jnp.where(mine == 0, got, own)
    small = unpack_small(own_ref, rows) + unpack_small(got_ref, rows)
    if not last:
        pack_small(out_ref, 2 * rows, small)
        return
    taps_x, bias_x, gain_x, skip_x, bias_dt, rate_x, taps_bc, bias_bc, gain_in, held = small_ref
    inner, maps, part = bias_x.shape[1], bias_bc.shape[1], gain_in.shape[1]
    heads = skip_x.shape[1]
    reach = taps_x.shape[0]
    taps_x[...] = small[:reach, :inner]
    bias_x[...] = small[4:5, :inner]
    gain_x[...] = small[5:6, :inner]
    skip_x[...] = per_head(small[:, :inner], expander(heads, inner), 3)[6:7]
    bias_dt[...] = small[7:8, :heads]
    rate_x[...] = small[7:8, 128 : 128 + heads]
    taps_bc[...] = small[:reach, inner : inner + maps]
    bias_bc[...] = small[4:5, inner : inner + maps]
    held[...] = small[:, inner + maps :]
    gain_in[...] = held[:1, pl.ds(pl.multiple_of(meta[1] * part, part), part)]


def end_sums(terms, owned, shared, more, heads, reach, part):
    keep, got = terms
    rows, lanes = keep.shape
    width = owned.shape[1] + shared.shape[1]
    extra = 16 * (width // lanes)
    (held,) = yield open_body, [keep, got, owned, shared, more], [((rows + extra, lanes), BF16)]
    bits = lax.axis_size("seq").bit_length() - 1
    for bit in range(bits):
        got = swap(held, "seq", 1 << bit)
        last = bit == bits - 1
        outs = [((2 * rows + (0 if last else extra), lanes), BF16)]
        if last:
            inner = owned.shape[1]
            small = [(reach, inner), (1, inner), (1, inner), (1, heads), (1, heads), (1, heads)]
            small += [(reach, lanes), (1, lanes), (1, part), (8, width - inner - lanes)]
            outs += [(one, F32) for one in small]
        found = yield functools.partial(widen_body, bit, rows, last), [held, got], outs
        held, rows = found[0], 2 * rows
    mine = lax.axis_index("head") & 1
    other = swap(held, "head", 1)
    low, high = jnp.where(mine == 0, held, other), jnp.where(mine == 0, other, held)
    yield None, (jnp.concatenate([low, high], axis=0).astype(F32), found[1:-1])


def pair_of(forward, meta, own_ref, got_ref):
    state = own_ref.shape[0] - 8
    own_last = (meta[2] & 1) == (1 if forward else 0)
    own_fade, fade = own_ref[state:, :], got_ref[state:, :]
    own, other = own_ref[:state, :], got_ref[:state, :]
    pair = jnp.where(own_last, own_fade[:1] * other + own, fade[:1] * own + other)
    return pair, own_fade * fade


def pair_body(forward, meta, own_ref, got_ref, sent_ref, pair):
    half = pair.shape[0] // 2
    pair[...], fade = pair_of(forward, meta, own_ref, got_ref)
    sent_ref[:half, :] = pair[pl.ds(pl.multiple_of((meta[2] & 1) * half, half), half), :]
    sent_ref[half:, :] = fade


def whole_pair_body(forward, meta, own_ref, got_ref, sent_ref):
    state = sent_ref.shape[0] - 16
    pair, fade = pair_of(forward, meta, own_ref, got_ref)
    sent_ref[:state, :] = pair.astype(BF16)
    sent_ref[state:, :] = jnp.concatenate(
        [part.astype(F32) for part in halves_of(fade)], axis=0
    ).astype(BF16)


def whole_join_body(forward, count, meta, *refs):
    got_ref, out_ref = refs[count:]
    state = out_ref.shape[0]
    total = jnp.zeros(out_ref.shape, F32)
    for one in reversed(refs[:count]):
        tail = one[state:, :].astype(F32)
        total = (tail[:1] + tail[8:9]) * total + one[:state, :].astype(F32)
    own_last = (meta[2] & 1) == (1 if forward else 0)
    fade, other = got_ref[state : state + 1, :], got_ref[:state, :]
    out_ref[...] = jnp.where(own_last, fade * total + other, total)


def fold_body(count, meta, *refs):
    total_ref = refs[count]
    half = total_ref.shape[0]
    total = jnp.zeros(total_ref.shape, F32)
    for one in reversed(refs[:count]):
        total = one[half : half + 1, :] * total + one[:half, :]
    total_ref[...] = total


def join_body(forward, meta, total_ref, rest_ref, got_ref, out_ref):
    state = out_ref.shape[0]
    odd = meta[2] & 1
    own_last = odd == (1 if forward else 0)
    total, rest = total_ref[...], rest_ref[...]
    low, high = jnp.where(odd == 0, total, rest), jnp.where(odd == 0, rest, total)
    total = jnp.concatenate([low, high], axis=0)
    fade, other = got_ref[state : state + 1, :], got_ref[:state, :]
    out_ref[...] = jnp.where(own_last, fade * total + other, total)


def chain(meta, message, forward):
    size = lax.axis_size("seq")
    rows, lanes = message.shape
    state = rows - 8
    half = state // 2

    def small(body, arrays, shape, scratch, name, after=(), carry=(), dtype=F32):
        return call(
            body,
            (1,),
            [meta] + [whole_of(one) for one in arrays],
            [(shape, dtype, whole(shape))],
            scratch,
            (1, 1000),
            name,
            after=after,
            carry=carry,
            room=8,
        )

    got = swap(message, "seq", 1)
    after = yield None
    if forward:
        body = functools.partial(whole_pair_body, forward)
        sent = small(body, [message, got], (state + 16, lanes), [], "pair", after, dtype=BF16)[0]
    else:
        sent = small(
            functools.partial(pair_body, forward),
            [message, got],
            (half + 8, lanes),
            [pltpu.VMEM((state, lanes), F32)],
            "pair",
            after,
        )[0]
    found = []
    for by in range(2, size, 2):
        if forward:
            pairs = [(i, i + by) for i in range(size - by)]
        else:
            pairs = [(i + by, i) for i in range(size - by)]
        found.append(lax.ppermute(sent, "seq", pairs))
    after = yield sent
    if forward:
        body = functools.partial(whole_join_body, forward, len(found))
        yield small(body, found + [got], (state, lanes), [], "join", after)
    total = small(
        functools.partial(fold_body, len(found)), found, (half, lanes), [], "fold", after
    )[0]
    rest = swap(total, "seq", 1)
    after, carry = yield total
    body = functools.partial(join_body, forward)
    yield small(body, [total, rest, got], (state, lanes), [], "join", after, carry)


def on_device(
    inputs,
    input_norm_scale,
    w_z,
    w_x,
    w_bc,
    w_dt,
    conv_x_w,
    conv_x_b,
    conv_bc_w,
    conv_bc_b,
    dt_bias,
    a_log,
    d_skip,
    norm_inner,
    w_out,
    cotangent,
    lengths,
    order,
):
    tokens, part = inputs.shape
    shards = lax.axis_size("head")
    seq_size = lax.axis_size("seq")
    me = lax.axis_index("head")
    seq = lax.axis_index("seq")
    width = part * shards
    share = width // seq_size
    inner = w_z.shape[1]
    heads = dt_bias.shape[0]
    size = inner // heads
    state = w_bc.shape[1] // 2
    channels = inner + 2 * state
    taps_count = conv_x_w.shape[0]
    rows = 2 * SPAN
    spans = rows // SPAN
    count = tokens // rows
    half = tokens // 2
    half_count = count // 2
    first = seq * tokens

    number = lengths.shape[0]
    picker = (order[:, None] == jnp.arange(number, dtype=jnp.int32)[None, :]).astype(jnp.int32)
    placed = jnp.sum(picker * lengths[None, :], axis=1)
    starts = jnp.cumsum(placed) - placed
    spots = first + jnp.arange(tokens, dtype=jnp.int32)
    begin = jnp.max(jnp.where(starts[None, :] <= spots[:, None], starts[None, :], 0), axis=1)
    begin = begin.astype(jnp.int32)
    begin_col = jnp.broadcast_to(begin[:, None], (tokens, 128))
    begin_row = jnp.broadcast_to(begin[None, :], (8, tokens))
    meta = Place(tokens)

    edge = lax.ppermute(
        inputs[tokens - EDGE :], "seq", [(i, i + 1) for i in range(seq_size - 1)]
    )
    edges = gather_near(edge, gather_far(edge))
    own_halves = [inputs[:half], inputs[half:]]
    xs = [gather_near(own_halves[0], gather_far(own_halves[0]))]
    late_half = handed(meta, own_halves[1], [xs[0][2], edges[2]])
    late_far = gather_far(late_half)
    cots = []

    scale = input_norm_scale.reshape(shards, 1, part)
    taps = jnp.concatenate([conv_x_w, conv_bc_w], axis=1)
    bias = jnp.concatenate([conv_x_b, conv_bc_b])[None, :]
    rate = -jnp.exp(a_log)[None, :]
    w_maps = jnp.concatenate([w_bc, w_dt, jnp.zeros((width, 128 - heads), BF16)], axis=1)
    skip = jnp.repeat(d_skip, size)[None, :]
    inner_gain = norm_inner[None, :]
    scale_row = input_norm_scale[None, :]
    prepared = [begin_row, skip, inner_gain, scale_row, rate]

    def fore(i):
        return i

    def back(i):
        return count - 1 - i

    big = [
        ((tokens, width), BF16, "rows", FAR),
        ((tokens, inner), BF16, "rows", FAR),
        ((tokens, 2 * state), BF16, "rows", FAR),
        ((tokens, inner), BF16, "rows", NEAR),
        ((tokens, inner), BF16, "rows", NEAR),
        ((tokens, 2 * state), BF16, "rows", NEAR),
        ((tokens, inner), BF16, "rows", FAR),
        ((tokens, 2 * state), BF16, "rows", FAR),
        ((tokens, 128), F32, "rows", NEAR),
        ((heads, tokens), F32, "lanes", NEAR),
        ((tokens // SPAN, state, inner), F32, "stack", NEAR),
        ((tokens // SPAN, 8, inner), F32, "stack", NEAR),
        ((tokens // SPAN, 8, inner), F32, "stack", NEAR),
    ]

    def spec_of(shape, kind, step):
        if kind == "rows":
            return rows_at(rows, shape[1], step)
        if kind == "lanes":
            return lanes_at(shape[0], rows, step)
        return stack_at((spans,) + shape[1:], step)

    carried = None
    for chunk in range(2):
        opens, closes = chunk == 0, chunk == 1
        start = chunk * half_count

        def here(i, start=start):
            return start + i

        ins = [meta] + [(one, rows_at(rows, part, fore)) for one in xs[chunk]]
        if opens:
            ins += [whole_of(one) for one in edges]
        else:
            ins += [whole_of(one) for one in carried]
        ins += [(begin_col, rows_at(rows, 128, here))]
        ins += [
            whole_of(one)
            for one in (scale, w_x, w_maps, taps, bias, dt_bias[None, :], rate)
        ]
        outs = [
            (shape, dtype, spec_of(shape, kind, here), space) for shape, dtype, kind, space in big
        ]
        if opens:
            extra = [((EDGE, channels), BF16), ((EDGE, width), BF16)]
        else:
            extra = []
        if closes:
            extra += [((state + 8, inner), F32)]
        else:
            extra += [((EDGE, channels), BF16), ((state, inner), F32), ((8, inner), F32)]
        outs += [(shape, dtype, whole(shape)) for shape, dtype in extra]
        found = call(
            functools.partial(
                project_body, shards, inner, state, heads, start, half_count, opens, closes
            ),
            (half_count,),
            ins,
            outs,
            [
                pltpu.VMEM((rows + 8, channels), F32),
                pltpu.VMEM((state, inner), F32),
                pltpu.VMEM((8, inner), F32),
            ],
            (12, 1000000),
            "project",
            room=ROOM_PROJECT,
            after=prepared if opens else [],
            carry=[cotangent[chunk * half : (chunk + 1) * half]],
            kept=None if opens else dict(enumerate(held)),
        )
        held = found[: len(big)]
        if opens:
            late_far = {k: handed(meta, one, [found[-2]]) for k, one in late_far.items()}
            xs.append(gather_near(late_half, late_far))
            early_cot, early_cot_far = found[-1], gather_far(found[-1])
        else:
            late_cot, late_cot_far = found[-1], gather_far(found[-1])
            early_cot_far = {k: handed(meta, one, [found[-2]]) for k, one in early_cot_far.items()}
            cots.append(gather_near(early_cot, early_cot_far))
        if opens:
            pre_edge, edge_normed = found[len(big) : len(big) + 2]
            carried = found[len(big) + 2 : -2]
        else:
            message = found[len(big)]
    (
        normed,
        pre_x,
        pre_bc,
        x,
        xdt,
        bc,
        slope_x,
        slope_bc,
        cols,
        runt,
        states,
        upto,
        own,
    ) = held

    links = chain(meta, message, True)
    next(links)
    found = None
    for chunk in range(2):
        start = chunk * half_count
        if chunk == 1:
            sent = links.send([found[-1]])
            late_cot_far = {k: handed(meta, one, [sent]) for k, one in late_cot_far.items()}
            cots.append(gather_near(late_cot, late_cot_far))

        def here(i, start=start):
            return start + i

        found = call(
            functools.partial(inside_body, shards, state, heads, start),
            (half_count,),
            [meta]
            + [(one, rows_at(rows, part, fore)) for one in cots[chunk]]
            + [
                (begin_col, rows_at(rows, 128, here)),
                (bc, rows_at(rows, 2 * state, here)),
                (xdt, rows_at(rows, inner, here)),
                (cols, rows_at(rows, 128, here)),
                (runt, lanes_at(heads, rows, here)),
                (normed, rows_at(rows, width, here)),
                whole_of(w_z),
                whole_of(w_out),
            ],
            [((tokens, inner), F32, rows_at(rows, inner, here), NEAR)] * 3,
            [pltpu.VMEM((rows, width), BF16)],
            (8, 1000000),
            "inside",
            room=ROOM_INSIDE,
            kept=None if found is None else dict(enumerate(found[:3])),
            after=() if found is None else [sent],
        )
    inside, z, grad_y, done = found
    incoming, _ = links.send([done])

    y, sums, done = call(
        functools.partial(gate_body, state, heads),
        (count,),
        [meta]
        + [
            (bc, rows_at(rows, 2 * state, fore)),
            (x, rows_at(rows, inner, fore)),
            (cols, rows_at(rows, 128, fore)),
            (z, rows_at(rows, inner, fore)),
            (grad_y, rows_at(rows, inner, fore)),
            (inside, rows_at(rows, inner, fore)),
            (states, stack_at((spans, state, inner), fore)),
            (upto, stack_at((spans, 8, inner), fore)),
            whole_of(incoming),
            whole_of(skip),
            whole_of(inner_gain),
        ],
        [
            ((tokens, inner), F32, rows_at(rows, inner, fore), NEAR),
            ((8, tokens), F32, lanes_at(8, rows, fore)),
        ],
        [],
        (9, 1000000),
        "gate",
        room=ROOM_GATE,
    )

    all_sums = [sums] + [swap(sums, "head", k) for k in range(1, shards)]

    y_norm, dz, dy, dstates, after, message, g_norm_inner, g_skip, done = call(
        functools.partial(norm_body, shards, state, heads, count),
        (count,),
        [meta]
        + [(one, lanes_at(8, rows, back)) for one in all_sums]
        + [
            (bc, rows_at(rows, 2 * state, back)),
            (x, rows_at(rows, inner, back)),
            (cols, rows_at(rows, 128, back)),
            (z, rows_at(rows, inner, back)),
            (y, rows_at(rows, inner, back)),
            (grad_y, rows_at(rows, inner, back)),
            (own, stack_at((spans, 8, inner), back)),
            whole_of(skip),
            whole_of(inner_gain),
        ],
        [
            ((tokens, inner), BF16, rows_at(rows, inner, back), NEAR),
            ((tokens, inner), BF16, rows_at(rows, inner, back), NEAR),
            ((tokens, inner), F32, rows_at(rows, inner, back), NEAR),
            ((tokens // SPAN, state, inner), F32, stack_at((spans, state, inner), back), NEAR),
            ((tokens // SPAN, 8, inner), F32, stack_at((spans, 8, inner), back), NEAR),
            ((state + 8, inner), F32, whole((state + 8, inner))),
            ((8, inner), F32, whole((8, inner))),
            ((8, inner), F32, whole((8, inner))),
        ],
        [pltpu.VMEM((state, inner), F32), pltpu.VMEM((8, inner), F32)],
        (12, 1000000),
        "norm",
        room=ROOM_NORM,
    )


    def inside_back(chunk, kept, after):
        def here(i):
            return chunk * half_count + i

        return call(
            functools.partial(inside_back_body, state, heads, chunk * half_count),
            (half_count,),
            [
                meta,
                (begin_row, lanes_at(8, rows, here)),
                (bc, rows_at(rows, 2 * state, here)),
                (xdt, rows_at(rows, inner, here)),
                (dy, rows_at(rows, inner, here)),
                (cols, rows_at(rows, 128, here)),
                (runt, lanes_at(heads, rows, here)),
            ],
            [
                ((tokens, inner), F32, rows_at(rows, inner, here), NEAR),
                ((tokens, 2 * state), F32, rows_at(rows, 2 * state, here), NEAR),
            ],
            [],
            (7, 1000000),
            "inside_back",
            room=ROOM_INSIDE,
            kept=None if kept is None else dict(enumerate(kept[:2])),
            after=after,
        )

    links = chain(meta, message, False)
    next(links)
    held = inside_back(0, None, [])
    sent = links.send([held[-1]])

    pair_shape = (seq_size // 2, share, 2 * inner)
    found = call(
        functools.partial(early_body, shards, count),
        (count,),
        [meta]
        + [
            (one, rows_at(rows, part, lambda i: jnp.minimum(i, half_count - 1)))
            for one in cots[0]
        ]
        + [
            (one, rows_at(rows, part, lambda i: jnp.maximum(i - half_count, 0)))
            for one in cots[1]
        ]
        + [
            (normed, rows_at(rows, width, fore)),
            (y_norm, rows_at(rows, inner, fore)),
            (dz, rows_at(rows, inner, fore)),
            whole_of(w_out),
            whole_of(w_z),
        ],
        [((tokens, part), BF16, rows_at(rows, part, fore), FAR)] * shards
        + [
            (pair_shape, BF16, whole(pair_shape), FAR),
            (pair_shape, BF16, whole(pair_shape), FAR),
            ((8, width), F32, whole((8, width))),
        ],
        [
            pltpu.VMEM((rows, width), BF16),
            pltpu.VMEM((width, inner), F32),
            pltpu.VMEM((width, inner), F32),
        ],
        (12, 1000000),
        "early",
        after=[held[-1], sent],
        room=ROOM_EARLY,
    )
    out_parts, (early_keep, early_send, gain_z, done) = found[:shards], found[shards:]
    out_parts = [bare(one) for one in out_parts]
    total = links.send(())
    dxdt, dbc, done = inside_back(1, held, [total])
    sent_late = [bare(early_send)] + out_parts[1::2]
    outgoing, token, early_send, *odd_parts = links.send(([done], sent_late))
    out_parts[1::2] = odd_parts
    out_near = scatter_near(out_parts)
    early = Stages(scatter_seq(bare(early_keep), early_send))


    found = call(
        functools.partial(maps_back_body, state, heads, count),
        (count,),
        [
            meta,
            (begin_col, rows_at(rows, 128, back)),
            (bc, rows_at(rows, 2 * state, back)),
            (xdt, rows_at(rows, inner, back)),
            (dy, rows_at(rows, inner, back)),
            (cols, rows_at(rows, 128, back)),
            (slope_bc, rows_at(rows, 2 * state, back)),
            (pre_bc, rows_at(rows, 2 * state, back)),
            whole_of(pre_edge),
            (normed, rows_at(rows, width, back)),
            whole_of(edge_normed),
            whole_of(w_bc),
            (dbc, rows_at(rows, 2 * state, back)),
            (states, stack_at((spans, state, inner), back)),
            (upto, stack_at((spans, 8, inner), back)),
            (dstates, stack_at((spans, state, inner), back)),
            (after, stack_at((spans, 8, inner), back)),
            (own, stack_at((spans, 8, inner), back)),
            whole_of(incoming),
            whole_of(outgoing),
            whole_of(conv_bc_w),
        ],
        [
            ((tokens, 2 * state), BF16, rows_at(rows, 2 * state, back), NEAR),
            ((tokens // SPAN, 8, heads), F32, stack_at((spans, 8, heads), back), NEAR),
            ((tokens // SPAN, state, inner), F32, stack_at((spans, state, inner), back), NEAR),
            ((EDGE, 2 * state), F32, whole((EDGE, 2 * state))),
            ((EDGE, 2 * state), F32, whole((EDGE, 2 * state))),
            ((taps_count, 8, 2 * state), F32, whole((taps_count, 8, 2 * state))),
            ((8, 2 * state), F32, whole((8, 2 * state))),
            ((width // 2, 2 * state), F32, whole((width // 2, 2 * state))),
            ((width // 2, 2 * state), F32, whole((width // 2, 2 * state))),
            ((8, width), F32, whole((8, width))),
        ],
        [
            pltpu.VMEM((rows + 8, 2 * state), F32),
            pltpu.VMEM((rows + 8, 128), jnp.int32),
            pltpu.VMEM((width, 2 * state), F32),
        ],
        (12, 1000000),
        "maps_back",
        room=ROOM_MAPS,
    )
    dpre_bc, through, ds_all, tail_bc, left_bc, taps_bc, bias_bc = found[:7]
    bc_keep, bc_send, gain_bc, done = found[7:]
    left_pairs = [(i + 1, i) for i in range(seq_size - 1)]
    right_bc = lax.ppermute(left_bc, "seq", left_pairs)
    bc_sums = Stages(sum_rows_everywhere(bc_keep, bc_send))
    out_sums = Stages(scatter_far(out_parts, out_near))
    sent, _ = run_stages(meta, [bc_sums, out_sums], [done])

    late_width = inner + 128
    late_shape = (seq_size // 2, share, late_width)

    def inner_back(opens, start, fresh_steps, extra, after):
        steps = fresh_steps if opens else fresh_steps + 1

        def now(i):
            return start + jnp.minimum(i, fresh_steps - 1)

        def late(i):
            return jnp.maximum(i - 1, 0) if opens else start - 1 + i

        def written(i):
            return jnp.maximum(i - 1, 0) if opens else i

        outs = [
            ((half, inner), BF16, rows_at(rows, inner, written), NEAR),
            ((half, heads), BF16, rows_at(rows, heads, written)),
        ]
        sums = [
            ((taps_count, 8, inner), F32, whole((taps_count, 8, inner))),
            ((8, inner), F32, whole((8, inner))),
            ((16, heads), F32, whole((16, heads))),
        ]
        sums_scratch = []
        if opens:
            outs += sums + [
                ((rows, inner), F32, whole((rows, inner)), NEAR),
                ((rows, heads), BF16, whole((rows, heads))),
                ((EDGE, inner), F32, whole((EDGE, inner))),
                ((width, late_width), F32, whole((width, late_width)), NEAR),
            ]
        else:
            outs += [
                (late_shape, BF16, whole(late_shape), FAR),
                (late_shape, BF16, whole(late_shape), FAR),
                ((8, inner), F32, whole((8, inner))),
                ((8, 2 * state + width), F32, whole((8, 2 * state + width))),
            ]
            sums_scratch = [pltpu.VMEM(shape, F32) for shape, _, _ in sums]
            sums_scratch += [pltpu.VMEM((width, late_width), F32)]
        return call(
            functools.partial(inner_back_body, state, heads, start, fresh_steps, opens),
            (steps,),
            [
                meta,
                (begin_col, rows_at(rows, 128, now)),
                (begin_col, rows_at(rows, 128, late)),
                (bc, rows_at(rows, 2 * state, now)),
                (Held(bare(x), FAR), rows_at(rows, inner, now)),
                (xdt, rows_at(rows, inner, now)),
                (dy, rows_at(rows, inner, now)),
                (Held(bare(y), FAR), rows_at(rows, inner, now)),
                (cols, rows_at(rows, 128, now)),
                (slope_x, rows_at(rows, inner, now)),
                (pre_x, rows_at(rows, inner, late)),
                (normed, rows_at(rows, width, late)),
                (dxdt, rows_at(rows, inner, now)),
                (through, stack_at((spans, 8, heads), now)),
                (ds_all, stack_at((spans, state, inner), now)),
                whole_of(skip),
                whole_of(rate),
                whole_of(conv_x_w),
            ]
            + [whole_of(one) for one in extra],
            outs,
            sums_scratch
            + [
                pltpu.VMEM((rows + 8, inner), F32),
                pltpu.VMEM((rows + 8, 128), jnp.int32),
                pltpu.VMEM((rows, inner), F32),
                pltpu.VMEM((rows, heads), BF16),
                pltpu.VMEM((rows, heads), BF16),
            ],
            (6 * fresh_steps, 1000000),
            "inner_back",
            after=after,
            room=ROOM_INNER,
        )

    found = inner_back(True, 0, count - 1, [pre_edge], sent + [right_bc])
    sent, _ = run_stages(meta, [early, bc_sums, out_sums], [found[-1]])
    dpre_low, ddt_low, taps_x, bias_x, scalars, held_du, held_ddt, left_x, weight_x, done = found
    right_x = lax.ppermute(left_x, "seq", left_pairs)

    def input_grad(chunk, dpre, ddt, extra, after, carry=()):
        start = chunk * half_count

        def here(i):
            return start + i

        whole_rows = half + EDGE
        return call(
            functools.partial(input_body, shards, half_count, chunk == 1),
            (half_count,),
            [meta]
            + [(Held(one, FAR), rows_at(rows, part, fore)) for one in xs[chunk]]
            + [
                (Held(bare(dz), FAR), rows_at(rows, inner, here)),
                (dpre, rows_at(rows, inner, fore)),
                (Held(bare(dpre_bc), FAR), rows_at(rows, 2 * state, here)),
                (ddt, rows_at(rows, heads, fore)),
            ]
            + [whole_of(one) for one in [w_z, w_x, w_bc, w_dt, scale] + extra],
            [((whole_rows, part), BF16, whole((whole_rows, part)))] * shards,
            [pltpu.VMEM((rows, 2 * state), BF16), pltpu.VMEM((EDGE, part), F32)],
            (8, 1000000),
            "input_grad",
            room=ROOM_INPUT,
            after=after,
            carry=carry,
        )

    found = inner_back(
        False,
        count - 1,
        1,
        [held_du, held_ddt, right_x, taps_x, bias_x, scalars, weight_x]
        + [w_x, w_dt, scale_row, gain_z, gain_bc]
        + [g_norm_inner, g_skip, taps_bc, bias_bc],
        sent,
    )
    dpre_high, ddt_high, late_keep, late_send, owned, shared, done = found
    late = Stages(scatter_seq(bare(late_keep), bare(late_send)))
    shared_sums = Stages(add_head(shared))
    sent, _ = run_stages(meta, [bc_sums, out_sums], [done])
    sent += out_sums.terms(meta)[2:] + [early.job[1][1]]
    *parts_low, done = input_grad(0, dpre_low, ddt_low, [], sent)
    low_sums = Stages(scatter_far(parts_low, scatter_near(parts_low)))
    sent, _ = run_stages(meta, [bc_sums, shared_sums, low_sums, early], [done])
    early_terms, mixed = early.terms(meta), out_sums.terms(meta)
    results = input_grad(
        1,
        dpre_high,
        ddt_high,
        [tail_bc, right_bc],
        sent,
        [mixed[0], early_terms[0]],
    )
    parts_high, (done, *own_terms) = results[:shards], results[shards:]
    mixed[0], early_keep = own_terms
    ends = Stages(
        end_sums(
            bc_sums.terms(meta), owned, *shared_sums.terms(meta), heads, taps_count, part
        )
    )
    far_low = low_sums.terms(meta)
    _, parts_high[1::2] = run_stages(
        meta, [late, ends], [done, far_low[-1], early_terms[1]], parts_high[1::2]
    )
    high_sums = Stages(scatter_far(parts_high, scatter_near(parts_high)))
    run_stages(meta, [late, high_sums, ends], ())
    far_high = high_sums.terms(meta)
    run_stages(meta, [late, ends], ())

    def low(i):
        return jnp.minimum(i, half_count - 1)

    def high(i):
        return jnp.maximum(i - half_count, 0)

    ins = []
    for terms, step in ((far_low, low), (far_high, high)):
        ins += [(one, rows_at(rows, part, step)) for one in terms]
        ins += [(one, pl.BlockSpec((EDGE, part), lambda i, *meta: (half // EDGE, 0))) for one in terms]
    grad_input, output, done = call(
        functools.partial(final_body, shards, heads, count),
        (count,),
        [meta]
        + ins
        + [(one, rows_at(rows, part, fore)) for one in mixed]
        + [
            (Held(inputs, FAR), rows_at(rows, part, fore)),
            (Held(cotangent, FAR), rows_at(rows, part, fore)),
            (cols, rows_at(rows, 128, fore)),
            whole_of(scale),
        ],
        [
            ((tokens, part), F32, rows_at(rows, part, fore)),
            ((tokens, part), BF16, rows_at(rows, part, fore)),
        ],
        [],
        (5, 1000000),
        "finals",
        room=10,
    )
    grad_w_z, grad_w_out, grad_w_x, grad_w_dt, _ = call(
        functools.partial(weights_body, inner, heads),
        (1,),
        [meta] + [whole_of(one) for one in (early_keep, early_terms[1]) + late.terms(meta)],
        [
            ((share, inner), F32, whole((share, inner))),
            ((inner, share), F32, whole((inner, share))),
            ((share, inner), F32, whole((share, inner))),
            ((heads, share), F32, whole((heads, share))),
        ],
        [],
        (2, 1000000),
        "weights",
        room=10,
    )
    grad_w_bc, small = ends.terms(meta, [done])
    taps_x, bias_x, gain_x, skip_x, bias_dt, rate_x, taps_bc, bias_bc, gain_in = small
    return (
        output,
        grad_input,
        gain_in.reshape(-1),
        grad_w_z,
        grad_w_x,
        grad_w_bc,
        grad_w_dt.T,
        taps_x,
        bias_x.reshape(-1),
        taps_bc,
        bias_bc.reshape(-1),
        bias_dt.reshape(-1),
        rate_x.reshape(-1),
        skip_x.reshape(-1),
        gain_x.reshape(-1),
        grad_w_out,
    )


def solution(mesh):
    placed = (
        P("seq", "head"),
        P(),
        P(None, "head"),
        P(None, "head"),
        P(),
        P(None, "head"),
        P(None, "head"),
        P("head"),
        P(),
        P(),
        P("head"),
        P("head"),
        P("head"),
        P("head"),
        P("head", None),
        P("seq", "head"),
        P(),
        P(),
    )
    return jax.shard_map(
        on_device,
        mesh=mesh,
        in_specs=placed,
        out_specs=(
            P("seq", "head"),
            P("seq", "head"),
            P("head"),
            P("seq", "head"),
            P("seq", "head"),
            P(),
            P("seq", "head"),
            P(None, "head"),
            P("head"),
            P(),
            P(),
            P("head"),
            P("head"),
            P("head"),
            P("head"),
            P("head", "seq"),
        ),
        check_vma=False,
    )
```
